512 devices in a mesh: dp: 16 (over x_hi, y, core), ctx: 32 (over z, x_lo).
Axes of the slice: x: 4 (x_hi: 2, x_lo: 2; x = x_hi * 2 + x_lo), y: 4, z: 16, core: 2. Of those that a mesh axis runs over, the one named last changes fastest.
Arguments:
- series: bfloat16 [16, 4096, 512], P('dp', 'ctx'), may hold values from -40 to 40
- norm_gain: float32 [512], replicated, may hold values from 0.5 to 1.5
- query_kernel: bfloat16 [3, 512, 512], P(None, 'dp'), may hold values from -6.251302 to 6.251302
- key_kernel: bfloat16 [3, 512, 512], P(None, 'dp'), may hold values from -0.104613624 to 0.104613624
- value_weight: bfloat16 [512, 512], P('dp'), may hold values from -0.25 to 0.25
- out_weight: bfloat16 [512, 512], P('dp'), may hold values from -0.25 to 0.25
- block_links: int32 [16, 32, 8, 4], P('dp', 'ctx'), may hold values 0 or 1
- grad_out: bfloat16 [16, 4096, 512], P('dp', 'ctx'), may hold values from -36 to 36
Outputs:
- mixed: bfloat16 [16, 4096, 512], P('dp', 'ctx')
- grad_series: bfloat16 [16, 4096, 512], P('dp', 'ctx')
- grad_gain: float32 [512], replicated
- grad_query_kernel: float32 [3, 512, 512], P(None, 'dp')
- grad_key_kernel: float32 [3, 512, 512], P(None, 'dp')
- grad_value_weight: float32 [512, 512], P('dp')
- grad_out_weight: float32 [512, 512], P('dp')
The draws below stay inside these ranges and needn't reach their ends.
All inputs are finite; a program needn't handle non-finite values. No bound on the sum of `block_links` on one device may be relied on, other than what follows from the above.
Results may differ from the reference program's by a relative error of at most 0.039.
The reference program's roundings to bfloat16 on the way count: a program that leaves them out, or rounds other values in their place, can miss the bound.
Values may be sent and summed in bfloat16 or wider, within the bound.
No kernel may reach another device: no remote copies, remote signals or barrier semaphores. Data moves between devices by JAX's collectives and lax.ppermute only.
A program may use at most 64 MiB of HBM per device.

```python
import math
import jax
import jax.numpy as jnp
from jax import lax

D = 512
H = 8
LINKS = 4
NBLK = 32
LENGTH = 4096
SEQS = 16


def shared_kernel(key):
    return jax.random.truncated_normal(key, -4.0, 4.0, (3, D, D), jnp.float32) * (3 * D) ** (-0.5)


def draw_series(key, part):
    key = jax.random.fold_in(key, 11)
    scale_key, base_key = jax.random.split(key, 2)
    scale = jnp.exp(jax.random.uniform(scale_key, (SEQS, LENGTH, 1), jnp.float32, 0.0, math.log(10.0)))
    base = jax.random.truncated_normal(base_key, -4.0, 4.0, (SEQS, LENGTH, D), jnp.float32)
    return (base * scale).astype(jnp.bfloat16)


def draw_grad_out(key, part):
    key = jax.random.fold_in(key, 13)
    scale_key, base_key = jax.random.split(key, 2)
    scale = jnp.exp(jax.random.uniform(scale_key, (SEQS, LENGTH, 1), jnp.float32, 0.0, math.log(3.0)))
    rising = 1.0 + 2.0 * jnp.arange(LENGTH, dtype=jnp.float32) / LENGTH
    scale = scale * rising[None, :, None]
    base = jax.random.truncated_normal(base_key, -4.0, 4.0, (SEQS, LENGTH, D), jnp.float32)
    return (base * scale).astype(jnp.bfloat16)


def draw_key_kernel(key, part):
    return shared_kernel(key).astype(jnp.bfloat16)


def draw_query_kernel(key, part):
    key = jax.random.fold_in(key, 17)
    noise_key = jax.random.fold_in(key, 1)
    noise = jax.random.truncated_normal(noise_key, -4.0, 4.0, (3, D, D), jnp.float32) * (3 * D) ** (-0.5)
    return noise.astype(jnp.bfloat16)


def set_ends(values, stream_key, smallest, high):
    spot = [jax.random.randint(jax.random.fold_in(stream_key, axis), (), 0, length) for axis, length in enumerate(values.shape)]
    widest = values.shape.index(max(values.shape))
    beside = spot[:widest] + [(spot[widest] + 1) % values.shape[widest]] + spot[widest + 1:]
    return values.at[tuple(spot)].set(smallest).at[tuple(beside)].set(high)


def shard_levels(key, extent, cuts, smallest, high):
    level, own = 1.0, jax.random.fold_in(key, 6)
    for dim, blocks in cuts:
        steps = jnp.exp(jax.random.uniform(jax.random.fold_in(own, dim), (blocks,), jnp.float32, smallest / len(cuts), high / len(cuts)))
        level = level * jnp.repeat(steps, extent[dim] // blocks).reshape([-1 if axis == dim else 1 for axis in range(len(extent))])
    return level


def centred(stream_key, extent, spread, most, cuts=(), kind=jnp.bfloat16):
    values = spread * jax.random.normal(stream_key, extent, jnp.float32)
    if cuts:
        values = values * shard_levels(stream_key, extent, cuts, -0.22, 0.18)
    return jnp.clip(values, -most, most).astype(kind)


def setup_inputs(seed: int = 0) -> dict:
    key_of = jax.random.split(jax.random.key(seed), 9)
    series = draw_series(jax.random.fold_in(key_of[8], 71), 0)
    norm_gain = jnp.clip(1.0 + 0.1 * jax.random.normal(key_of[1], (D,), jnp.float32), 0.5, 1.5)
    query_kernel = draw_query_kernel(jax.random.fold_in(key_of[8], 71), 0)
    key_kernel = draw_key_kernel(jax.random.fold_in(key_of[8], 71), 0)
    value_weight = centred(key_of[4], (D, D), D ** -0.5, 0.25, ((0, 16),))
    out_weight = centred(key_of[5], (D, D), D ** -0.5, 0.25, ((0, 16),))
    block_links = set_ends((jax.random.randint(key_of[6], (SEQS, NBLK, H, LINKS), 0, 4) < 3).astype(jnp.int32), jax.random.fold_in(key_of[6], 1), 0, 1)
    grad_out = draw_grad_out(jax.random.fold_in(key_of[8], 71), 0)
    return {"series": series, "norm_gain": norm_gain, "query_kernel": query_kernel, "key_kernel": key_kernel, "value_weight": value_weight, "out_weight": out_weight, "block_links": block_links, "grad_out": grad_out}


block_offsets = (1, 2, 4, 8)
epsilon = 1e-06

def normalize(values, norm_gain):
    scale = lax.rsqrt(lax.optimization_barrier(jnp.mean(values * values, axis=-1, keepdims=True)) + epsilon)
    return values * scale * norm_gain

def product(left, right):
    return jnp.dot(left, right, preferred_element_type=jnp.float32)

def product_right_t(left, right):
    return lax.dot_general(left, right, (((1,), (1,)), ((), ())), preferred_element_type=jnp.float32)

def product_left_t(left, right):
    return lax.dot_general(left, right, (((0,), (0,)), ((), ())), preferred_element_type=jnp.float32)

def rounded(values):
    return lax.optimization_barrier(values.astype(jnp.bfloat16)).astype(jnp.float32)

def convolve(window, kernel, count):
    result = product(window[2:2 + count], kernel[0])
    result = result + product(window[1:1 + count], kernel[1])
    return result + product(window[0:count], kernel[2])

def visibility(count, total, allowed):
    column = jnp.arange(total)
    source = column // count
    inside = column % count
    causal = (source[None, :] > 0) | (inside[None, :] <= jnp.arange(count)[:, None])
    linked = jnp.repeat(allowed, count, axis=1)
    return causal[None, :, :] & linked[:, None, :]

def probabilities(query, keys, allowed):
    count, features = query.shape
    heads = allowed.shape[0]
    head_width = features // heads
    total = keys.shape[0]
    query_heads = query.astype(jnp.float32).reshape(count, heads, head_width)
    key_heads = keys.astype(jnp.float32).reshape(total, heads, head_width)
    scores = jnp.einsum('thd,uhd->htu', query_heads, key_heads) * head_width ** (-0.5)
    visible = visibility(count, total, allowed)
    scores = jnp.where(visible, scores, -1e+30)
    highest = lax.optimization_barrier(jnp.max(scores, axis=-1, keepdims=True))
    weights = jnp.where(visible, jnp.exp(scores - highest), 0.0)
    return weights / lax.optimization_barrier(jnp.sum(weights, axis=-1, keepdims=True))

def attend(query, keys, values, allowed):
    count, features = query.shape
    heads = allowed.shape[0]
    head_width = features // heads
    probs = rounded(probabilities(query, keys, allowed))
    value_heads = values.astype(jnp.float32).reshape(-1, heads, head_width)
    result = jnp.einsum('htu,uhd->thd', probs, value_heads)
    return result.reshape(count, features).astype(jnp.bfloat16)

def attend_back(query, keys, values, allowed, upstream):
    count, features = query.shape
    total = keys.shape[0]
    heads = allowed.shape[0]
    head_width = features // heads
    probs = probabilities(query, keys, allowed)
    query_heads = query.astype(jnp.float32).reshape(count, heads, head_width)
    key_heads = keys.astype(jnp.float32).reshape(total, heads, head_width)
    value_heads = values.astype(jnp.float32).reshape(total, heads, head_width)
    upper_heads = upstream.astype(jnp.float32).reshape(count, heads, head_width)
    d_prob = jnp.einsum('thd,uhd->htu', upper_heads, value_heads)
    centre = lax.optimization_barrier(jnp.sum(probs * d_prob, axis=-1, keepdims=True))
    d_score = rounded(probs * (d_prob - centre) * head_width ** (-0.5))
    d_query = jnp.einsum('htu,uhd->thd', d_score, key_heads).reshape(count, features)
    d_key = jnp.einsum('htu,thd->uhd', d_score, query_heads).reshape(total, features)
    d_value = jnp.einsum('htu,thd->uhd', rounded(probs), upper_heads).reshape(total, features)
    return (d_query, d_key, d_value)

def shift_blocks(blocks, offset):
    count = blocks.shape[0]
    step_size = min(offset, count)
    return jnp.concatenate([jnp.zeros_like(blocks[:step_size]), blocks[:count - step_size]], axis=0)

def unshift_blocks(blocks, offset):
    count = blocks.shape[0]
    step_size = min(offset, count)
    return jnp.concatenate([blocks[step_size:], jnp.zeros_like(blocks[:step_size])], axis=0)

def reference(series, norm_gain, query_kernel, key_kernel, value_weight, out_weight, block_links, grad_out):
    heads = block_links.shape[2]
    features = series.shape[2]
    blocks = block_links.shape[1]
    length = series.shape[1]
    count = length // blocks
    offsets = jnp.array(block_offsets, dtype=jnp.int32)
    index = jnp.arange(blocks, dtype=jnp.int32)

    def one_sequence(carry, inputs):
        piece, link_rows, cotangent = inputs
        values = piece.astype(jnp.float32)
        normed = normalize(values, norm_gain).astype(jnp.bfloat16)
        padded = jnp.concatenate([jnp.zeros((2, features), jnp.bfloat16), normed], axis=0)
        query = convolve(padded, query_kernel, length).astype(jnp.bfloat16)
        keyed = convolve(padded, key_kernel, length).astype(jnp.bfloat16)
        value = product(normed, value_weight).astype(jnp.bfloat16)
        query_blocks = query.reshape(blocks, count, features)
        key_blocks = keyed.reshape(blocks, count, features)
        value_blocks = value.reshape(blocks, count, features)
        key_sources = jnp.concatenate([key_blocks] + [shift_blocks(key_blocks, offset) for offset in block_offsets], axis=1)
        value_sources = jnp.concatenate([value_blocks] + [shift_blocks(value_blocks, offset) for offset in block_offsets], axis=1)
        reach = (link_rows > 0) & (index[:, None, None] >= offsets[None, None, :])
        allowed = jnp.concatenate([jnp.ones((blocks, heads, 1), jnp.bool_), reach], axis=2)
        attn = lax.map(lambda item: attend(item[0], item[1], item[2], item[3]), (query_blocks, key_sources, value_sources, allowed)).reshape(length, features)
        mixed = (values + product(attn, out_weight)).astype(jnp.bfloat16)
        upstream = product_right_t(cotangent, out_weight).astype(jnp.bfloat16)
        d_query, key_terms, value_terms = lax.map(lambda item: attend_back(item[0], item[1], item[2], item[3], item[4]), (query_blocks, key_sources, value_sources, allowed, upstream.reshape(blocks, count, features)))
        key_terms = key_terms.reshape(blocks, 5, count, features)
        value_terms = value_terms.reshape(blocks, 5, count, features)
        d_key = key_terms[:, 0]
        d_value = value_terms[:, 0]
        for slot, offset in enumerate(block_offsets):
            d_key = d_key + unshift_blocks(key_terms[:, slot + 1], offset)
            d_value = d_value + unshift_blocks(value_terms[:, slot + 1], offset)
        d_query = d_query.reshape(length, features).astype(jnp.bfloat16)
        d_key = d_key.reshape(length, features).astype(jnp.bfloat16)
        d_value = d_value.reshape(length, features).astype(jnp.bfloat16)
        tail = jnp.zeros((2, features), jnp.bfloat16)
        after_query = jnp.concatenate([d_query, tail], axis=0)
        after_key = jnp.concatenate([d_key, tail], axis=0)
        d_normed = product_right_t(d_value, value_weight)
        for tap in range(3):
            d_normed = d_normed + product_right_t(after_query[tap:tap + length], query_kernel[tap])
            d_normed = d_normed + product_right_t(after_key[tap:tap + length], key_kernel[tap])
        unused, pull = jax.vjp(normalize, values, norm_gain)
        d_values, d_gain = pull(d_normed)
        grad_series = (cotangent.astype(jnp.float32) + d_values).astype(jnp.bfloat16)

        def block_terms(sums, block):
            start = block * count
            window = lax.dynamic_slice_in_dim(padded, start, count + 2, 0)
            rows_query = lax.dynamic_slice_in_dim(d_query, start, count, 0)
            rows_key = lax.dynamic_slice_in_dim(d_key, start, count, 0)
            rows_value = lax.dynamic_slice_in_dim(d_value, start, count, 0)
            rows_attn = lax.dynamic_slice_in_dim(attn, start, count, 0)
            rows_grad = lax.dynamic_slice_in_dim(cotangent, start, count, 0)
            terms = [product_left_t(window[2 - tap:2 - tap + count], rows_query) for tap in range(3)]
            terms = terms + [product_left_t(window[2 - tap:2 - tap + count], rows_key) for tap in range(3)]
            terms = terms + [product_left_t(window[2:], rows_value), product_left_t(rows_attn, rows_grad)]
            return (tuple((total + rounded(term) for total, term in zip(sums, terms))), None)
        weight_sums, unused_out = lax.scan(block_terms, carry[0], index)
        return ((weight_sums, carry[1] + d_gain), (mixed, grad_series))
    zero_square = jnp.zeros((features, features), jnp.float32)
    start_carry = (tuple((zero_square for tap in range(8))), jnp.zeros((features,), jnp.float32))
    final, outputs = lax.scan(one_sequence, start_carry, (series, block_links, grad_out))
    sums = final[0]
    return (outputs[0], outputs[1], final[1], jnp.stack(sums[0:3]), jnp.stack(sums[3:6]), sums[6], sums[7])
```

```python
import jax
import jax.numpy as jnp
from jax import lax
from jax.sharding import PartitionSpec as P

block_offsets = (1, 2, 4, 8)
epsilon = 1e-06
f32 = jnp.float32
bf16 = jnp.bfloat16


def shift_ctx(shard, by):
    devices = lax.axis_size("ctx")
    pairs = [(i, i + by) for i in range(devices) if 0 <= i + by < devices]
    return lax.ppermute(shard, "ctx", pairs)


def dp_to(shard, dx, dy, dc):
    def target(i):
        x, y, c = i // 8, (i // 2) % 4, i % 2
        return ((x + dx) % 2) * 8 + ((y + dy) % 4) * 2 + (c + dc) % 2

    return lax.ppermute(shard, "dp", [(i, target(i)) for i in range(16)])


def normalize(values, norm_gain):
    scale = lax.rsqrt(jnp.mean(values * values, axis=-1, keepdims=True) + epsilon)
    return values * scale * norm_gain


def product(left, right):
    return jnp.dot(left, right, preferred_element_type=f32)


def product_right_t(left, right):
    return lax.dot_general(left, right, (((1,), (1,)), ((), ())), preferred_element_type=f32)


def product_left_t(left, right):
    return lax.dot_general(left, right, (((0,), (0,)), ((), ())), preferred_element_type=f32)


def take(array, index, axis):
    return lax.dynamic_index_in_dim(array, index, axis, keepdims=False)


def in_place(mine, other, place, axis):
    return jnp.where(
        place == 0, jnp.stack([mine, other], axis), jnp.stack([other, mine], axis)
    )


def unroll_y(pieces, y, axis):
    order = [pieces[0], pieces[3], pieces[2], pieces[1]]
    twice = jnp.stack(order + order, axis)
    return lax.dynamic_slice_in_dim(twice, (4 - y) % 4, 4, axis)


def gather_weights(shard, x, y, core):
    first, second = shard[:4], shard[4:]
    second_y = [second] + [dp_to(second, 0, r, 0) for r in (1, 2, 3)]
    first_x = in_place(first, dp_to(first, 1, 0, 0), x, 0)
    first_xy = unroll_y([first_x] + [dp_to(first_x, 0, r, 0) for r in (1, 2, 3)], y, 1)
    second_yy = unroll_y(second_y, y, 0)
    second_xy = in_place(second_yy, dp_to(second_yy, 1, 0, 0), x, 0)
    result = []
    for part in (first_xy, second_xy):
        whole = in_place(part, dp_to(part, 0, 0, 1), core, 2)
        whole = jnp.transpose(whole, (3, 0, 1, 2, 4, 5))
        result.append(whole.reshape(4, 512, 512))
    return result


def total(parts):
    result = parts[0].astype(f32)
    for part in parts[1:]:
        result = result + part.astype(f32)
    return result.astype(bf16)


def spread(array, x_or_y, axis):
    return [take(array, (x_or_y + r) % 4, axis) for r in range(4)]


def scatter_partials(terms, x, y, core):
    kept = take(terms, core, 2)
    half = total([kept, dp_to(take(terms, 1 - core, 2), 0, 0, 1)])
    first, second = half[:, :, :128], half[:, :, 128:]
    out_y = spread(second, y, 1)
    second = total([out_y[0]] + [dp_to(out_y[r], 0, r, 0) for r in (1, 2, 3)])
    first = total([take(first, x, 0), dp_to(take(first, 1 - x, 0), 1, 0, 0)])
    out_y = spread(first, y, 0)
    first = total([out_y[0]] + [dp_to(out_y[r], 0, r, 0) for r in (1, 2, 3)])
    second = total([take(second, x, 0), dp_to(take(second, 1 - x, 0), 1, 0, 0)])
    return jnp.concatenate([first, second], axis=0)


def heads_of(array, heads):
    return array.reshape(array.shape[:-1] + (heads, array.shape[-1] // heads))


def body(
    series, norm_gain, query_kernel, key_kernel, value_weight, out_weight, block_links, grad_out
):
    place = lax.axis_index("dp")
    x, y, core = place // 8, (place // 2) % 4, place % 2
    block = lax.axis_index("ctx")
    heads = block_links.shape[2]
    own = series[0]
    cotangent = grad_out[0]
    count, features = own.shape
    width = features // heads
    scaling = width ** (-0.5)

    halo = shift_ctx(own[count - 2 :], 1)
    window = jnp.concatenate([halo, own], axis=0)
    carried = jnp.concatenate([window, cotangent], axis=0)
    shard = jnp.concatenate(
        [key_kernel, value_weight[None], query_kernel, out_weight[None]], axis=0
    )
    early, late = gather_weights(shard, x, y, core)
    full_key, full_value, full_query, full_out = early[:3], early[3], late[:3], late[3]
    before = [shift_ctx(window, offset) for offset in block_offsets]
    after = [shift_ctx(carried, -offset) for offset in block_offsets]

    key_windows = normalize(jnp.stack([window] + before).astype(f32), norm_gain).astype(bf16)
    query_windows = normalize(
        jnp.stack([window] + [piece[: count + 2] for piece in after]).astype(f32), norm_gain
    ).astype(bf16)
    uppers = jnp.stack([cotangent] + [piece[count + 2 :] for piece in after])

    def convolve(windows, kernel):
        result = product(windows[:, 2 : 2 + count], kernel[0])
        result = result + product(windows[:, 1 : 1 + count], kernel[1])
        return (result + product(windows[:, 0:count], kernel[2])).astype(bf16)

    keys = heads_of(convolve(key_windows, full_key), heads)
    values = heads_of(product(key_windows[:, 2:], full_value).astype(bf16), heads)
    queries = heads_of(convolve(query_windows, full_query), heads)
    upstream = heads_of(
        lax.dot_general(
            uppers, full_out, (((2,), (1,)), ((), ())), preferred_element_type=f32
        ).astype(bf16),
        heads,
    )

    offsets = jnp.array(block_offsets, dtype=jnp.int32)
    reach = (block_links[0, 0] > 0) & (block >= offsets)[None, :]
    allowed = jnp.concatenate([jnp.ones((heads, 1), jnp.bool_), reach], axis=1)
    row = lax.broadcasted_iota(jnp.int32, (count, 5, count), 0)
    slot = lax.broadcasted_iota(jnp.int32, (count, 5, count), 1)
    column = lax.broadcasted_iota(jnp.int32, (count, 5, count), 2)
    visible = ((slot > 0) | (column <= row))[None] & allowed[:, None, :, None]

    query, upper = queries[0], upstream[0]
    scores = jnp.einsum("thd,kuhd->htku", query, keys, preferred_element_type=f32) * scaling
    scores = jnp.where(visible, scores, -1e30)
    highest = jnp.max(scores, axis=(2, 3), keepdims=True)
    weights = jnp.where(visible, jnp.exp(scores - highest), 0.0)
    inverse = 1.0 / jnp.sum(weights, axis=(2, 3), keepdims=True)
    probs = weights * inverse
    probs_low = probs.astype(bf16)
    d_prob = jnp.einsum("thd,kuhd->htku", upper, values, preferred_element_type=f32)
    centre = jnp.sum(probs * d_prob, axis=(2, 3), keepdims=True)
    statistics = [
        jnp.concatenate(
            [
                jnp.where(reach[:, i][:, None], highest[:, :, 0, 0], 1e30),
                inverse[:, :, 0, 0],
                centre[:, :, 0, 0],
            ],
            axis=0,
        )
        for i in range(4)
    ]
    returned = [shift_ctx(statistics[i], -block_offsets[i]) for i in range(4)]
    attn = jnp.einsum("htku,kuhd->thd", probs_low, values, preferred_element_type=f32)
    attn = attn.reshape(count, features).astype(bf16)
    mixed = (own.astype(f32) + product(attn, full_out)).astype(bf16)
    d_score = (probs * (d_prob - centre) * scaling).astype(bf16)
    d_query = jnp.einsum("htku,kuhd->thd", d_score, keys, preferred_element_type=f32)
    d_query = d_query.reshape(count, features).astype(bf16)
    d_key = jnp.einsum("htu,thd->uhd", d_score[:, :, 0], query, preferred_element_type=f32)
    d_value = jnp.einsum("htu,thd->uhd", probs_low[:, :, 0], upper, preferred_element_type=f32)

    stacked = jnp.stack(returned).reshape(4, 3, heads, count)
    scores = jnp.einsum("kthd,uhd->khtu", queries[1:], keys[0], preferred_element_type=f32)
    probs = jnp.exp(scores * scaling - stacked[:, 0][..., None]) * stacked[:, 1][..., None]
    d_prob = jnp.einsum("kthd,uhd->khtu", upstream[1:], values[0], preferred_element_type=f32)
    d_score = (probs * (d_prob - stacked[:, 2][..., None]) * scaling).astype(bf16)
    d_key = d_key + jnp.einsum("khtu,kthd->uhd", d_score, queries[1:], preferred_element_type=f32)
    d_value = d_value + jnp.einsum(
        "khtu,kthd->uhd", probs.astype(bf16), upstream[1:], preferred_element_type=f32
    )
    d_key = d_key.reshape(count, features).astype(bf16)
    d_value = d_value.reshape(count, features).astype(bf16)

    leading = shift_ctx(jnp.concatenate([d_query[:2], d_key[:2]], axis=1), -1)
    base = key_windows[0]
    terms = [product_left_t(base[2 - tap : 2 - tap + count], d_key) for tap in range(3)]
    terms = terms + [product_left_t(base[2:], d_value)]
    terms = terms + [product_left_t(base[2 - tap : 2 - tap + count], d_query) for tap in range(3)]
    terms = terms + [product_left_t(attn, cotangent)]
    terms = jnp.stack([term.astype(bf16).reshape(16, 32, features) for term in terms], axis=1)
    rows = scatter_partials(terms.reshape(2, 4, 2, 256, features), x, y, core)

    after_query = jnp.concatenate([d_query, leading[:, :features]], axis=0)
    after_key = jnp.concatenate([d_key, leading[:, features:]], axis=0)
    d_normed = product_right_t(d_value, full_value)
    for tap in range(3):
        d_normed = d_normed + product_right_t(after_query[tap : tap + count], full_query[tap])
        d_normed = d_normed + product_right_t(after_key[tap : tap + count], full_key[tap])
    unused, pull = jax.vjp(normalize, own.astype(f32), norm_gain)
    d_values, d_gain = pull(d_normed)
    grad_series = (cotangent.astype(f32) + d_values).astype(bf16)
    for step in ((0, 0, 1), (0, 2, 0), (1, 0, 0)):
        d_gain = d_gain + dp_to(d_gain, *step)
    d_gain = d_gain + lax.ppermute(d_gain, "dp", [(i, i ^ 2) for i in range(16)])

    top = d_gain.astype(bf16)
    middle = (d_gain - top.astype(f32)).astype(bf16)
    low = (d_gain - top.astype(f32) - middle.astype(f32)).astype(bf16)
    extra = jnp.concatenate(
        [jnp.stack([top, middle, low]), jnp.zeros((5, features), bf16)], axis=0
    )
    payload = jnp.concatenate(
        [rows.reshape(32, 8, features), jnp.broadcast_to(extra[None], (32, 8, features))], axis=1
    )
    arrived = lax.all_to_all(payload, "ctx", 0, 0, tiled=True).astype(f32)
    gain_total = jnp.sum(arrived[:, 8:11], axis=(0, 1))
    summed = jnp.sum(arrived[:, :8], axis=0).astype(bf16)
    final = lax.all_to_all(
        jnp.broadcast_to(summed[None], (32, 8, features)), "ctx", 0, 0, tiled=True
    )
    final = final.reshape(8, 32, features).astype(f32)
    return (mixed[None], grad_series[None], gain_total, final[4:7], final[:3], final[3], final[7])


def solution(mesh):
    placed = (
        P("dp", "ctx", None),
        P(),
        P(None, "dp", None),
        P(None, "dp", None),
        P("dp", None),
        P("dp", None),
        P("dp", "ctx", None, None),
        P("dp", "ctx", None),
    )
    return jax.shard_map(
        body,
        mesh=mesh,
        in_specs=placed,
        out_specs=(
            P("dp", "ctx", None),
            P("dp", "ctx", None),
            P(),
            P(None, "dp", None),
            P(None, "dp", None),
            P("dp", None),
            P("dp", None),
        ),
        check_vma=False,
    )
```

```python
import jax
import jax.numpy as jnp
from jax import lax
from jax.experimental import pallas as pl
from jax.experimental.pallas import tpu as pltpu
from jax.sharding import PartitionSpec as P

block_offsets = (1, 2, 4, 8)
epsilon = 1e-06
hidden = -1e30
f32 = jnp.float32
bf16 = jnp.bfloat16
edge = 16
chip_groups = [[2 * i + c for i in range(8)] for c in range(2)]


def shift_ctx(shard, by):
    devices = lax.axis_size("ctx")
    pairs = [(i, i + by) for i in range(devices) if 0 <= i + by < devices]
    return lax.ppermute(shard, "ctx", pairs)


def other_core(shard):
    return lax.ppermute(shard, "dp", [(i, i ^ 1) for i in range(16)])


def over_chips(stacked):
    return lax.all_to_all(stacked, "dp", 0, 0, axis_index_groups=chip_groups, tiled=True)


def product(left, right):
    return jnp.dot(left, right, preferred_element_type=f32)


def product_right_t(left, right):
    return lax.dot_general(left, right, (((1,), (1,)), ((), ())), preferred_element_type=f32)


def product_left_t(left, right):
    return lax.dot_general(left, right, (((0,), (0,)), ((), ())), preferred_element_type=f32)


def inverse_rms(values):
    return lax.rsqrt(jnp.mean(values * values, axis=-1, keepdims=True) + epsilon)


def normed_taps(window, gain):
    values = window.astype(f32)
    normed = values * inverse_rms(values) * gain
    count = window.shape[0] - edge
    return [normed[edge - tap : edge - tap + count].astype(bf16) for tap in range(3)]


def call(kernel, outs, scratch=(), smem=0, inputs=0):
    return pl.pallas_call(
        kernel,
        out_shape=[jax.ShapeDtypeStruct(shape, kind) for shape, kind in outs],
        in_specs=[pl.BlockSpec(memory_space=pltpu.SMEM)] * smem
        + [pl.BlockSpec(memory_space=pltpu.VMEM)] * (inputs - smem),
        out_specs=[pl.BlockSpec(memory_space=pltpu.VMEM)] * len(outs),
        scratch_shapes=list(scratch),
        compiler_params=pltpu.CompilerParams(vmem_limit_bytes=50 * 1024 * 1024),
    )


def split_heads(pair, first):
    wide = pair.astype(f32)
    return jnp.concatenate(
        [jnp.where(first, wide, 0.0), jnp.where(first, 0.0, wide)], axis=0
    ).astype(bf16)


def join_heads(stacked, first):
    count = stacked.shape[0] // 2
    return jnp.where(first, stacked[:count], stacked[count:])


def rows_kernel(
    core_ref, links_ref, mine_ref, other_ref, window_ref, one_ref, two_ref, four_ref, eight_ref,
    upstream_ref, gain_ref, barred_ref,
    weights_ref, mixed_ref, attn_ref, d_query_ref, query_ref, upper_ref, key_ref, value_ref,
    taps_ref, own_stats_ref, stats_ref,
    lines_ref, keys_ref, values_ref,
):
    even = core_ref[0] == 0
    for chip in range(8):
        for matrix in range(8):
            mine, other = mine_ref[chip, matrix], other_ref[chip, matrix]
            weights_ref[matrix, chip * 64 : chip * 64 + 32] = jnp.where(even, mine, other)
            weights_ref[matrix, chip * 64 + 32 : chip * 64 + 64] = jnp.where(even, other, mine)
    gain = gain_ref[...]
    count = one_ref.shape[0]
    one = jnp.concatenate([two_ref[count:], one_ref[...]], axis=0)
    for slot, window in enumerate(
        (window_ref[...], one, two_ref[...], four_ref[...], eight_ref[...])
    ):
        for tap, part in enumerate(normed_taps(window, gain)):
            lines_ref[tap, slot * count : (slot + 1) * count] = part
    for tap in range(3):
        taps_ref[tap] = lines_ref[tap, :count]
    keys = product(lines_ref[0], weights_ref[0])
    keys = keys + product(lines_ref[1], weights_ref[1])
    keys_ref[...] = (keys + product(lines_ref[2], weights_ref[2])).astype(bf16)
    values_ref[...] = product(lines_ref[0], weights_ref[3]).astype(bf16)
    query = product(taps_ref[0], weights_ref[4])
    query = query + product(taps_ref[1], weights_ref[5])
    query_ref[...] = (query + product(taps_ref[2], weights_ref[6])).astype(bf16)
    upper_ref[...] = product_right_t(upstream_ref[...], weights_ref[7]).astype(bf16)
    key_ref[...] = keys_ref[:count]
    value_ref[...] = values_ref[:count]

    lane = lax.broadcasted_iota(jnp.int32, (count, 128), 1)
    row = lax.broadcasted_iota(jnp.int32, (count, 128), 0)
    first = lane < 64
    causal = jnp.where(lane <= row, 0.0, hidden)
    table = jnp.zeros((count, 128), f32)
    scaling = 64 ** (-0.5)
    for pair in range(4):
        span = slice(pair * 128, (pair + 1) * 128)
        query = split_heads(query_ref[:, span], first)
        upper = split_heads(upper_ref[:, span], first)
        key, value = keys_ref[:, span], values_ref[:, span]
        scores = product_right_t(query, key) * scaling
        d_prob = product_right_t(upper, value)
        probs_low, d_score = [], []
        for inner in range(2):
            head = pair * 2 + inner
            mine = scores[inner * count : (inner + 1) * count]
            parts = [mine[:, :count] + causal]
            for i in range(4):
                bias = jnp.where(links_ref[head, i] > 0, 0.0, hidden)
                parts.append(mine[:, (i + 1) * count : (i + 2) * count] + bias)
            mine = jnp.concatenate(parts, axis=1)
            highest = jnp.max(mine, axis=1, keepdims=True)
            weight = jnp.exp(mine - highest)
            inverse = 1.0 / jnp.sum(weight, axis=1, keepdims=True)
            probs = weight * inverse
            slope = d_prob[inner * count : (inner + 1) * count]
            centre = jnp.sum(probs * slope, axis=1, keepdims=True)
            probs_low.append(probs.astype(bf16))
            d_score.append((probs * (slope - centre) * scaling).astype(bf16))
            table = jnp.where(lane == head, highest, table)
            table = jnp.where(lane == 8 + head, inverse, table)
            table = jnp.where(lane == 16 + head, centre, table)
        attn = product(jnp.concatenate(probs_low, axis=0), value)
        attn_ref[:, span] = join_heads(attn, first).astype(bf16)
        d_query = product(jnp.concatenate(d_score, axis=0), key)
        d_query_ref[:, span] = join_heads(d_query, first).astype(bf16)
    across = jnp.transpose(table)
    own_stats_ref[...] = across[:24]
    for i in range(4):
        stats_ref[i, :8] = jnp.maximum(across[:8], barred_ref[i])
        stats_ref[i, 8:] = across[8:24]
    mixed = window_ref[edge:].astype(f32) + product(attn_ref[...], weights_ref[7])
    mixed_ref[...] = mixed.astype(bf16)


def later_kernel(
    own_ref, one_ref, two_ref, four_ref, eight_ref, gain_ref, weights_ref,
    queries_ref, uppers_ref,
    lines_ref, cots_ref,
):
    gain = gain_ref[...]
    count = own_ref.shape[0]
    one = jnp.concatenate([own_ref[count - edge :], one_ref[:count]], axis=0)
    size = count + edge
    windows = (one, two_ref[:size], four_ref[:size], eight_ref[:size])
    cots = (one_ref[count:], two_ref[size:], four_ref[size:], eight_ref[size:])
    for slot in range(4):
        rows = slice(slot * count, (slot + 1) * count)
        cots_ref[rows] = cots[slot]
        for tap, part in enumerate(normed_taps(windows[slot], gain)):
            lines_ref[tap, rows] = part
    queries = product(lines_ref[0], weights_ref[4])
    queries = queries + product(lines_ref[1], weights_ref[5])
    queries_ref[...] = (queries + product(lines_ref[2], weights_ref[6])).astype(bf16)
    uppers_ref[...] = product_right_t(cots_ref[...], weights_ref[7]).astype(bf16)


def store_partials(even, term, keep_ref, send_ref, matrix):
    term = term.astype(bf16)
    for chip in range(8):
        low = term[chip * 64 : chip * 64 + 32]
        high = term[chip * 64 + 32 : chip * 64 + 64]
        keep_ref[chip, matrix] = jnp.where(even, low, high)
        send_ref[chip, matrix] = jnp.where(even, high, low)


def partials_kernel(core_ref, taps_ref, d_query_ref, attn_ref, upstream_ref, keep_ref, send_ref):
    even = core_ref[0] == 0
    for tap in range(3):
        term = product_left_t(taps_ref[tap], d_query_ref[...])
        store_partials(even, term, keep_ref, send_ref, tap)
    term = product_left_t(attn_ref[...], upstream_ref[...])
    store_partials(even, term, keep_ref, send_ref, 3)


def columns_kernel(
    core_ref, key_ref, value_ref, query_ref, upper_ref, queries_ref, uppers_ref, taps_ref,
    own_ref, one_ref, two_ref, four_ref, eight_ref,
    d_key_ref, d_value_ref, keep_ref, send_ref,
):
    even = core_ref[0] == 0
    count = key_ref.shape[0]
    lane = lax.broadcasted_iota(jnp.int32, (count, 128), 1)
    row = lax.broadcasted_iota(jnp.int32, (count, 128), 0)
    first = lane < 64
    causal = jnp.concatenate([row <= lane] * 2, axis=1)
    scaling = 64 ** (-0.5)
    all_stats = [own_ref[...], one_ref[...], two_ref[...], four_ref[...], eight_ref[...]]
    all_stats = [
        (jnp.where(stats[8:16] > 0.0, stats[:8], 1e30), stats[8:16], stats[16:24])
        for stats in all_stats
    ]
    for pair in range(4):
        span = slice(pair * 128, (pair + 1) * 128)
        key, value = key_ref[:, span], value_ref[:, span]
        d_key = jnp.zeros((count, 128), f32)
        d_value = jnp.zeros((count, 128), f32)
        for slot in range(5):
            if slot == 0:
                query, upper = query_ref[:, span], upper_ref[:, span]
            else:
                rows = slice((slot - 1) * count, slot * count)
                query, upper = queries_ref[rows, span], uppers_ref[rows, span]
            query, upper = split_heads(query, first), split_heads(upper, first)
            highest, inverse, centre = [
                jnp.concatenate([part[pair * 2 : pair * 2 + 1], part[pair * 2 + 1 : pair * 2 + 2]], axis=1)
                for part in all_stats[slot]
            ]
            scores = product_right_t(key, query) * scaling
            probs = jnp.exp(scores - highest) * inverse
            if slot == 0:
                probs = jnp.where(causal, probs, 0.0)
            d_prob = product_right_t(value, upper)
            d_score = (probs * (d_prob - centre) * scaling).astype(bf16)
            d_key = d_key + product(d_score, query)
            d_value = d_value + product(probs.astype(bf16), upper)
        d_key_ref[:, span] = d_key.astype(bf16)
        d_value_ref[:, span] = d_value.astype(bf16)
    for tap in range(3):
        term = product_left_t(taps_ref[tap], d_key_ref[...])
        store_partials(even, term, keep_ref, send_ref, tap)
    store_partials(even, product_left_t(taps_ref[0], d_value_ref[...]), keep_ref, send_ref, 3)


def series_kernel(
    d_query_ref, d_key_ref, d_value_ref, leading_ref, weights_ref, own_ref, upstream_ref, gain_ref,
    grad_ref, d_gain_ref,
):
    count, features = own_ref.shape
    d_normed = product_right_t(d_value_ref[...], weights_ref[3])
    for which, (ref, base) in enumerate(((d_query_ref, 4), (d_key_ref, 0))):
        after = leading_ref[:, which * features : (which + 1) * features]
        window = jnp.concatenate([ref[...], after], axis=0).astype(f32)
        for tap in range(3):
            part = window[tap : tap + count].astype(bf16)
            d_normed = d_normed + product_right_t(part, weights_ref[base + tap])
    values = own_ref[...].astype(f32)
    scale = inverse_rms(values)
    d_gain_ref[...] = jnp.sum(d_normed * values * scale, axis=0, keepdims=True)
    slope = d_normed * gain_ref[...]
    along = jnp.mean(slope * values, axis=-1, keepdims=True)
    d_values = scale * slope - values * (scale * scale * scale * along)
    grad_ref[...] = (upstream_ref[...].astype(f32) + d_values).astype(bf16)


def reduce_rows(keep, send):
    half = (keep.astype(f32) + other_core(send).astype(f32)).astype(bf16)
    return jnp.sum(over_chips(half).astype(f32), axis=0).astype(bf16)


def body(
    series, norm_gain, query_kernel, key_kernel, value_weight, out_weight, block_links, grad_out
):
    core = (lax.axis_index("dp") % 2).reshape(1)
    block = lax.axis_index("ctx")
    heads = block_links.shape[2]
    own, cotangent = series[0], grad_out[0]
    count, features = own.shape
    gain = norm_gain.reshape(1, features)
    shard = jnp.concatenate(
        [key_kernel, value_weight[None], query_kernel, out_weight[None]], axis=0
    )
    mine = over_chips(jnp.broadcast_to(shard[None], (8,) + shard.shape))

    before_one = shift_ctx(own, 1)
    after_one = shift_ctx(jnp.concatenate([own, cotangent], axis=0), -1)
    window = jnp.concatenate([before_one[count - edge :], own], axis=0)
    before_two = shift_ctx(window, 2)
    after_two = shift_ctx(jnp.concatenate([window, cotangent], axis=0), -2)
    before_four = shift_ctx(before_two, 2)
    after_four = shift_ctx(after_two, -2)
    before_eight = shift_ctx(before_four, 4)
    after_eight = shift_ctx(after_four, -4)
    other = other_core(mine)

    offsets = jnp.array(block_offsets, dtype=jnp.int32)
    reach = (block_links[0, 0] > 0) & (block >= offsets)[None, :]
    barred = jnp.where(reach.T[:, :, None], -3e38, 1e30).astype(f32)
    barred = jnp.broadcast_to(barred, (4, heads, 128))

    half = ((count, features), bf16)
    (
        weights, mixed, attn, d_query, query, upper, key, value, taps, own_stats, stats
    ) = call(
        rows_kernel,
        [((8, features, features), bf16)] + [half] * 7
        + [((3, count, features), bf16), ((24, count), f32), ((4, 24, count), f32)],
        [
            pltpu.VMEM((3, 5 * count, features), bf16),
            pltpu.VMEM((5 * count, features), bf16),
            pltpu.VMEM((5 * count, features), bf16),
        ],
        smem=2,
        inputs=12,
    )(
        core, reach.astype(jnp.int32), mine, other, window, before_one, before_two, before_four,
        before_eight, cotangent, gain, barred,
    )
    returned = [shift_ctx(stats[i], -block_offsets[i]) for i in range(4)]
    parts = ((8, 4, 32, features), bf16)
    keep, send = call(partials_kernel, [parts, parts], smem=1, inputs=5)(
        core, taps, d_query, attn, cotangent
    )
    queries, uppers = call(
        later_kernel,
        [((4 * count, features), bf16)] * 2,
        [pltpu.VMEM((3, 4 * count, features), bf16), pltpu.VMEM((4 * count, features), bf16)],
        inputs=7,
    )(own, after_one, after_two, after_four, after_eight, gain, weights)
    rows_query = reduce_rows(keep, send)
    d_key, d_value, keep, send = call(
        columns_kernel, [half, half, parts, parts], smem=1, inputs=13
    )(core, key, value, query, upper, queries, uppers, taps, own_stats, *returned)
    leading = shift_ctx(jnp.concatenate([d_query[:edge], d_key[:edge]], axis=1), -1)
    rows_key = reduce_rows(keep, send)
    grad_series, d_gain = call(
        series_kernel, [half, ((1, features), f32)], inputs=8
    )(d_query, d_key, d_value, leading, weights, own, cotangent, gain)

    d_gain = jnp.broadcast_to(d_gain.reshape(1, 4, 128), (16, 4, 128))
    d_gain = jnp.sum(lax.all_to_all(d_gain, "dp", 0, 0, tiled=True), axis=0)
    top = d_gain.astype(bf16)
    rest = (d_gain - top.astype(f32)).astype(bf16)
    extra = jnp.broadcast_to(jnp.concatenate([top, rest], axis=0)[None], (32, 8, 128))
    rows = jnp.concatenate([rows_query, rows_key], axis=0).reshape(32, 8, features)
    payload = jnp.concatenate([rows, extra], axis=2)
    arrived = lax.all_to_all(payload, "ctx", 0, 0, tiled=True).astype(f32)
    summed = jnp.sum(arrived, axis=0)
    gain_total = (summed[:4, features:] + summed[4:, features:]).reshape(features)
    summed = summed[:, :features].astype(bf16)
    final = lax.all_to_all(
        jnp.broadcast_to(summed[None], (32, 8, features)), "ctx", 0, 0, tiled=True
    )
    final = final.reshape(8, 32, features).astype(f32)
    return (mixed[None], grad_series[None], gain_total, final[:3], final[4:7], final[7], final[3])


def solution(mesh):
    placed = (
        P("dp", "ctx", None),
        P(),
        P(None, "dp", None),
        P(None, "dp", None),
        P("dp", None),
        P("dp", None),
        P("dp", "ctx", None, None),
        P("dp", "ctx", None),
    )
    return jax.shard_map(
        body,
        mesh=mesh,
        in_specs=placed,
        out_specs=(
            P("dp", "ctx", None),
            P("dp", "ctx", None),
            P(),
            P(None, "dp", None),
            P(None, "dp", None),
            P("dp", None),
            P("dp", None),
        ),
        check_vma=False,
    )
```

```python
import jax
import jax.numpy as jnp
from jax import lax
from jax.experimental import pallas as pl
from jax.experimental.pallas import tpu as pltpu
from jax.sharding import PartitionSpec as P

block_offsets = (1, 2, 4, 8)
epsilon = 1e-06
hidden = -1e30
f32 = jnp.float32
bf16 = jnp.bfloat16
edge = 16
chip_groups = [[2 * i + c for i in range(8)] for c in range(2)]


def shift_ctx(shard, by):
    devices = lax.axis_size("ctx")
    pairs = [(i, i + by) for i in range(devices) if 0 <= i + by < devices]
    return lax.ppermute(shard, "ctx", pairs)


def other_core(shard):
    return lax.ppermute(shard, "dp", [(i, i ^ 1) for i in range(16)])


def over_chips(stacked):
    return lax.all_to_all(stacked, "dp", 0, 0, axis_index_groups=chip_groups, tiled=True)


def product(left, right):
    return jnp.dot(left, right, preferred_element_type=f32)


def product_right_t(left, right):
    return lax.dot_general(left, right, (((1,), (1,)), ((), ())), preferred_element_type=f32)


def product_left_t(left, right):
    return lax.dot_general(left, right, (((0,), (0,)), ((), ())), preferred_element_type=f32)


def in_two(values):
    top = values.astype(bf16)
    return top, (values - top.astype(f32)).astype(bf16)


def inverse_rms(values):
    return lax.rsqrt(jnp.mean(values * values, axis=-1, keepdims=True) + epsilon)


def normed_taps(window, gain):
    values = window.astype(f32)
    normed = values * inverse_rms(values) * gain
    count = window.shape[0] - edge
    return [normed[edge - tap : edge - tap + count].astype(bf16) for tap in range(3)]


def call(kernel, outs, scratch=(), smem=0, inputs=0):
    return pl.pallas_call(
        kernel,
        out_shape=[jax.ShapeDtypeStruct(shape, kind) for shape, kind in outs],
        in_specs=[pl.BlockSpec(memory_space=pltpu.SMEM)] * smem
        + [pl.BlockSpec(memory_space=pltpu.VMEM)] * (inputs - smem),
        out_specs=[pl.BlockSpec(memory_space=pltpu.VMEM)] * len(outs),
        scratch_shapes=list(scratch),
        compiler_params=pltpu.CompilerParams(vmem_limit_bytes=50 * 1024 * 1024),
    )


def split_heads(pair, first):
    wide = pair.astype(f32)
    return jnp.concatenate(
        [jnp.where(first, wide, 0.0), jnp.where(first, 0.0, wide)], axis=0
    ).astype(bf16)


def join_heads(stacked, first):
    count = stacked.shape[0] // 2
    return jnp.where(first, stacked[:count], stacked[count:])


def rows_kernel(
    core_ref, links_ref, mine_ref, other_ref, window_ref, one_ref, two_ref, four_ref, eight_ref,
    upstream_ref, gain_ref, barred_ref,
    weights_ref, mixed_ref, attn_ref, d_query_ref, query_ref, upper_ref, key_ref, value_ref,
    taps_ref, own_stats_ref, stats_ref,
    lines_ref, keys_ref, values_ref,
):
    even = core_ref[0] == 0
    for chip in range(8):
        for matrix in range(8):
            mine, other = mine_ref[chip, matrix], other_ref[chip, matrix]
            weights_ref[matrix, chip * 64 : chip * 64 + 32] = jnp.where(even, mine, other)
            weights_ref[matrix, chip * 64 + 32 : chip * 64 + 64] = jnp.where(even, other, mine)
    gain = gain_ref[...]
    count = one_ref.shape[0]
    one = jnp.concatenate([two_ref[count:], one_ref[...]], axis=0)
    for slot, window in enumerate(
        (window_ref[...], one, two_ref[...], four_ref[...], eight_ref[...])
    ):
        for tap, part in enumerate(normed_taps(window, gain)):
            lines_ref[tap, slot * count : (slot + 1) * count] = part
    for tap in range(3):
        taps_ref[tap] = lines_ref[tap, :count]
    keys = product(lines_ref[0], weights_ref[0])
    keys = keys + product(lines_ref[1], weights_ref[1])
    keys_ref[...] = (keys + product(lines_ref[2], weights_ref[2])).astype(bf16)
    values_ref[...] = product(lines_ref[0], weights_ref[3]).astype(bf16)
    query = product(taps_ref[0], weights_ref[4])
    query = query + product(taps_ref[1], weights_ref[5])
    query_ref[...] = (query + product(taps_ref[2], weights_ref[6])).astype(bf16)
    upper_ref[...] = product_right_t(upstream_ref[...], weights_ref[7]).astype(bf16)
    key_ref[...] = keys_ref[:count]
    value_ref[...] = values_ref[:count]

    lane = lax.broadcasted_iota(jnp.int32, (count, 128), 1)
    row = lax.broadcasted_iota(jnp.int32, (count, 128), 0)
    first = lane < 64
    causal = jnp.where(lane <= row, 0.0, hidden)
    table = jnp.zeros((count, 128), f32)
    scaling = 64 ** (-0.5)
    for pair in range(4):
        span = slice(pair * 128, (pair + 1) * 128)
        query = split_heads(query_ref[:, span], first)
        upper = split_heads(upper_ref[:, span], first)
        key, value = keys_ref[:, span], values_ref[:, span]
        scores = product_right_t(query, key) * scaling
        d_prob = product_right_t(upper, value)
        probs_low, d_score = [], []
        for inner in range(2):
            head = pair * 2 + inner
            mine = scores[inner * count : (inner + 1) * count]
            parts = [mine[:, :count] + causal]
            for i in range(4):
                bias = jnp.where(links_ref[head, i] > 0, 0.0, hidden)
                parts.append(mine[:, (i + 1) * count : (i + 2) * count] + bias)
            mine = jnp.concatenate(parts, axis=1)
            highest = jnp.max(mine, axis=1, keepdims=True)
            weight = jnp.exp(mine - highest)
            inverse = 1.0 / jnp.sum(weight, axis=1, keepdims=True)
            probs = weight * inverse
            slope = d_prob[inner * count : (inner + 1) * count]
            centre = jnp.sum(probs * slope, axis=1, keepdims=True)
            probs_low.append(probs.astype(bf16))
            d_score.append((probs * (slope - centre) * scaling).astype(bf16))
            table = jnp.where(lane == head, highest, table)
            table = jnp.where(lane == 8 + head, inverse, table)
            table = jnp.where(lane == 16 + head, centre, table)
        attn = product(jnp.concatenate(probs_low, axis=0), value)
        attn_ref[:, span] = join_heads(attn, first).astype(bf16)
        d_query = product(jnp.concatenate(d_score, axis=0), key)
        d_query_ref[:, span] = join_heads(d_query, first).astype(bf16)
    across = jnp.transpose(table)
    own_stats_ref[...] = across[:24]
    for i in range(4):
        stats_ref[i, :8] = jnp.maximum(across[:8], barred_ref[i])
        stats_ref[i, 8:] = across[8:24]
    mixed = window_ref[edge:].astype(f32) + product(attn_ref[...], weights_ref[7])
    mixed_ref[...] = mixed.astype(bf16)


def later_kernel(
    own_ref, one_ref, two_ref, four_ref, eight_ref, gain_ref, weights_ref,
    queries_ref, uppers_ref,
    lines_ref, cots_ref,
):
    gain = gain_ref[...]
    count = own_ref.shape[0]
    one = jnp.concatenate([own_ref[count - edge :], one_ref[:count]], axis=0)
    size = count + edge
    windows = (one, two_ref[:size], four_ref[:size], eight_ref[:size])
    cots = (one_ref[count:], two_ref[size:], four_ref[size:], eight_ref[size:])
    for slot in range(4):
        rows = slice(slot * count, (slot + 1) * count)
        cots_ref[rows] = cots[slot]
        for tap, part in enumerate(normed_taps(windows[slot], gain)):
            lines_ref[tap, rows] = part
    queries = product(lines_ref[0], weights_ref[4])
    queries = queries + product(lines_ref[1], weights_ref[5])
    queries_ref[...] = (queries + product(lines_ref[2], weights_ref[6])).astype(bf16)
    uppers_ref[...] = product_right_t(cots_ref[...], weights_ref[7]).astype(bf16)


def store_partials(even, term, keep_ref, send_ref, matrix):
    term = term.astype(bf16)
    for chip in range(8):
        low = term[chip * 64 : chip * 64 + 32]
        high = term[chip * 64 + 32 : chip * 64 + 64]
        keep_ref[chip, matrix] = jnp.where(even, low, high)
        send_ref[chip, matrix] = jnp.where(even, high, low)


def partials_kernel(core_ref, taps_ref, d_query_ref, attn_ref, upstream_ref, keep_ref, send_ref):
    even = core_ref[0] == 0
    for tap in range(3):
        term = product_left_t(taps_ref[tap], d_query_ref[...])
        store_partials(even, term, keep_ref, send_ref, tap)
    term = product_left_t(attn_ref[...], upstream_ref[...])
    store_partials(even, term, keep_ref, send_ref, 3)


def columns_kernel(
    core_ref, key_ref, value_ref, query_ref, upper_ref, queries_ref, uppers_ref, taps_ref,
    own_ref, one_ref, two_ref, four_ref, eight_ref,
    d_key_ref, d_value_ref, keep_ref, send_ref,
):
    even = core_ref[0] == 0
    count = key_ref.shape[0]
    lane = lax.broadcasted_iota(jnp.int32, (count, 128), 1)
    row = lax.broadcasted_iota(jnp.int32, (count, 128), 0)
    first = lane < 64
    causal = jnp.concatenate([row <= lane] * 2, axis=1)
    scaling = 64 ** (-0.5)
    all_stats = [own_ref[...], one_ref[...], two_ref[...], four_ref[...], eight_ref[...]]
    all_stats = [
        (jnp.where(stats[8:16] > 0.0, stats[:8], 1e30), stats[8:16], stats[16:24])
        for stats in all_stats
    ]
    for pair in range(4):
        span = slice(pair * 128, (pair + 1) * 128)
        key, value = key_ref[:, span], value_ref[:, span]
        d_key = jnp.zeros((count, 128), f32)
        d_value = jnp.zeros((count, 128), f32)
        for slot in range(5):
            if slot == 0:
                query, upper = query_ref[:, span], upper_ref[:, span]
            else:
                rows = slice((slot - 1) * count, slot * count)
                query, upper = queries_ref[rows, span], uppers_ref[rows, span]
            query, upper = split_heads(query, first), split_heads(upper, first)
            highest, inverse, centre = [
                jnp.concatenate([part[pair * 2 : pair * 2 + 1], part[pair * 2 + 1 : pair * 2 + 2]], axis=1)
                for part in all_stats[slot]
            ]
            scores = product_right_t(key, query) * scaling
            probs = jnp.exp(scores - highest) * inverse
            if slot == 0:
                probs = jnp.where(causal, probs, 0.0)
            d_prob = product_right_t(value, upper)
            d_score = (probs * (d_prob - centre) * scaling).astype(bf16)
            d_key = d_key + product(d_score, query)
            d_value = d_value + product(probs.astype(bf16), upper)
        d_key_ref[:, span] = d_key.astype(bf16)
        d_value_ref[:, span] = d_value.astype(bf16)
    for tap in range(3):
        term = product_left_t(taps_ref[tap], d_key_ref[...])
        store_partials(even, term, keep_ref, send_ref, tap)
    store_partials(even, product_left_t(taps_ref[0], d_value_ref[...]), keep_ref, send_ref, 3)


def series_kernel(
    d_query_ref, d_key_ref, d_value_ref, leading_ref, weights_ref, own_ref, upstream_ref, gain_ref,
    grad_ref, d_gain_ref,
):
    count, features = own_ref.shape
    d_normed = product_right_t(d_value_ref[...], weights_ref[3])
    for which, (ref, base) in enumerate(((d_query_ref, 4), (d_key_ref, 0))):
        after = leading_ref[:, which * features : (which + 1) * features]
        window = jnp.concatenate([ref[...], after], axis=0).astype(f32)
        for tap in range(3):
            part = window[tap : tap + count].astype(bf16)
            d_normed = d_normed + product_right_t(part, weights_ref[base + tap])
    values = own_ref[...].astype(f32)
    scale = inverse_rms(values)
    top, rest = in_two(jnp.sum(d_normed * values * scale, axis=0, keepdims=True))
    blank = jnp.zeros((d_gain_ref.shape[0] - 2, features), f32)
    d_gain_ref[...] = jnp.concatenate(
        [top.astype(f32), rest.astype(f32), blank], axis=0
    ).astype(bf16)
    slope = d_normed * gain_ref[...]
    along = jnp.mean(slope * values, axis=-1, keepdims=True)
    d_values = scale * slope - values * (scale * scale * scale * along)
    grad_ref[...] = (upstream_ref[...].astype(f32) + d_values).astype(bf16)


def halve(keep, send):
    return (keep.astype(f32) + other_core(send).astype(f32)).astype(bf16)


def body(
    series, norm_gain, query_kernel, key_kernel, value_weight, out_weight, block_links, grad_out
):
    core = (lax.axis_index("dp") % 2).reshape(1)
    block = lax.axis_index("ctx")
    heads = block_links.shape[2]
    own, cotangent = series[0], grad_out[0]
    count, features = own.shape
    gain = norm_gain.reshape(1, features)

    before_one = shift_ctx(own, 1)
    after_one = shift_ctx(jnp.concatenate([own, cotangent], axis=0), -1)
    window = jnp.concatenate([before_one[count - edge :], own], axis=0)
    carried = jnp.concatenate([window, cotangent], axis=0)
    before_four, before_two = shift_ctx(window, 4), shift_ctx(window, 2)
    after_four, after_two = shift_ctx(carried, -4), shift_ctx(carried, -2)
    before_eight, after_eight = shift_ctx(before_four, 4), shift_ctx(after_four, -4)
    shard = jnp.concatenate(
        [key_kernel, value_weight[None], query_kernel, out_weight[None]], axis=0
    )
    mine = lax.all_gather(
        shard.reshape(256, features), "dp", axis=0, axis_index_groups=chip_groups, tiled=True
    ).reshape(8, 8, 32, features)
    (
        mine, before_two, before_four, before_eight, after_one, after_two, after_four, after_eight
    ) = lax.optimization_barrier(
        (mine, before_two, before_four, before_eight, after_one, after_two, after_four, after_eight)
    )
    other = other_core(mine)

    offsets = jnp.array(block_offsets, dtype=jnp.int32)
    reach = (block_links[0, 0] > 0) & (block >= offsets)[None, :]
    barred = jnp.where(reach.T[:, :, None], -3e38, 1e30).astype(f32)
    barred = jnp.broadcast_to(barred, (4, heads, 128))

    half = ((count, features), bf16)
    (
        weights, mixed, attn, d_query, query, upper, key, value, taps, own_stats, stats
    ) = call(
        rows_kernel,
        [((8, features, features), bf16)] + [half] * 7
        + [((3, count, features), bf16), ((24, count), f32), ((4, 24, count), f32)],
        [
            pltpu.VMEM((3, 5 * count, features), bf16),
            pltpu.VMEM((5 * count, features), bf16),
            pltpu.VMEM((5 * count, features), bf16),
        ],
        smem=2,
        inputs=12,
    )(
        core, reach.astype(jnp.int32), mine, other, window, before_one, before_two, before_four,
        before_eight, cotangent, gain, barred,
    )
    returned = [shift_ctx(stats[i], -block_offsets[i]) for i in range(4)]
    parts = ((8, 4, 32, features), bf16)
    keep, send = call(partials_kernel, [parts, parts], smem=1, inputs=5)(
        core, taps, d_query, attn, cotangent
    )
    queries, uppers = call(
        later_kernel,
        [((4 * count, features), bf16)] * 2,
        [pltpu.VMEM((3, 4 * count, features), bf16), pltpu.VMEM((4 * count, features), bf16)],
        inputs=7,
    )(own, after_one, after_two, after_four, after_eight, gain, weights)
    partial = halve(keep, send)
    partial, queries, uppers = lax.optimization_barrier((partial, queries, uppers))
    rows_query = jnp.sum(over_chips(partial).astype(f32), axis=0).astype(bf16)
    rows_query, key = lax.optimization_barrier((rows_query, key))
    d_key, d_value, keep, send = call(
        columns_kernel, [half, half, parts, parts], smem=1, inputs=13
    )(core, key, value, query, upper, queries, uppers, taps, own_stats, *returned)
    leading = shift_ctx(jnp.concatenate([d_query[:edge], d_key[:edge]], axis=1), -1)
    partial = halve(keep, send).reshape(8, 128, features)
    grad_series, d_gain = call(
        series_kernel, [half, ((edge, features), bf16)], inputs=8
    )(d_query, d_key, d_value, leading, weights, own, cotangent, gain)
    d_gain = jnp.broadcast_to(d_gain[None], (8, edge, features))
    arrived = over_chips(jnp.concatenate([partial, d_gain], axis=1))
    arrived = jnp.sum(arrived.astype(f32), axis=0)
    rows_key = arrived[:128].astype(bf16).reshape(4, 32, features)
    chip_gain = jnp.sum(arrived[128:], axis=0).reshape(4, 128)
    top, rest = in_two(chip_gain)
    extra = jnp.broadcast_to(jnp.concatenate([top, rest], axis=0)[None], (32, 8, 128))
    rows = jnp.concatenate([rows_query, rows_key], axis=0).reshape(32, 8, features)
    payload = jnp.concatenate([rows, extra], axis=2)
    arrived = lax.all_to_all(payload, "ctx", 0, 0, tiled=True).astype(f32)
    summed = jnp.sum(arrived, axis=0)
    core_gain = summed[:4, features:] + summed[4:, features:]
    gain_total = (core_gain + other_core(core_gain)).reshape(features)
    summed = summed[:, :features].astype(bf16)
    final = lax.all_to_all(
        jnp.broadcast_to(summed[None], (32, 8, features)), "ctx", 0, 0, tiled=True
    )
    final = final.reshape(8, 32, features).astype(f32)
    return (mixed[None], grad_series[None], gain_total, final[:3], final[4:7], final[7], final[3])


def solution(mesh):
    placed = (
        P("dp", "ctx", None),
        P(),
        P(None, "dp", None),
        P(None, "dp", None),
        P("dp", None),
        P("dp", None),
        P("dp", "ctx", None, None),
        P("dp", "ctx", None),
    )
    return jax.shard_map(
        body,
        mesh=mesh,
        in_specs=placed,
        out_specs=(
            P("dp", "ctx", None),
            P("dp", "ctx", None),
            P(),
            P(None, "dp", None),
            P(None, "dp", None),
            P("dp", None),
            P("dp", None),
        ),
        check_vma=False,
    )
```

```python
import jax
import jax.numpy as jnp
from jax import lax
from jax.experimental import pallas as pl
from jax.experimental.pallas import tpu as pltpu
from jax.sharding import PartitionSpec as P

block_offsets = (1, 2, 4, 8)
epsilon = 1e-06
hidden = -1e30
f32 = jnp.float32
bf16 = jnp.bfloat16
edge = 16
chip_groups = [[2 * i + c for i in range(8)] for c in range(2)]


def shift_ctx(shard, by):
    devices = lax.axis_size("ctx")
    pairs = [(i, i + by) for i in range(devices) if 0 <= i + by < devices]
    return lax.ppermute(shard, "ctx", pairs)


def dp_to(shard, dx, dy, dc):
    def target(i):
        x, y, c = i // 8, (i // 2) % 4, i % 2
        return ((x + dx) % 2) * 8 + ((y + dy) % 4) * 2 + (c + dc) % 2

    return lax.ppermute(shard, "dp", [(i, target(i)) for i in range(16)])


def other_core(shard):
    return dp_to(shard, 0, 0, 1)


def over_chips(stacked):
    return lax.all_to_all(stacked, "dp", 0, 0, axis_index_groups=chip_groups, tiled=True)


def product(left, right):
    return jnp.dot(left, right, preferred_element_type=f32)


def product_right_t(left, right):
    return lax.dot_general(left, right, (((1,), (1,)), ((), ())), preferred_element_type=f32)


def product_left_t(left, right):
    return lax.dot_general(left, right, (((0,), (0,)), ((), ())), preferred_element_type=f32)


def in_two(values):
    top = values.astype(bf16)
    return top, (values - top.astype(f32)).astype(bf16)


def inverse_rms(values):
    return lax.rsqrt(jnp.mean(values * values, axis=-1, keepdims=True) + epsilon)


def normed_taps(window, gain):
    values = window.astype(f32)
    normed = values * inverse_rms(values) * gain
    count = window.shape[0] - edge
    return [normed[edge - tap : edge - tap + count].astype(bf16) for tap in range(3)]


def call(kernel, outs, scratch=(), smem=0, inputs=0):
    return pl.pallas_call(
        kernel,
        out_shape=[jax.ShapeDtypeStruct(shape, kind) for shape, kind in outs],
        in_specs=[pl.BlockSpec(memory_space=pltpu.SMEM)] * smem
        + [pl.BlockSpec(memory_space=pltpu.VMEM)] * (inputs - smem),
        out_specs=[pl.BlockSpec(memory_space=pltpu.VMEM)] * len(outs),
        scratch_shapes=list(scratch),
        compiler_params=pltpu.CompilerParams(vmem_limit_bytes=50 * 1024 * 1024),
    )


def split_heads(pair, first):
    wide = pair.astype(f32)
    return jnp.concatenate(
        [jnp.where(first, wide, 0.0), jnp.where(first, 0.0, wide)], axis=0
    ).astype(bf16)


def join_heads(stacked, first):
    count = stacked.shape[0] // 2
    return jnp.where(first, stacked[:count], stacked[count:])


def rows_kernel(
    place_ref, links_ref, mine_0, mine_1, mine_2, mine_3, other_0, other_1, other_2, other_3,
    window_ref, one_ref, two_ref, four_ref, eight_ref, upstream_ref, gain_ref, barred_ref,
    weights_ref, mixed_ref, attn_ref, d_query_ref, query_ref, upper_ref, key_ref, value_ref,
    taps_ref, own_stats_ref, stats_ref,
    lines_ref, keys_ref, values_ref,
):
    x, y, core = place_ref[0], place_ref[1], place_ref[2]
    pieces = ((mine_0, other_0), (mine_1, other_1), (mine_2, other_2), (mine_3, other_3))
    for back in range(4):
        for side in range(2):
            chip = (x if side == 0 else 1 - x) * 4 + lax.rem(y + 4 - back, 4)
            for inner in range(2):
                start = chip * 64 + (core if inner == 0 else 1 - core) * 32
                rows = pl.ds(pl.multiple_of(start, 32), 32)
                for matrix in range(8):
                    weights_ref[matrix, rows] = pieces[back][inner][side, matrix]
    gain = gain_ref[...]
    count = one_ref.shape[0]
    one = jnp.concatenate([two_ref[count:], one_ref[...]], axis=0)
    for slot, window in enumerate(
        (window_ref[...], one, two_ref[...], four_ref[...], eight_ref[...])
    ):
        for tap, part in enumerate(normed_taps(window, gain)):
            lines_ref[tap, slot * count : (slot + 1) * count] = part
    for tap in range(3):
        taps_ref[tap] = lines_ref[tap, :count]
    keys = product(lines_ref[0], weights_ref[0])
    keys = keys + product(lines_ref[1], weights_ref[1])
    keys_ref[...] = (keys + product(lines_ref[2], weights_ref[2])).astype(bf16)
    values_ref[...] = product(lines_ref[0], weights_ref[3]).astype(bf16)
    query = product(taps_ref[0], weights_ref[4])
    query = query + product(taps_ref[1], weights_ref[5])
    query_ref[...] = (query + product(taps_ref[2], weights_ref[6])).astype(bf16)
    upper_ref[...] = product_right_t(upstream_ref[...], weights_ref[7]).astype(bf16)
    key_ref[...] = keys_ref[:count]
    value_ref[...] = values_ref[:count]

    lane = lax.broadcasted_iota(jnp.int32, (count, 128), 1)
    row = lax.broadcasted_iota(jnp.int32, (count, 128), 0)
    first = lane < 64
    causal = jnp.where(lane <= row, 0.0, hidden)
    table = jnp.zeros((count, 128), f32)
    scaling = 64 ** (-0.5)
    for pair in range(4):
        span = slice(pair * 128, (pair + 1) * 128)
        query = split_heads(query_ref[:, span], first)
        upper = split_heads(upper_ref[:, span], first)
        key, value = keys_ref[:, span], values_ref[:, span]
        scores = product_right_t(query, key) * scaling
        d_prob = product_right_t(upper, value)
        probs_low, d_score = [], []
        for inner in range(2):
            head = pair * 2 + inner
            mine = scores[inner * count : (inner + 1) * count]
            parts = [mine[:, :count] + causal]
            for i in range(4):
                bias = jnp.where(links_ref[head, i] > 0, 0.0, hidden)
                parts.append(mine[:, (i + 1) * count : (i + 2) * count] + bias)
            mine = jnp.concatenate(parts, axis=1)
            highest = jnp.max(mine, axis=1, keepdims=True)
            weight = jnp.exp(mine - highest)
            inverse = 1.0 / jnp.sum(weight, axis=1, keepdims=True)
            probs = weight * inverse
            slope = d_prob[inner * count : (inner + 1) * count]
            centre = jnp.sum(probs * slope, axis=1, keepdims=True)
            probs_low.append(probs.astype(bf16))
            d_score.append((probs * (slope - centre) * scaling).astype(bf16))
            table = jnp.where(lane == head, highest, table)
            table = jnp.where(lane == 8 + head, inverse, table)
            table = jnp.where(lane == 16 + head, centre, table)
        attn = product(jnp.concatenate(probs_low, axis=0), value)
        attn_ref[:, span] = join_heads(attn, first).astype(bf16)
        d_query = product(jnp.concatenate(d_score, axis=0), key)
        d_query_ref[:, span] = join_heads(d_query, first).astype(bf16)
    across = jnp.transpose(table)
    own_stats_ref[...] = across[:24]
    for i in range(4):
        stats_ref[i, :8] = jnp.maximum(across[:8], barred_ref[i])
        stats_ref[i, 8:] = across[8:24]
    mixed = window_ref[edge:].astype(f32) + product(attn_ref[...], weights_ref[7])
    mixed_ref[...] = mixed.astype(bf16)


def later_kernel(
    own_ref, one_ref, two_ref, four_ref, eight_ref, gain_ref, weights_ref,
    queries_ref, uppers_ref,
    lines_ref, cots_ref,
):
    gain = gain_ref[...]
    count = own_ref.shape[0]
    one = jnp.concatenate([own_ref[count - edge :], one_ref[:count]], axis=0)
    size = count + edge
    windows = (one, two_ref[:size], four_ref[:size], eight_ref[:size])
    cots = (one_ref[count:], two_ref[size:], four_ref[size:], eight_ref[size:])
    for slot in range(4):
        rows = slice(slot * count, (slot + 1) * count)
        cots_ref[rows] = cots[slot]
        for tap, part in enumerate(normed_taps(windows[slot], gain)):
            lines_ref[tap, rows] = part
    queries = product(lines_ref[0], weights_ref[4])
    queries = queries + product(lines_ref[1], weights_ref[5])
    queries_ref[...] = (queries + product(lines_ref[2], weights_ref[6])).astype(bf16)
    uppers_ref[...] = product_right_t(cots_ref[...], weights_ref[7]).astype(bf16)


def store_partials(even, term, keep_ref, send_ref, matrix):
    term = term.astype(bf16)
    for chip in range(8):
        low = term[chip * 64 : chip * 64 + 32]
        high = term[chip * 64 + 32 : chip * 64 + 64]
        keep_ref[chip, matrix] = jnp.where(even, low, high)
        send_ref[chip, matrix] = jnp.where(even, high, low)


def partials_kernel(core_ref, taps_ref, d_query_ref, attn_ref, upstream_ref, keep_ref, send_ref):
    even = core_ref[0] == 0
    for tap in range(3):
        term = product_left_t(taps_ref[tap], d_query_ref[...])
        store_partials(even, term, keep_ref, send_ref, tap)
    term = product_left_t(attn_ref[...], upstream_ref[...])
    store_partials(even, term, keep_ref, send_ref, 3)


def columns_kernel(
    core_ref, key_ref, value_ref, query_ref, upper_ref, queries_ref, uppers_ref, taps_ref,
    own_ref, one_ref, two_ref, four_ref, eight_ref,
    d_key_ref, d_value_ref, keep_ref, send_ref,
):
    even = core_ref[0] == 0
    count = key_ref.shape[0]
    lane = lax.broadcasted_iota(jnp.int32, (count, 128), 1)
    row = lax.broadcasted_iota(jnp.int32, (count, 128), 0)
    first = lane < 64
    causal = jnp.concatenate([row <= lane] * 2, axis=1)
    scaling = 64 ** (-0.5)
    all_stats = [own_ref[...], one_ref[...], two_ref[...], four_ref[...], eight_ref[...]]
    all_stats = [
        (jnp.where(stats[8:16] > 0.0, stats[:8], 1e30), stats[8:16], stats[16:24])
        for stats in all_stats
    ]
    for pair in range(4):
        span = slice(pair * 128, (pair + 1) * 128)
        key, value = key_ref[:, span], value_ref[:, span]
        d_key = jnp.zeros((count, 128), f32)
        d_value = jnp.zeros((count, 128), f32)
        for slot in range(5):
            if slot == 0:
                query, upper = query_ref[:, span], upper_ref[:, span]
            else:
                rows = slice((slot - 1) * count, slot * count)
                query, upper = queries_ref[rows, span], uppers_ref[rows, span]
            query, upper = split_heads(query, first), split_heads(upper, first)
            highest, inverse, centre = [
                jnp.concatenate([part[pair * 2 : pair * 2 + 1], part[pair * 2 + 1 : pair * 2 + 2]], axis=1)
                for part in all_stats[slot]
            ]
            scores = product_right_t(key, query) * scaling
            probs = jnp.exp(scores - highest) * inverse
            if slot == 0:
                probs = jnp.where(causal, probs, 0.0)
            d_prob = product_right_t(value, upper)
            d_score = (probs * (d_prob - centre) * scaling).astype(bf16)
            d_key = d_key + product(d_score, query)
            d_value = d_value + product(probs.astype(bf16), upper)
        d_key_ref[:, span] = d_key.astype(bf16)
        d_value_ref[:, span] = d_value.astype(bf16)
    for tap in range(3):
        term = product_left_t(taps_ref[tap], d_key_ref[...])
        store_partials(even, term, keep_ref, send_ref, tap)
    store_partials(even, product_left_t(taps_ref[0], d_value_ref[...]), keep_ref, send_ref, 3)


def series_kernel(
    d_query_ref, d_key_ref, d_value_ref, leading_ref, weights_ref, own_ref, upstream_ref, gain_ref,
    grad_ref, d_gain_ref,
):
    count, features = own_ref.shape
    d_normed = product_right_t(d_value_ref[...], weights_ref[3])
    for which, (ref, base) in enumerate(((d_query_ref, 4), (d_key_ref, 0))):
        after = leading_ref[:, which * features : (which + 1) * features]
        window = jnp.concatenate([ref[...], after], axis=0).astype(f32)
        for tap in range(3):
            part = window[tap : tap + count].astype(bf16)
            d_normed = d_normed + product_right_t(part, weights_ref[base + tap])
    values = own_ref[...].astype(f32)
    scale = inverse_rms(values)
    top, rest = in_two(jnp.sum(d_normed * values * scale, axis=0, keepdims=True))
    blank = jnp.zeros((d_gain_ref.shape[0] - 2, features), f32)
    d_gain_ref[...] = jnp.concatenate(
        [top.astype(f32), rest.astype(f32), blank], axis=0
    ).astype(bf16)
    slope = d_normed * gain_ref[...]
    along = jnp.mean(slope * values, axis=-1, keepdims=True)
    d_values = scale * slope - values * (scale * scale * scale * along)
    grad_ref[...] = (upstream_ref[...].astype(f32) + d_values).astype(bf16)


def halve(keep, send):
    return (keep.astype(f32) + other_core(send).astype(f32)).astype(bf16)


def body(
    series, norm_gain, query_kernel, key_kernel, value_weight, out_weight, block_links, grad_out
):
    position = lax.axis_index("dp")
    place = jnp.stack([position // 8, (position // 2) % 4, position % 2])
    core = (position % 2).reshape(1)
    block = lax.axis_index("ctx")
    heads = block_links.shape[2]
    own, cotangent = series[0], grad_out[0]
    count, features = own.shape
    gain = norm_gain.reshape(1, features)

    shard = jnp.concatenate(
        [key_kernel, value_weight[None], query_kernel, out_weight[None]], axis=0
    )
    across = dp_to(shard, 1, 0, 0)
    before_one = shift_ctx(own, 1)
    after_one = shift_ctx(jnp.concatenate([own, cotangent], axis=0), -1)
    across, before_one = lax.optimization_barrier((across, before_one))
    shards = jnp.stack([shard, across])
    mine = [shards] + [dp_to(shards, 0, by, 0) for by in (1, 2, 3)]
    window = jnp.concatenate([before_one[count - edge :], own], axis=0)
    carried = jnp.concatenate([window, cotangent], axis=0)
    before_four, before_two = shift_ctx(window, 4), shift_ctx(window, 2)
    after_four, after_two = shift_ctx(carried, -4), shift_ctx(carried, -2)
    before_eight, after_eight = shift_ctx(before_four, 4), shift_ctx(after_four, -4)
    other = [other_core(piece) for piece in mine]
    before, after, other = lax.optimization_barrier(
        (
            (before_two, before_four, before_eight),
            (after_one, after_two, after_four, after_eight),
            other,
        )
    )

    offsets = jnp.array(block_offsets, dtype=jnp.int32)
    reach = (block_links[0, 0] > 0) & (block >= offsets)[None, :]
    barred = jnp.where(reach.T[:, :, None], -3e38, 1e30).astype(f32)
    barred = jnp.broadcast_to(barred, (4, heads, 128))

    half = ((count, features), bf16)
    (
        weights, mixed, attn, d_query, query, upper, key, value, taps, own_stats, stats
    ) = call(
        rows_kernel,
        [((8, features, features), bf16)] + [half] * 7
        + [((3, count, features), bf16), ((24, count), f32), ((4, 24, count), f32)],
        [
            pltpu.VMEM((3, 5 * count, features), bf16),
            pltpu.VMEM((5 * count, features), bf16),
            pltpu.VMEM((5 * count, features), bf16),
        ],
        smem=2,
        inputs=18,
    )(
        place, reach.astype(jnp.int32), *mine, *other, window, before_one, *before, cotangent, gain,
        barred,
    )
    returned = [shift_ctx(stats[i], -block_offsets[i]) for i in range(4)]
    parts = ((8, 4, 32, features), bf16)
    keep, send = call(partials_kernel, [parts, parts], smem=1, inputs=5)(
        core, taps, d_query, attn, cotangent
    )
    queries, uppers = call(
        later_kernel,
        [((4 * count, features), bf16)] * 2,
        [pltpu.VMEM((3, 4 * count, features), bf16), pltpu.VMEM((4 * count, features), bf16)],
        inputs=7,
    )(own, *after, gain, weights)
    partial = halve(keep, send)
    partial, queries, uppers, returned = lax.optimization_barrier(
        (partial, queries, uppers, returned)
    )
    rows_query = jnp.sum(over_chips(partial).astype(f32), axis=0).astype(bf16)
    d_key, d_value, keep, send = call(
        columns_kernel, [half, half, parts, parts], smem=1, inputs=13
    )(core, key, value, query, upper, queries, uppers, taps, own_stats, *returned)
    leading = shift_ctx(jnp.concatenate([d_query[:edge], d_key[:edge]], axis=1), -1)
    partial = halve(keep, send).reshape(8, 128, features)
    grad_series, d_gain = call(
        series_kernel, [half, ((edge, features), bf16)], inputs=8
    )(d_query, d_key, d_value, leading, weights, own, cotangent, gain)
    d_gain = jnp.broadcast_to(d_gain[None], (8, edge, features))
    partial, rows_query = lax.optimization_barrier(
        (jnp.concatenate([partial, d_gain], axis=1), rows_query)
    )
    arrived = jnp.sum(over_chips(partial).astype(f32), axis=0)
    rows_key = arrived[:128].astype(bf16).reshape(4, 32, features)
    top, rest = in_two(jnp.sum(arrived[128:], axis=0).reshape(4, 128))
    extra = jnp.broadcast_to(jnp.concatenate([top, rest], axis=0)[None], (32, 8, 128))
    rows = jnp.concatenate([rows_query, rows_key], axis=0).reshape(32, 8, features)
    payload = jnp.concatenate([rows, extra], axis=2)
    arrived = lax.all_to_all(payload, "ctx", 0, 0, tiled=True).astype(f32)
    summed = jnp.sum(arrived, axis=0)
    core_gain = summed[:4, features:] + summed[4:, features:]
    gain_total = (core_gain + other_core(core_gain)).reshape(features)
    summed = summed[:, :features].astype(bf16)
    final = lax.all_to_all(
        jnp.broadcast_to(summed[None], (32, 8, features)), "ctx", 0, 0, tiled=True
    )
    final = final.reshape(8, 32, features).astype(f32)
    return (mixed[None], grad_series[None], gain_total, final[:3], final[4:7], final[7], final[3])


def solution(mesh):
    placed = (
        P("dp", "ctx", None),
        P(),
        P(None, "dp", None),
        P(None, "dp", None),
        P("dp", None),
        P("dp", None),
        P("dp", "ctx", None, None),
        P("dp", "ctx", None),
    )
    return jax.shard_map(
        body,
        mesh=mesh,
        in_specs=placed,
        out_specs=(
            P("dp", "ctx", None),
            P("dp", "ctx", None),
            P(),
            P(None, "dp", None),
            P(None, "dp", None),
            P("dp", None),
            P("dp", None),
        ),
        check_vma=False,
    )
```

```python
import jax
import jax.numpy as jnp
from jax import lax
from jax.experimental import pallas as pl
from jax.experimental.pallas import tpu as pltpu
from jax.sharding import PartitionSpec as P

block_offsets = (1, 2, 4, 8)
epsilon = 1e-06
hidden = -1e30
f32 = jnp.float32
bf16 = jnp.bfloat16
edge = 16
plane_groups = [
    [(2 * chip + core) * 32 + 2 * z + side for chip in range(8) for side in range(2)]
    for core in range(2)
    for z in range(16)
]
z_groups = [[2 * z + side for z in range(16)] for side in range(2)]


def shift_ctx(shard, by):
    devices = lax.axis_size("ctx")
    pairs = [(i, i + by) for i in range(devices) if 0 <= i + by < devices]
    return lax.ppermute(shard, "ctx", pairs)


def dp_to(shard, dx, dy, dc):
    def target(i):
        x, y, c = i // 8, (i // 2) % 4, i % 2
        return ((x + dx) % 2) * 8 + ((y + dy) % 4) * 2 + (c + dc) % 2

    return lax.ppermute(shard, "dp", [(i, target(i)) for i in range(16)])


def other_core(shard):
    return dp_to(shard, 0, 0, 1)


def over_plane(stacked):
    return lax.all_to_all(
        stacked, ("dp", "ctx"), 0, 0, axis_index_groups=plane_groups, tiled=True
    )


def over_z(stacked):
    return lax.all_to_all(stacked, "ctx", 0, 0, axis_index_groups=z_groups, tiled=True)


def other_side(shard):
    return lax.ppermute(shard, "ctx", [(i, i ^ 1) for i in range(32)])


def product(left, right):
    return jnp.dot(left, right, preferred_element_type=f32)


def product_right_t(left, right):
    return lax.dot_general(left, right, (((1,), (1,)), ((), ())), preferred_element_type=f32)


def product_left_t(left, right):
    return lax.dot_general(left, right, (((0,), (0,)), ((), ())), preferred_element_type=f32)


def in_two(values):
    top = values.astype(bf16)
    return top, (values - top.astype(f32)).astype(bf16)


def inverse_rms(values):
    return lax.rsqrt(jnp.mean(values * values, axis=-1, keepdims=True) + epsilon)


def normed_taps(window, gain):
    values = window.astype(f32)
    normed = values * inverse_rms(values) * gain
    count = window.shape[0] - edge
    return [normed[edge - tap : edge - tap + count].astype(bf16) for tap in range(3)]


def call(kernel, outs, scratch=(), smem=0, inputs=0):
    return pl.pallas_call(
        kernel,
        out_shape=[jax.ShapeDtypeStruct(shape, kind) for shape, kind in outs],
        in_specs=[pl.BlockSpec(memory_space=pltpu.SMEM)] * smem
        + [pl.BlockSpec(memory_space=pltpu.VMEM)] * (inputs - smem),
        out_specs=[pl.BlockSpec(memory_space=pltpu.VMEM)] * len(outs),
        scratch_shapes=list(scratch),
        compiler_params=pltpu.CompilerParams(vmem_limit_bytes=50 * 1024 * 1024),
    )


def split_heads(pair, first):
    wide = pair.astype(f32)
    return jnp.concatenate(
        [jnp.where(first, wide, 0.0), jnp.where(first, 0.0, wide)], axis=0
    ).astype(bf16)


def join_heads(stacked, first):
    count = stacked.shape[0] // 2
    return jnp.where(first, stacked[:count], stacked[count:])


def rows_kernel(
    place_ref, links_ref, mine_0, mine_1, mine_2, mine_3, other_0, other_1, other_2, other_3,
    window_ref, one_ref, two_ref, four_ref, eight_ref, upstream_ref, gain_ref, barred_ref,
    weights_ref, mixed_ref, attn_ref, d_query_ref, query_ref, upper_ref, key_ref, value_ref,
    taps_ref, own_stats_ref, stats_ref,
    lines_ref, keys_ref, values_ref,
):
    x, y, core = place_ref[0], place_ref[1], place_ref[2]
    pieces = ((mine_0, other_0), (mine_1, other_1), (mine_2, other_2), (mine_3, other_3))
    for back in range(4):
        for side in range(2):
            chip = (x if side == 0 else 1 - x) * 4 + lax.rem(y + 4 - back, 4)
            for inner in range(2):
                start = chip * 64 + (core if inner == 0 else 1 - core) * 32
                rows = pl.ds(pl.multiple_of(start, 32), 32)
                for matrix in range(8):
                    weights_ref[matrix, rows] = pieces[back][inner][side, matrix]
    gain = gain_ref[...]
    count = one_ref.shape[0]
    one = jnp.concatenate([two_ref[count:], one_ref[...]], axis=0)
    for slot, window in enumerate(
        (window_ref[...], one, two_ref[...], four_ref[...], eight_ref[...])
    ):
        for tap, part in enumerate(normed_taps(window, gain)):
            lines_ref[tap, slot * count : (slot + 1) * count] = part
    for tap in range(3):
        taps_ref[tap] = lines_ref[tap, :count]
    keys = product(lines_ref[0], weights_ref[0])
    keys = keys + product(lines_ref[1], weights_ref[1])
    keys_ref[...] = (keys + product(lines_ref[2], weights_ref[2])).astype(bf16)
    values_ref[...] = product(lines_ref[0], weights_ref[3]).astype(bf16)
    query = product(taps_ref[0], weights_ref[4])
    query = query + product(taps_ref[1], weights_ref[5])
    query_ref[...] = (query + product(taps_ref[2], weights_ref[6])).astype(bf16)
    upper_ref[...] = product_right_t(upstream_ref[...], weights_ref[7]).astype(bf16)
    key_ref[...] = keys_ref[:count]
    value_ref[...] = values_ref[:count]

    lane = lax.broadcasted_iota(jnp.int32, (count, 128), 1)
    row = lax.broadcasted_iota(jnp.int32, (count, 128), 0)
    first = lane < 64
    causal = jnp.where(lane <= row, 0.0, hidden)
    table = jnp.zeros((count, 128), f32)
    scaling = 64 ** (-0.5)
    for pair in range(4):
        span = slice(pair * 128, (pair + 1) * 128)
        query = split_heads(query_ref[:, span], first)
        upper = split_heads(upper_ref[:, span], first)
        key, value = keys_ref[:, span], values_ref[:, span]
        scores = product_right_t(query, key) * scaling
        d_prob = product_right_t(upper, value)
        probs_low, d_score = [], []
        for inner in range(2):
            head = pair * 2 + inner
            mine = scores[inner * count : (inner + 1) * count]
            parts = [mine[:, :count] + causal]
            for i in range(4):
                bias = jnp.where(links_ref[head, i] > 0, 0.0, hidden)
                parts.append(mine[:, (i + 1) * count : (i + 2) * count] + bias)
            mine = jnp.concatenate(parts, axis=1)
            highest = jnp.max(mine, axis=1, keepdims=True)
            weight = jnp.exp(mine - highest)
            inverse = 1.0 / jnp.sum(weight, axis=1, keepdims=True)
            probs = weight * inverse
            slope = d_prob[inner * count : (inner + 1) * count]
            centre = jnp.sum(probs * slope, axis=1, keepdims=True)
            probs_low.append(probs.astype(bf16))
            d_score.append((probs * (slope - centre) * scaling).astype(bf16))
            table = jnp.where(lane == head, highest, table)
            table = jnp.where(lane == 8 + head, inverse, table)
            table = jnp.where(lane == 16 + head, centre, table)
        attn = product(jnp.concatenate(probs_low, axis=0), value)
        attn_ref[:, span] = join_heads(attn, first).astype(bf16)
        d_query = product(jnp.concatenate(d_score, axis=0), key)
        d_query_ref[:, span] = join_heads(d_query, first).astype(bf16)
    across = jnp.transpose(table)
    own_stats_ref[...] = across[:24]
    for i in range(4):
        stats_ref[i, :8] = jnp.maximum(across[:8], barred_ref[i])
        stats_ref[i, 8:] = across[8:24]
    mixed = window_ref[edge:].astype(f32) + product(attn_ref[...], weights_ref[7])
    mixed_ref[...] = mixed.astype(bf16)


def later_kernel(
    own_ref, one_ref, two_ref, four_ref, eight_ref, gain_ref, weights_ref,
    queries_ref, uppers_ref,
    lines_ref, cots_ref,
):
    gain = gain_ref[...]
    count = own_ref.shape[0]
    one = jnp.concatenate([own_ref[count - edge :], one_ref[:count]], axis=0)
    size = count + edge
    windows = (one, two_ref[:size], four_ref[:size], eight_ref[:size])
    cots = (one_ref[count:], two_ref[size:], four_ref[size:], eight_ref[size:])
    for slot in range(4):
        rows = slice(slot * count, (slot + 1) * count)
        cots_ref[rows] = cots[slot]
        for tap, part in enumerate(normed_taps(windows[slot], gain)):
            lines_ref[tap, rows] = part
    queries = product(lines_ref[0], weights_ref[4])
    queries = queries + product(lines_ref[1], weights_ref[5])
    queries_ref[...] = (queries + product(lines_ref[2], weights_ref[6])).astype(bf16)
    uppers_ref[...] = product_right_t(cots_ref[...], weights_ref[7]).astype(bf16)


def store_partials(even, term, keep_ref, send_ref, matrix):
    term = term.astype(bf16)
    for chip in range(8):
        low = term[chip * 64 : chip * 64 + 32]
        high = term[chip * 64 + 32 : chip * 64 + 64]
        keep_ref[chip, matrix] = jnp.where(even, low, high)
        send_ref[chip, matrix] = jnp.where(even, high, low)


def partials_kernel(core_ref, taps_ref, d_query_ref, attn_ref, upstream_ref, keep_ref, send_ref):
    even = core_ref[0] == 0
    for tap in range(3):
        term = product_left_t(taps_ref[tap], d_query_ref[...])
        store_partials(even, term, keep_ref, send_ref, tap)
    term = product_left_t(attn_ref[...], upstream_ref[...])
    store_partials(even, term, keep_ref, send_ref, 3)


def columns_kernel(
    core_ref, key_ref, value_ref, query_ref, upper_ref, queries_ref, uppers_ref, taps_ref,
    own_ref, one_ref, two_ref, four_ref, eight_ref,
    d_key_ref, d_value_ref, keep_ref, send_ref,
):
    even = core_ref[0] == 0
    count = key_ref.shape[0]
    lane = lax.broadcasted_iota(jnp.int32, (count, 128), 1)
    row = lax.broadcasted_iota(jnp.int32, (count, 128), 0)
    first = lane < 64
    causal = jnp.concatenate([row <= lane] * 2, axis=1)
    scaling = 64 ** (-0.5)
    all_stats = [own_ref[...], one_ref[...], two_ref[...], four_ref[...], eight_ref[...]]
    all_stats = [
        (jnp.where(stats[8:16] > 0.0, stats[:8], 1e30), stats[8:16], stats[16:24])
        for stats in all_stats
    ]
    for pair in range(4):
        span = slice(pair * 128, (pair + 1) * 128)
        key, value = key_ref[:, span], value_ref[:, span]
        d_key = jnp.zeros((count, 128), f32)
        d_value = jnp.zeros((count, 128), f32)
        for slot in range(5):
            if slot == 0:
                query, upper = query_ref[:, span], upper_ref[:, span]
            else:
                rows = slice((slot - 1) * count, slot * count)
                query, upper = queries_ref[rows, span], uppers_ref[rows, span]
            query, upper = split_heads(query, first), split_heads(upper, first)
            highest, inverse, centre = [
                jnp.concatenate([part[pair * 2 : pair * 2 + 1], part[pair * 2 + 1 : pair * 2 + 2]], axis=1)
                for part in all_stats[slot]
            ]
            scores = product_right_t(key, query) * scaling
            probs = jnp.exp(scores - highest) * inverse
            if slot == 0:
                probs = jnp.where(causal, probs, 0.0)
            d_prob = product_right_t(value, upper)
            d_score = (probs * (d_prob - centre) * scaling).astype(bf16)
            d_key = d_key + product(d_score, query)
            d_value = d_value + product(probs.astype(bf16), upper)
        d_key_ref[:, span] = d_key.astype(bf16)
        d_value_ref[:, span] = d_value.astype(bf16)
    for tap in range(3):
        term = product_left_t(taps_ref[tap], d_key_ref[...])
        store_partials(even, term, keep_ref, send_ref, tap)
    store_partials(even, product_left_t(taps_ref[0], d_value_ref[...]), keep_ref, send_ref, 3)


def series_kernel(
    d_query_ref, d_key_ref, d_value_ref, leading_ref, weights_ref, own_ref, upstream_ref, gain_ref,
    grad_ref, d_gain_ref,
):
    count, features = own_ref.shape
    d_normed = product_right_t(d_value_ref[...], weights_ref[3])
    for which, (ref, base) in enumerate(((d_query_ref, 4), (d_key_ref, 0))):
        after = leading_ref[:, which * features : (which + 1) * features]
        window = jnp.concatenate([ref[...], after], axis=0).astype(f32)
        for tap in range(3):
            part = window[tap : tap + count].astype(bf16)
            d_normed = d_normed + product_right_t(part, weights_ref[base + tap])
    values = own_ref[...].astype(f32)
    scale = inverse_rms(values)
    top, rest = in_two(jnp.sum(d_normed * values * scale, axis=0, keepdims=True))
    blank = jnp.zeros((d_gain_ref.shape[0] - 2, features), f32)
    d_gain_ref[...] = jnp.concatenate(
        [top.astype(f32), rest.astype(f32), blank], axis=0
    ).astype(bf16)
    slope = d_normed * gain_ref[...]
    along = jnp.mean(slope * values, axis=-1, keepdims=True)
    d_values = scale * slope - values * (scale * scale * scale * along)
    grad_ref[...] = (upstream_ref[...].astype(f32) + d_values).astype(bf16)


def halve(keep, send):
    return (keep.astype(f32) + other_core(send).astype(f32)).astype(bf16)


def body(
    series, norm_gain, query_kernel, key_kernel, value_weight, out_weight, block_links, grad_out
):
    position = lax.axis_index("dp")
    place = jnp.stack([position // 8, (position // 2) % 4, position % 2])
    core = (position % 2).reshape(1)
    block = lax.axis_index("ctx")
    heads = block_links.shape[2]
    own, cotangent = series[0], grad_out[0]
    count, features = own.shape
    gain = norm_gain.reshape(1, features)

    shard = jnp.concatenate(
        [key_kernel, value_weight[None], query_kernel, out_weight[None]], axis=0
    )
    across = dp_to(shard, 1, 0, 0)
    before_one = shift_ctx(own, 1)
    after_one = shift_ctx(jnp.concatenate([own, cotangent], axis=0), -1)
    across, before_one = lax.optimization_barrier((across, before_one))
    shards = jnp.stack([shard, across])
    mine = [shards] + [dp_to(shards, 0, by, 0) for by in (1, 2, 3)]
    window = jnp.concatenate([before_one[count - edge :], own], axis=0)
    carried = jnp.concatenate([window, cotangent], axis=0)
    before = [shift_ctx(window, by) for by in (2, 4, 8)]
    after_four, after_two = shift_ctx(carried, -4), shift_ctx(carried, -2)
    other = [other_core(piece) for piece in mine]
    before, after_one, after_two, after_four, other = lax.optimization_barrier(
        (before, after_one, after_two, after_four, other)
    )
    after = (after_one, after_two, after_four, shift_ctx(after_four, -4))

    offsets = jnp.array(block_offsets, dtype=jnp.int32)
    reach = (block_links[0, 0] > 0) & (block >= offsets)[None, :]
    barred = jnp.where(reach.T[:, :, None], -3e38, 1e30).astype(f32)
    barred = jnp.broadcast_to(barred, (4, heads, 128))

    half = ((count, features), bf16)
    (
        weights, mixed, attn, d_query, query, upper, key, value, taps, own_stats, stats
    ) = call(
        rows_kernel,
        [((8, features, features), bf16)] + [half] * 7
        + [((3, count, features), bf16), ((24, count), f32), ((4, 24, count), f32)],
        [
            pltpu.VMEM((3, 5 * count, features), bf16),
            pltpu.VMEM((5 * count, features), bf16),
            pltpu.VMEM((5 * count, features), bf16),
        ],
        smem=2,
        inputs=18,
    )(
        place, reach.astype(jnp.int32), *mine, *other, window, before_one, *before, cotangent, gain,
        barred,
    )
    returned = [shift_ctx(stats[i], -block_offsets[i]) for i in range(4)]
    parts = ((8, 4, 32, features), bf16)
    keep, send = call(partials_kernel, [parts, parts], smem=1, inputs=5)(
        core, taps, d_query, attn, cotangent
    )
    queries, uppers = call(
        later_kernel,
        [((4 * count, features), bf16)] * 2,
        [pltpu.VMEM((3, 4 * count, features), bf16), pltpu.VMEM((4 * count, features), bf16)],
        inputs=7,
    )(own, *after, gain, weights)
    query_half = halve(keep, send)
    d_key, d_value, keep, send = call(
        columns_kernel, [half, half, parts, parts], smem=1, inputs=13
    )(core, key, value, query, upper, queries, uppers, taps, own_stats, *returned)
    leading = shift_ctx(jnp.concatenate([d_query[:edge], d_key[:edge]], axis=1), -1)
    key_half = halve(keep, send)
    grad_series, d_gain = call(
        series_kernel, [half, ((edge, features), bf16)], inputs=8
    )(d_query, d_key, d_value, leading, weights, own, cotangent, gain)
    terms = jnp.stack([query_half, key_half], axis=1).reshape(16, 128, features)
    d_gain = jnp.broadcast_to(d_gain[None], (16, edge, features))
    arrived = over_plane(jnp.concatenate([terms, d_gain], axis=1))
    arrived = jnp.sum(arrived.astype(f32), axis=0)
    rows = arrived[:128].astype(bf16).reshape(16, 8, features)
    top, rest = in_two(jnp.sum(arrived[128:], axis=0).reshape(4, 128))
    extra = jnp.broadcast_to(jnp.concatenate([top, rest], axis=0)[None], (16, 8, 128))
    arrived = over_z(jnp.concatenate([rows, extra], axis=2)).astype(f32)
    summed = jnp.sum(arrived, axis=0)
    core_gain = summed[:4, features:] + summed[4:, features:]
    gain_total = (core_gain + other_core(core_gain)).reshape(features)
    summed = summed[:, :features].astype(bf16)
    mine = over_z(jnp.broadcast_to(summed[None], (16, 8, features)))
    other = other_side(mine)
    first = block % 2 == 0
    for_query = jnp.where(first, mine, other).reshape(4, 32, features).astype(f32)
    for_key = jnp.where(first, other, mine).reshape(4, 32, features).astype(f32)
    return (
        mixed[None],
        grad_series[None],
        gain_total,
        for_query[:3],
        for_key[:3],
        for_key[3],
        for_query[3],
    )


def solution(mesh):
    placed = (
        P("dp", "ctx", None),
        P(),
        P(None, "dp", None),
        P(None, "dp", None),
        P("dp", None),
        P("dp", None),
        P("dp", "ctx", None, None),
        P("dp", "ctx", None),
    )
    return jax.shard_map(
        body,
        mesh=mesh,
        in_specs=placed,
        out_specs=(
            P("dp", "ctx", None),
            P("dp", "ctx", None),
            P(),
            P(None, "dp", None),
            P(None, "dp", None),
            P("dp", None),
            P("dp", None),
        ),
        check_vma=False,
    )
```

```python
import jax
import jax.numpy as jnp
from jax import lax
from jax.experimental import pallas as pl
from jax.experimental.pallas import tpu as pltpu
from jax.sharding import PartitionSpec as P

block_offsets = (1, 2, 4, 8)
epsilon = 1e-06
hidden = -1e30
f32 = jnp.float32
bf16 = jnp.bfloat16
edge = 16
plane_groups = [
    [(2 * chip + core) * 32 + 2 * z + side for chip in range(8) for side in range(2)]
    for core in range(2)
    for z in range(16)
]
chip_groups = [[2 * chip + core for chip in range(8)] for core in range(2)]
z_groups = [[2 * z + side for z in range(16)] for side in range(2)]


def shift_ctx(shard, by):
    devices = lax.axis_size("ctx")
    pairs = [(i, i + by) for i in range(devices) if 0 <= i + by < devices]
    return lax.ppermute(shard, "ctx", pairs)


def dp_to(shard, dx, dy, dc):
    def target(i):
        x, y, c = i // 8, (i // 2) % 4, i % 2
        return ((x + dx) % 2) * 8 + ((y + dy) % 4) * 2 + (c + dc) % 2

    return lax.ppermute(shard, "dp", [(i, target(i)) for i in range(16)])


def other_core(shard):
    return dp_to(shard, 0, 0, 1)


def over_chips(stacked):
    return lax.all_to_all(stacked, "dp", 0, 0, axis_index_groups=chip_groups, tiled=True)


def over_plane(stacked):
    return lax.all_to_all(
        stacked, ("dp", "ctx"), 0, 0, axis_index_groups=plane_groups, tiled=True
    )


def over_z(stacked):
    return lax.all_to_all(stacked, "ctx", 0, 0, axis_index_groups=z_groups, tiled=True)


def other_side(shard):
    return lax.ppermute(shard, "ctx", [(i, i ^ 1) for i in range(32)])


def product(left, right):
    return jnp.dot(left, right, preferred_element_type=f32)


def product_right_t(left, right):
    return lax.dot_general(left, right, (((1,), (1,)), ((), ())), preferred_element_type=f32)


def product_left_t(left, right):
    return lax.dot_general(left, right, (((0,), (0,)), ((), ())), preferred_element_type=f32)


def in_two(values):
    top = values.astype(bf16)
    return top, (values - top.astype(f32)).astype(bf16)


def inverse_rms(values):
    return lax.rsqrt(jnp.mean(values * values, axis=-1, keepdims=True) + epsilon)


def normed_taps(window, gain):
    values = window.astype(f32)
    normed = values * inverse_rms(values) * gain
    count = window.shape[0] - edge
    return [normed[edge - tap : edge - tap + count].astype(bf16) for tap in range(3)]


def call(kernel, outs, scratch=(), smem=0, inputs=0):
    return pl.pallas_call(
        kernel,
        out_shape=[jax.ShapeDtypeStruct(shape, kind) for shape, kind in outs],
        in_specs=[pl.BlockSpec(memory_space=pltpu.SMEM)] * smem
        + [pl.BlockSpec(memory_space=pltpu.VMEM)] * (inputs - smem),
        out_specs=[pl.BlockSpec(memory_space=pltpu.VMEM)] * len(outs),
        scratch_shapes=list(scratch),
        compiler_params=pltpu.CompilerParams(vmem_limit_bytes=50 * 1024 * 1024),
    )


def split_heads(pair, first):
    wide = pair.astype(f32)
    return jnp.concatenate(
        [jnp.where(first, wide, 0.0), jnp.where(first, 0.0, wide)], axis=0
    ).astype(bf16)


def join_heads(stacked, first):
    count = stacked.shape[0] // 2
    return jnp.where(first, stacked[:count], stacked[count:])


def rows_kernel(
    core_ref, links_ref, mine_ref, other_ref, window_ref, one_ref, two_ref, four_ref, eight_ref, upstream_ref, gain_ref, barred_ref,
    weights_ref, mixed_ref, attn_ref, d_query_ref, query_ref, upper_ref, key_ref, value_ref,
    taps_ref, own_stats_ref, stats_ref,
    lines_ref, keys_ref, values_ref,
):
    even = core_ref[0] == 0
    for chip in range(8):
        for matrix in range(8):
            mine, other = mine_ref[chip, matrix], other_ref[chip, matrix]
            weights_ref[matrix, chip * 64 : chip * 64 + 32] = jnp.where(even, mine, other)
            weights_ref[matrix, chip * 64 + 32 : chip * 64 + 64] = jnp.where(even, other, mine)
    gain = gain_ref[...]
    count = one_ref.shape[0]
    one = jnp.concatenate([two_ref[count:], one_ref[...]], axis=0)
    for slot, window in enumerate(
        (window_ref[...], one, two_ref[...], four_ref[...], eight_ref[...])
    ):
        for tap, part in enumerate(normed_taps(window, gain)):
            lines_ref[tap, slot * count : (slot + 1) * count] = part
    for tap in range(3):
        taps_ref[tap] = lines_ref[tap, :count]
    keys = product(lines_ref[0], weights_ref[0])
    keys = keys + product(lines_ref[1], weights_ref[1])
    keys_ref[...] = (keys + product(lines_ref[2], weights_ref[2])).astype(bf16)
    values_ref[...] = product(lines_ref[0], weights_ref[3]).astype(bf16)
    query = product(taps_ref[0], weights_ref[4])
    query = query + product(taps_ref[1], weights_ref[5])
    query_ref[...] = (query + product(taps_ref[2], weights_ref[6])).astype(bf16)
    upper_ref[...] = product_right_t(upstream_ref[...], weights_ref[7]).astype(bf16)
    key_ref[...] = keys_ref[:count]
    value_ref[...] = values_ref[:count]

    lane = lax.broadcasted_iota(jnp.int32, (count, 128), 1)
    row = lax.broadcasted_iota(jnp.int32, (count, 128), 0)
    first = lane < 64
    causal = jnp.where(lane <= row, 0.0, hidden)
    table = jnp.zeros((count, 128), f32)
    scaling = 64 ** (-0.5)
    for pair in range(4):
        span = slice(pair * 128, (pair + 1) * 128)
        query = split_heads(query_ref[:, span], first)
        upper = split_heads(upper_ref[:, span], first)
        key, value = keys_ref[:, span], values_ref[:, span]
        scores = product_right_t(query, key) * scaling
        d_prob = product_right_t(upper, value)
        probs_low, d_score = [], []
        for inner in range(2):
            head = pair * 2 + inner
            mine = scores[inner * count : (inner + 1) * count]
            parts = [mine[:, :count] + causal]
            for i in range(4):
                bias = jnp.where(links_ref[head, i] > 0, 0.0, hidden)
                parts.append(mine[:, (i + 1) * count : (i + 2) * count] + bias)
            mine = jnp.concatenate(parts, axis=1)
            highest = jnp.max(mine, axis=1, keepdims=True)
            weight = jnp.exp(mine - highest)
            inverse = 1.0 / jnp.sum(weight, axis=1, keepdims=True)
            probs = weight * inverse
            slope = d_prob[inner * count : (inner + 1) * count]
            centre = jnp.sum(probs * slope, axis=1, keepdims=True)
            probs_low.append(probs.astype(bf16))
            d_score.append((probs * (slope - centre) * scaling).astype(bf16))
            table = jnp.where(lane == head, highest, table)
            table = jnp.where(lane == 8 + head, inverse, table)
            table = jnp.where(lane == 16 + head, centre, table)
        attn = product(jnp.concatenate(probs_low, axis=0), value)
        attn_ref[:, span] = join_heads(attn, first).astype(bf16)
        d_query = product(jnp.concatenate(d_score, axis=0), key)
        d_query_ref[:, span] = join_heads(d_query, first).astype(bf16)
    across = jnp.transpose(table)
    own_stats_ref[...] = across[:24]
    for i in range(4):
        stats_ref[i, :8] = jnp.maximum(across[:8], barred_ref[i])
        stats_ref[i, 8:] = across[8:24]
    mixed = window_ref[edge:].astype(f32) + product(attn_ref[...], weights_ref[7])
    mixed_ref[...] = mixed.astype(bf16)


def later_kernel(
    own_ref, one_ref, two_ref, four_ref, eight_ref, gain_ref, weights_ref,
    queries_ref, uppers_ref,
    lines_ref, cots_ref,
):
    gain = gain_ref[...]
    count = own_ref.shape[0]
    one = jnp.concatenate([own_ref[count - edge :], one_ref[:count]], axis=0)
    size = count + edge
    windows = (one, two_ref[:size], four_ref[:size], eight_ref[:size])
    cots = (one_ref[count:], two_ref[size:], four_ref[size:], eight_ref[size:])
    for slot in range(4):
        rows = slice(slot * count, (slot + 1) * count)
        cots_ref[rows] = cots[slot]
        for tap, part in enumerate(normed_taps(windows[slot], gain)):
            lines_ref[tap, rows] = part
    queries = product(lines_ref[0], weights_ref[4])
    queries = queries + product(lines_ref[1], weights_ref[5])
    queries_ref[...] = (queries + product(lines_ref[2], weights_ref[6])).astype(bf16)
    uppers_ref[...] = product_right_t(cots_ref[...], weights_ref[7]).astype(bf16)


def store_partials(even, term, keep_ref, send_ref, matrix):
    term = term.astype(bf16)
    for chip in range(8):
        low = term[chip * 64 : chip * 64 + 32]
        high = term[chip * 64 + 32 : chip * 64 + 64]
        keep_ref[chip, matrix] = jnp.where(even, low, high)
        send_ref[chip, matrix] = jnp.where(even, high, low)


def partials_kernel(core_ref, taps_ref, d_query_ref, attn_ref, upstream_ref, keep_ref, send_ref):
    even = core_ref[0] == 0
    for tap in range(3):
        term = product_left_t(taps_ref[tap], d_query_ref[...])
        store_partials(even, term, keep_ref, send_ref, tap)
    term = product_left_t(attn_ref[...], upstream_ref[...])
    store_partials(even, term, keep_ref, send_ref, 3)


def columns_kernel(
    core_ref, key_ref, value_ref, query_ref, upper_ref, queries_ref, uppers_ref, taps_ref,
    own_ref, one_ref, two_ref, four_ref, eight_ref,
    d_key_ref, d_value_ref, keep_ref, send_ref,
):
    even = core_ref[0] == 0
    count = key_ref.shape[0]
    lane = lax.broadcasted_iota(jnp.int32, (count, 128), 1)
    row = lax.broadcasted_iota(jnp.int32, (count, 128), 0)
    first = lane < 64
    causal = jnp.concatenate([row <= lane] * 2, axis=1)
    scaling = 64 ** (-0.5)
    all_stats = [own_ref[...], one_ref[...], two_ref[...], four_ref[...], eight_ref[...]]
    all_stats = [
        (jnp.where(stats[8:16] > 0.0, stats[:8], 1e30), stats[8:16], stats[16:24])
        for stats in all_stats
    ]
    for pair in range(4):
        span = slice(pair * 128, (pair + 1) * 128)
        key, value = key_ref[:, span], value_ref[:, span]
        d_key = jnp.zeros((count, 128), f32)
        d_value = jnp.zeros((count, 128), f32)
        for slot in range(5):
            if slot == 0:
                query, upper = query_ref[:, span], upper_ref[:, span]
            else:
                rows = slice((slot - 1) * count, slot * count)
                query, upper = queries_ref[rows, span], uppers_ref[rows, span]
            query, upper = split_heads(query, first), split_heads(upper, first)
            highest, inverse, centre = [
                jnp.concatenate([part[pair * 2 : pair * 2 + 1], part[pair * 2 + 1 : pair * 2 + 2]], axis=1)
                for part in all_stats[slot]
            ]
            scores = product_right_t(key, query) * scaling
            probs = jnp.exp(scores - highest) * inverse
            if slot == 0:
                probs = jnp.where(causal, probs, 0.0)
            d_prob = product_right_t(value, upper)
            d_score = (probs * (d_prob - centre) * scaling).astype(bf16)
            d_key = d_key + product(d_score, query)
            d_value = d_value + product(probs.astype(bf16), upper)
        d_key_ref[:, span] = d_key.astype(bf16)
        d_value_ref[:, span] = d_value.astype(bf16)
    for tap in range(3):
        term = product_left_t(taps_ref[tap], d_key_ref[...])
        store_partials(even, term, keep_ref, send_ref, tap)
    store_partials(even, product_left_t(taps_ref[0], d_value_ref[...]), keep_ref, send_ref, 3)


def series_kernel(
    d_query_ref, d_key_ref, d_value_ref, leading_ref, weights_ref, own_ref, upstream_ref, gain_ref,
    grad_ref, d_gain_ref,
):
    count, features = own_ref.shape
    d_normed = product_right_t(d_value_ref[...], weights_ref[3])
    for which, (ref, base) in enumerate(((d_query_ref, 4), (d_key_ref, 0))):
        after = leading_ref[:, which * features : (which + 1) * features]
        window = jnp.concatenate([ref[...], after], axis=0).astype(f32)
        for tap in range(3):
            part = window[tap : tap + count].astype(bf16)
            d_normed = d_normed + product_right_t(part, weights_ref[base + tap])
    values = own_ref[...].astype(f32)
    scale = inverse_rms(values)
    top, rest = in_two(jnp.sum(d_normed * values * scale, axis=0, keepdims=True))
    blank = jnp.zeros((d_gain_ref.shape[0] - 2, features), f32)
    d_gain_ref[...] = jnp.concatenate(
        [top.astype(f32), rest.astype(f32), blank], axis=0
    ).astype(bf16)
    slope = d_normed * gain_ref[...]
    along = jnp.mean(slope * values, axis=-1, keepdims=True)
    d_values = scale * slope - values * (scale * scale * scale * along)
    grad_ref[...] = (upstream_ref[...].astype(f32) + d_values).astype(bf16)


def halve(keep, send):
    return (keep.astype(f32) + other_core(send).astype(f32)).astype(bf16)


def body(
    series, norm_gain, query_kernel, key_kernel, value_weight, out_weight, block_links, grad_out
):
    core = (lax.axis_index("dp") % 2).reshape(1)
    block = lax.axis_index("ctx")
    heads = block_links.shape[2]
    own, cotangent = series[0], grad_out[0]
    count, features = own.shape
    gain = norm_gain.reshape(1, features)

    shard = jnp.concatenate(
        [key_kernel, value_weight[None], query_kernel, out_weight[None]], axis=0
    )
    mine = over_chips(jnp.broadcast_to(shard[None], (8,) + shard.shape))
    before_one = shift_ctx(own, 1)
    after_one = shift_ctx(jnp.concatenate([own, cotangent], axis=0), -1)
    before_one, after_one = lax.optimization_barrier((before_one, after_one))
    window = jnp.concatenate([before_one[count - edge :], own], axis=0)
    carried = jnp.concatenate([window, cotangent], axis=0)
    before_two, before_four = shift_ctx(window, 2), shift_ctx(window, 4)
    after_two, after_four = shift_ctx(carried, -2), shift_ctx(carried, -4)
    mine, before_two, before_four, after_two, after_four = lax.optimization_barrier(
        (mine, before_two, before_four, after_two, after_four)
    )
    other = other_core(mine)
    other, before_eight, after_eight = lax.optimization_barrier(
        (other, shift_ctx(before_four, 4), shift_ctx(after_four, -4))
    )
    before = (before_two, before_four, before_eight)
    after = (after_one, after_two, after_four, after_eight)

    offsets = jnp.array(block_offsets, dtype=jnp.int32)
    reach = (block_links[0, 0] > 0) & (block >= offsets)[None, :]
    barred = jnp.where(reach.T[:, :, None], -3e38, 1e30).astype(f32)
    barred = jnp.broadcast_to(barred, (4, heads, 128))

    half = ((count, features), bf16)
    (
        weights, mixed, attn, d_query, query, upper, key, value, taps, own_stats, stats
    ) = call(
        rows_kernel,
        [((8, features, features), bf16)] + [half] * 7
        + [((3, count, features), bf16), ((24, count), f32), ((4, 24, count), f32)],
        [
            pltpu.VMEM((3, 5 * count, features), bf16),
            pltpu.VMEM((5 * count, features), bf16),
            pltpu.VMEM((5 * count, features), bf16),
        ],
        smem=2,
        inputs=12,
    )(
        core, reach.astype(jnp.int32), mine, other, window, before_one, *before, cotangent, gain,
        barred,
    )
    returned = [shift_ctx(stats[i], -block_offsets[i]) for i in range(4)]
    parts = ((8, 4, 32, features), bf16)
    keep, send = call(partials_kernel, [parts, parts], smem=1, inputs=5)(
        core, taps, d_query, attn, cotangent
    )
    queries, uppers = call(
        later_kernel,
        [((4 * count, features), bf16)] * 2,
        [pltpu.VMEM((3, 4 * count, features), bf16), pltpu.VMEM((4 * count, features), bf16)],
        inputs=7,
    )(own, *after, gain, weights)
    query_half = halve(keep, send)
    d_key, d_value, keep, send = call(
        columns_kernel, [half, half, parts, parts], smem=1, inputs=13
    )(core, key, value, query, upper, queries, uppers, taps, own_stats, *returned)
    leading = shift_ctx(jnp.concatenate([d_query[:edge], d_key[:edge]], axis=1), -1)
    key_half = halve(keep, send)
    grad_series, d_gain = call(
        series_kernel, [half, ((edge, features), bf16)], inputs=8
    )(d_query, d_key, d_value, leading, weights, own, cotangent, gain)
    terms = jnp.stack([query_half, key_half], axis=1).reshape(16, 128, features)
    d_gain = jnp.broadcast_to(d_gain[None], (16, edge, features))
    arrived = over_plane(jnp.concatenate([terms, d_gain], axis=1))
    arrived = jnp.sum(arrived.astype(f32), axis=0)
    rows = arrived[:128].astype(bf16).reshape(16, 8, features)
    top, rest = in_two(jnp.sum(arrived[128:], axis=0).reshape(4, 128))
    extra = jnp.broadcast_to(jnp.concatenate([top, rest], axis=0)[None], (16, 8, 128))
    arrived = over_z(jnp.concatenate([rows, extra], axis=2)).astype(f32)
    summed = jnp.sum(arrived, axis=0)
    core_gain = summed[:4, features:] + summed[4:, features:]
    gain_total = (core_gain + other_core(core_gain)).reshape(features)
    summed = summed[:, :features].astype(bf16)
    mine = over_z(jnp.broadcast_to(summed[None], (16, 8, features)))
    other = other_side(mine)
    first = block % 2 == 0
    for_query = jnp.where(first, mine, other).reshape(4, 32, features).astype(f32)
    for_key = jnp.where(first, other, mine).reshape(4, 32, features).astype(f32)
    return (
        mixed[None],
        grad_series[None],
        gain_total,
        for_query[:3],
        for_key[:3],
        for_key[3],
        for_query[3],
    )


def solution(mesh):
    placed = (
        P("dp", "ctx", None),
        P(),
        P(None, "dp", None),
        P(None, "dp", None),
        P("dp", None),
        P("dp", None),
        P("dp", "ctx", None, None),
        P("dp", "ctx", None),
    )
    return jax.shard_map(
        body,
        mesh=mesh,
        in_specs=placed,
        out_specs=(
            P("dp", "ctx", None),
            P("dp", "ctx", None),
            P(),
            P(None, "dp", None),
            P(None, "dp", None),
            P("dp", None),
            P("dp", None),
        ),
        check_vma=False,
    )
```

```python
import jax
import jax.numpy as jnp
from jax import lax
from jax.experimental import pallas as pl
from jax.experimental.pallas import tpu as pltpu
from jax.sharding import PartitionSpec as P

block_offsets = (1, 2, 4, 8)
epsilon = 1e-06
hidden = -1e30
f32 = jnp.float32
bf16 = jnp.bfloat16
edge = 16
plane_groups = [
    [(2 * chip + core) * 32 + 2 * z + side for chip in range(8) for side in range(2)]
    for core in range(2)
    for z in range(16)
]
chip_groups = [[2 * chip + core for chip in range(8)] for core in range(2)]
z_groups = [[2 * z + side for z in range(16)] for side in range(2)]


def shift_ctx(shard, by):
    devices = lax.axis_size("ctx")
    pairs = [(i, i + by) for i in range(devices) if 0 <= i + by < devices]
    return lax.ppermute(shard, "ctx", pairs)


def dp_to(shard, dx, dy, dc):
    def target(i):
        x, y, c = i // 8, (i // 2) % 4, i % 2
        return ((x + dx) % 2) * 8 + ((y + dy) % 4) * 2 + (c + dc) % 2

    return lax.ppermute(shard, "dp", [(i, target(i)) for i in range(16)])


def other_core(shard):
    return dp_to(shard, 0, 0, 1)


def over_chips(stacked):
    return lax.all_to_all(stacked, "dp", 0, 0, axis_index_groups=chip_groups, tiled=True)


def over_plane(stacked):
    return lax.all_to_all(
        stacked, ("dp", "ctx"), 0, 0, axis_index_groups=plane_groups, tiled=True
    )


def over_z(stacked):
    return lax.all_to_all(stacked, "ctx", 0, 0, axis_index_groups=z_groups, tiled=True)


def other_side(shard):
    return lax.ppermute(shard, "ctx", [(i, i ^ 1) for i in range(32)])


def product(left, right):
    return jnp.dot(left, right, preferred_element_type=f32)


def product_right_t(left, right):
    return lax.dot_general(left, right, (((1,), (1,)), ((), ())), preferred_element_type=f32)


def product_left_t(left, right):
    return lax.dot_general(left, right, (((0,), (0,)), ((), ())), preferred_element_type=f32)


def in_two(values):
    top = values.astype(bf16)
    return top, (values - top.astype(f32)).astype(bf16)


def inverse_rms(values):
    return lax.rsqrt(jnp.mean(values * values, axis=-1, keepdims=True) + epsilon)


def normed_taps(window, gain):
    values = window.astype(f32)
    normed = values * inverse_rms(values) * gain
    count = window.shape[0] - edge
    return [normed[edge - tap : edge - tap + count].astype(bf16) for tap in range(3)]


def call(kernel, outs, scratch=(), smem=0, inputs=0):
    return pl.pallas_call(
        kernel,
        out_shape=[jax.ShapeDtypeStruct(shape, kind) for shape, kind in outs],
        in_specs=[pl.BlockSpec(memory_space=pltpu.SMEM)] * smem
        + [pl.BlockSpec(memory_space=pltpu.VMEM)] * (inputs - smem),
        out_specs=[pl.BlockSpec(memory_space=pltpu.VMEM)] * len(outs),
        scratch_shapes=list(scratch),
        compiler_params=pltpu.CompilerParams(vmem_limit_bytes=50 * 1024 * 1024),
    )


def split_heads(pair, first):
    wide = pair.astype(f32)
    return jnp.concatenate(
        [jnp.where(first, wide, 0.0), jnp.where(first, 0.0, wide)], axis=0
    ).astype(bf16)


def join_heads(stacked, first):
    count = stacked.shape[0] // 2
    return jnp.where(first, stacked[:count], stacked[count:])


def rows_kernel(
    core_ref, links_ref, mine_ref, other_ref, window_ref, one_ref, two_ref, four_ref, eight_ref, upstream_ref, gain_ref, barred_ref,
    weights_ref, mixed_ref, attn_ref, d_query_ref, query_ref, upper_ref, key_ref, value_ref,
    taps_ref, own_stats_ref, stats_ref,
    lines_ref, keys_ref, values_ref,
):
    even = core_ref[0] == 0
    for chip in range(8):
        for matrix in range(8):
            mine, other = mine_ref[chip, matrix], other_ref[chip, matrix]
            weights_ref[matrix, chip * 64 : chip * 64 + 32] = jnp.where(even, mine, other)
            weights_ref[matrix, chip * 64 + 32 : chip * 64 + 64] = jnp.where(even, other, mine)
    gain = gain_ref[...]
    count = one_ref.shape[0]
    one = jnp.concatenate([two_ref[count:], one_ref[...]], axis=0)
    for slot, window in enumerate(
        (window_ref[...], one, two_ref[...], four_ref[...], eight_ref[...])
    ):
        for tap, part in enumerate(normed_taps(window, gain)):
            lines_ref[tap, slot * count : (slot + 1) * count] = part
    for tap in range(3):
        taps_ref[tap] = lines_ref[tap, :count]
    keys = product(lines_ref[0], weights_ref[0])
    keys = keys + product(lines_ref[1], weights_ref[1])
    keys_ref[...] = (keys + product(lines_ref[2], weights_ref[2])).astype(bf16)
    values_ref[...] = product(lines_ref[0], weights_ref[3]).astype(bf16)
    query = product(taps_ref[0], weights_ref[4])
    query = query + product(taps_ref[1], weights_ref[5])
    query_ref[...] = (query + product(taps_ref[2], weights_ref[6])).astype(bf16)
    upper_ref[...] = product_right_t(upstream_ref[...], weights_ref[7]).astype(bf16)
    key_ref[...] = keys_ref[:count]
    value_ref[...] = values_ref[:count]

    lane = lax.broadcasted_iota(jnp.int32, (count, 128), 1)
    row = lax.broadcasted_iota(jnp.int32, (count, 128), 0)
    first = lane < 64
    causal = jnp.where(lane <= row, 0.0, hidden)
    table = jnp.zeros((count, 128), f32)
    scaling = 64 ** (-0.5)
    for pair in range(4):
        span = slice(pair * 128, (pair + 1) * 128)
        query = split_heads(query_ref[:, span], first)
        upper = split_heads(upper_ref[:, span], first)
        key, value = keys_ref[:, span], values_ref[:, span]
        scores = product_right_t(query, key) * scaling
        d_prob = product_right_t(upper, value)
        probs_low, d_score = [], []
        for inner in range(2):
            head = pair * 2 + inner
            mine = scores[inner * count : (inner + 1) * count]
            parts = [mine[:, :count] + causal]
            for i in range(4):
                bias = jnp.where(links_ref[head, i] > 0, 0.0, hidden)
                parts.append(mine[:, (i + 1) * count : (i + 2) * count] + bias)
            mine = jnp.concatenate(parts, axis=1)
            highest = jnp.max(mine, axis=1, keepdims=True)
            weight = jnp.exp(mine - highest)
            inverse = 1.0 / jnp.sum(weight, axis=1, keepdims=True)
            probs = weight * inverse
            slope = d_prob[inner * count : (inner + 1) * count]
            centre = jnp.sum(probs * slope, axis=1, keepdims=True)
            probs_low.append(probs.astype(bf16))
            d_score.append((probs * (slope - centre) * scaling).astype(bf16))
            table = jnp.where(lane == head, highest, table)
            table = jnp.where(lane == 8 + head, inverse, table)
            table = jnp.where(lane == 16 + head, centre, table)
        attn = product(jnp.concatenate(probs_low, axis=0), value)
        attn_ref[:, span] = join_heads(attn, first).astype(bf16)
        d_query = product(jnp.concatenate(d_score, axis=0), key)
        d_query_ref[:, span] = join_heads(d_query, first).astype(bf16)
    across = jnp.transpose(table)
    own_stats_ref[...] = across[:24]
    for i in range(4):
        stats_ref[i, :8] = jnp.maximum(across[:8], barred_ref[i])
        stats_ref[i, 8:] = across[8:24]
    mixed = window_ref[edge:].astype(f32) + product(attn_ref[...], weights_ref[7])
    mixed_ref[...] = mixed.astype(bf16)


def later_kernel(
    own_ref, one_ref, two_ref, four_ref, eight_ref, gain_ref, weights_ref,
    queries_ref, uppers_ref,
    lines_ref, cots_ref,
):
    gain = gain_ref[...]
    count = own_ref.shape[0]
    one = jnp.concatenate([own_ref[count - edge :], one_ref[:count]], axis=0)
    size = count + edge
    windows = (one, two_ref[:size], four_ref[:size], eight_ref[:size])
    cots = (one_ref[count:], two_ref[size:], four_ref[size:], eight_ref[size:])
    for slot in range(4):
        rows = slice(slot * count, (slot + 1) * count)
        cots_ref[rows] = cots[slot]
        for tap, part in enumerate(normed_taps(windows[slot], gain)):
            lines_ref[tap, rows] = part
    queries = product(lines_ref[0], weights_ref[4])
    queries = queries + product(lines_ref[1], weights_ref[5])
    queries_ref[...] = (queries + product(lines_ref[2], weights_ref[6])).astype(bf16)
    uppers_ref[...] = product_right_t(cots_ref[...], weights_ref[7]).astype(bf16)


def store_partials(even, term, keep_ref, send_ref, matrix):
    term = term.astype(bf16)
    for chip in range(8):
        low = term[chip * 64 : chip * 64 + 32]
        high = term[chip * 64 + 32 : chip * 64 + 64]
        keep_ref[chip, matrix] = jnp.where(even, low, high)
        send_ref[chip, matrix] = jnp.where(even, high, low)


def partials_kernel(core_ref, taps_ref, d_query_ref, attn_ref, upstream_ref, keep_ref, send_ref):
    even = core_ref[0] == 0
    for tap in range(3):
        term = product_left_t(taps_ref[tap], d_query_ref[...])
        store_partials(even, term, keep_ref, send_ref, tap)
    term = product_left_t(attn_ref[...], upstream_ref[...])
    store_partials(even, term, keep_ref, send_ref, 3)


def columns_kernel(
    core_ref, key_ref, value_ref, query_ref, upper_ref, queries_ref, uppers_ref, taps_ref,
    own_ref, one_ref, two_ref, four_ref, eight_ref,
    d_key_ref, d_value_ref, keep_ref, send_ref,
):
    even = core_ref[0] == 0
    count = key_ref.shape[0]
    lane = lax.broadcasted_iota(jnp.int32, (count, 128), 1)
    row = lax.broadcasted_iota(jnp.int32, (count, 128), 0)
    first = lane < 64
    causal = jnp.concatenate([row <= lane] * 2, axis=1)
    scaling = 64 ** (-0.5)
    all_stats = [own_ref[...], one_ref[...], two_ref[...], four_ref[...], eight_ref[...]]
    all_stats = [
        (jnp.where(stats[8:16] > 0.0, stats[:8], 1e30), stats[8:16], stats[16:24])
        for stats in all_stats
    ]
    for pair in range(4):
        span = slice(pair * 128, (pair + 1) * 128)
        key, value = key_ref[:, span], value_ref[:, span]
        d_key = jnp.zeros((count, 128), f32)
        d_value = jnp.zeros((count, 128), f32)
        for slot in range(5):
            if slot == 0:
                query, upper = query_ref[:, span], upper_ref[:, span]
            else:
                rows = slice((slot - 1) * count, slot * count)
                query, upper = queries_ref[rows, span], uppers_ref[rows, span]
            query, upper = split_heads(query, first), split_heads(upper, first)
            highest, inverse, centre = [
                jnp.concatenate([part[pair * 2 : pair * 2 + 1], part[pair * 2 + 1 : pair * 2 + 2]], axis=1)
                for part in all_stats[slot]
            ]
            scores = product_right_t(key, query) * scaling
            probs = jnp.exp(scores - highest) * inverse
            if slot == 0:
                probs = jnp.where(causal, probs, 0.0)
            d_prob = product_right_t(value, upper)
            d_score = (probs * (d_prob - centre) * scaling).astype(bf16)
            d_key = d_key + product(d_score, query)
            d_value = d_value + product(probs.astype(bf16), upper)
        d_key_ref[:, span] = d_key.astype(bf16)
        d_value_ref[:, span] = d_value.astype(bf16)
    for tap in range(3):
        term = product_left_t(taps_ref[tap], d_key_ref[...])
        store_partials(even, term, keep_ref, send_ref, tap)
    store_partials(even, product_left_t(taps_ref[0], d_value_ref[...]), keep_ref, send_ref, 3)


def series_kernel(
    d_query_ref, d_key_ref, d_value_ref, leading_ref, weights_ref, own_ref, upstream_ref, gain_ref,
    grad_ref, d_gain_ref,
):
    count, features = own_ref.shape
    d_normed = product_right_t(d_value_ref[...], weights_ref[3])
    for which, (ref, base) in enumerate(((d_query_ref, 4), (d_key_ref, 0))):
        after = leading_ref[:, which * features : (which + 1) * features]
        window = jnp.concatenate([ref[...], after], axis=0).astype(f32)
        for tap in range(3):
            part = window[tap : tap + count].astype(bf16)
            d_normed = d_normed + product_right_t(part, weights_ref[base + tap])
    values = own_ref[...].astype(f32)
    scale = inverse_rms(values)
    top, rest = in_two(jnp.sum(d_normed * values * scale, axis=0, keepdims=True))
    blank = jnp.zeros((d_gain_ref.shape[0] - 2, features), f32)
    d_gain_ref[...] = jnp.concatenate(
        [top.astype(f32), rest.astype(f32), blank], axis=0
    ).astype(bf16)
    slope = d_normed * gain_ref[...]
    along = jnp.mean(slope * values, axis=-1, keepdims=True)
    d_values = scale * slope - values * (scale * scale * scale * along)
    grad_ref[...] = (upstream_ref[...].astype(f32) + d_values).astype(bf16)


def halve(keep, send):
    return (keep.astype(f32) + other_core(send).astype(f32)).astype(bf16)


def body(
    series, norm_gain, query_kernel, key_kernel, value_weight, out_weight, block_links, grad_out
):
    core = (lax.axis_index("dp") % 2).reshape(1)
    block = lax.axis_index("ctx")
    heads = block_links.shape[2]
    own, cotangent = series[0], grad_out[0]
    count, features = own.shape
    gain = norm_gain.reshape(1, features)

    shard = jnp.concatenate(
        [key_kernel, value_weight[None], query_kernel, out_weight[None]], axis=0
    )
    before_one = shift_ctx(own, 1)
    after_one = shift_ctx(jnp.concatenate([own, cotangent], axis=0), -1)
    shard, before_one, after_one = lax.optimization_barrier((shard, before_one, after_one))
    window = jnp.concatenate([before_one[count - edge :], own], axis=0)
    carried = jnp.concatenate([window, cotangent], axis=0)
    after_eight, after_four, after_two = [shift_ctx(carried, -by) for by in (8, 4, 2)]
    before_four, before_two = shift_ctx(window, 4), shift_ctx(window, 2)
    mine = over_chips(jnp.broadcast_to(shard[None], (8,) + shard.shape))
    mine, before_two, before_four, after_two, after_four, after_eight = lax.optimization_barrier(
        (mine, before_two, before_four, after_two, after_four, after_eight)
    )
    other, before_eight = lax.optimization_barrier((other_core(mine), shift_ctx(before_four, 4)))
    before = (before_two, before_four, before_eight)
    after = (after_one, after_two, after_four, after_eight)

    offsets = jnp.array(block_offsets, dtype=jnp.int32)
    reach = (block_links[0, 0] > 0) & (block >= offsets)[None, :]
    barred = jnp.where(reach.T[:, :, None], -3e38, 1e30).astype(f32)
    barred = jnp.broadcast_to(barred, (4, heads, 128))

    half = ((count, features), bf16)
    (
        weights, mixed, attn, d_query, query, upper, key, value, taps, own_stats, stats
    ) = call(
        rows_kernel,
        [((8, features, features), bf16)] + [half] * 7
        + [((3, count, features), bf16), ((24, count), f32), ((4, 24, count), f32)],
        [
            pltpu.VMEM((3, 5 * count, features), bf16),
            pltpu.VMEM((5 * count, features), bf16),
            pltpu.VMEM((5 * count, features), bf16),
        ],
        smem=2,
        inputs=12,
    )(
        core, reach.astype(jnp.int32), mine, other, window, before_one, *before, cotangent, gain,
        barred,
    )
    returned = [shift_ctx(stats[i], -block_offsets[i]) for i in range(4)]
    parts = ((8, 4, 32, features), bf16)
    keep, send = call(partials_kernel, [parts, parts], smem=1, inputs=5)(
        core, taps, d_query, attn, cotangent
    )
    queries, uppers = call(
        later_kernel,
        [((4 * count, features), bf16)] * 2,
        [pltpu.VMEM((3, 4 * count, features), bf16), pltpu.VMEM((4 * count, features), bf16)],
        inputs=7,
    )(own, *after, gain, weights)
    query_half = halve(keep, send)
    d_key, d_value, keep, send = call(
        columns_kernel, [half, half, parts, parts], smem=1, inputs=13
    )(core, key, value, query, upper, queries, uppers, taps, own_stats, *returned)
    leading = shift_ctx(jnp.concatenate([d_query[:edge], d_key[:edge]], axis=1), -1)
    key_half = halve(keep, send)
    grad_series, d_gain = call(
        series_kernel, [half, ((edge, features), bf16)], inputs=8
    )(d_query, d_key, d_value, leading, weights, own, cotangent, gain)
    terms = jnp.stack([query_half, key_half], axis=1).reshape(16, 128, features)
    d_gain = jnp.broadcast_to(d_gain[None], (16, edge, features))
    arrived = over_plane(jnp.concatenate([terms, d_gain], axis=1))
    arrived = jnp.sum(arrived.astype(f32), axis=0)
    rows = arrived[:128].astype(bf16).reshape(16, 8, features)
    top, rest = in_two(jnp.sum(arrived[128:], axis=0).reshape(4, 128))
    extra = jnp.broadcast_to(jnp.concatenate([top, rest], axis=0)[None], (16, 8, 128))
    arrived = over_z(jnp.concatenate([rows, extra], axis=2)).astype(f32)
    summed = jnp.sum(arrived, axis=0)
    core_gain = summed[:4, features:] + summed[4:, features:]
    gain_total = (core_gain + other_core(core_gain)).reshape(features)
    summed = summed[:, :features].astype(bf16)
    mine = over_z(jnp.broadcast_to(summed[None], (16, 8, features)))
    other = other_side(mine)
    first = block % 2 == 0
    for_query = jnp.where(first, mine, other).reshape(4, 32, features).astype(f32)
    for_key = jnp.where(first, other, mine).reshape(4, 32, features).astype(f32)
    return (
        mixed[None],
        grad_series[None],
        gain_total,
        for_query[:3],
        for_key[:3],
        for_key[3],
        for_query[3],
    )


def solution(mesh):
    placed = (
        P("dp", "ctx", None),
        P(),
        P(None, "dp", None),
        P(None, "dp", None),
        P("dp", None),
        P("dp", None),
        P("dp", "ctx", None, None),
        P("dp", "ctx", None),
    )
    return jax.shard_map(
        body,
        mesh=mesh,
        in_specs=placed,
        out_specs=(
            P("dp", "ctx", None),
            P("dp", "ctx", None),
            P(),
            P(None, "dp", None),
            P(None, "dp", None),
            P("dp", None),
            P("dp", None),
        ),
        check_vma=False,
    )
```

```python
import jax
import jax.numpy as jnp
from jax import lax
from jax.experimental import pallas as pl
from jax.experimental.pallas import tpu as pltpu
from jax.sharding import PartitionSpec as P

block_offsets = (1, 2, 4, 8)
epsilon = 1e-06
hidden = -1e30
f32 = jnp.float32
bf16 = jnp.bfloat16
edge = 16
plane_groups = [
    [(2 * chip + core) * 32 + 2 * z + side for chip in range(8) for side in range(2)]
    for core in range(2)
    for z in range(16)
]
chip_groups = [[2 * chip + core for chip in range(8)] for core in range(2)]
z_groups = [[2 * z + side for z in range(16)] for side in range(2)]


def shift_ctx(shard, by):
    devices = lax.axis_size("ctx")
    pairs = [(i, i + by) for i in range(devices) if 0 <= i + by < devices]
    return lax.ppermute(shard, "ctx", pairs)


def dp_to(shard, dx, dy, dc):
    def target(i):
        x, y, c = i // 8, (i // 2) % 4, i % 2
        return ((x + dx) % 2) * 8 + ((y + dy) % 4) * 2 + (c + dc) % 2

    return lax.ppermute(shard, "dp", [(i, target(i)) for i in range(16)])


def other_core(shard):
    return dp_to(shard, 0, 0, 1)


def over_chips(stacked):
    return lax.all_to_all(stacked, "dp", 0, 0, axis_index_groups=chip_groups, tiled=True)


def over_plane(stacked):
    return lax.all_to_all(
        stacked, ("dp", "ctx"), 0, 0, axis_index_groups=plane_groups, tiled=True
    )


def over_z(stacked):
    return lax.all_to_all(stacked, "ctx", 0, 0, axis_index_groups=z_groups, tiled=True)


def other_side(shard):
    return lax.ppermute(shard, "ctx", [(i, i ^ 1) for i in range(32)])


def product(left, right):
    return jnp.dot(left, right, preferred_element_type=f32)


def product_right_t(left, right):
    return lax.dot_general(left, right, (((1,), (1,)), ((), ())), preferred_element_type=f32)


def product_left_t(left, right):
    return lax.dot_general(left, right, (((0,), (0,)), ((), ())), preferred_element_type=f32)


def in_two(values):
    top = values.astype(bf16)
    return top, (values - top.astype(f32)).astype(bf16)


def inverse_rms(values):
    return lax.rsqrt(jnp.mean(values * values, axis=-1, keepdims=True) + epsilon)


def normed_taps(window, gain):
    values = window.astype(f32)
    normed = values * inverse_rms(values) * gain
    count = window.shape[0] - edge
    return [normed[edge - tap : edge - tap + count].astype(bf16) for tap in range(3)]


def call(kernel, outs, scratch=(), smem=0, inputs=0):
    return pl.pallas_call(
        kernel,
        out_shape=[jax.ShapeDtypeStruct(shape, kind) for shape, kind in outs],
        in_specs=[pl.BlockSpec(memory_space=pltpu.SMEM)] * smem
        + [pl.BlockSpec(memory_space=pltpu.VMEM)] * (inputs - smem),
        out_specs=[pl.BlockSpec(memory_space=pltpu.VMEM)] * len(outs),
        scratch_shapes=list(scratch),
        compiler_params=pltpu.CompilerParams(vmem_limit_bytes=50 * 1024 * 1024),
    )


def split_heads(pair, first):
    wide = pair.astype(f32)
    return jnp.concatenate(
        [jnp.where(first, wide, 0.0), jnp.where(first, 0.0, wide)], axis=0
    ).astype(bf16)


def join_heads(stacked, first):
    count = stacked.shape[0] // 2
    return jnp.where(first, stacked[:count], stacked[count:])


def rows_kernel(
    core_ref, links_ref, mine_ref, other_ref, window_ref, one_ref, two_ref, four_ref, eight_ref, upstream_ref, gain_ref, barred_ref,
    weights_ref, mixed_ref, attn_ref, d_query_ref, query_ref, upper_ref, key_ref, value_ref,
    taps_ref, own_stats_ref, stats_ref,
    lines_ref, keys_ref, values_ref,
):
    even = core_ref[0] == 0
    for chip in range(8):
        for matrix in range(8):
            mine, other = mine_ref[chip, matrix], other_ref[chip, matrix]
            weights_ref[matrix, chip * 64 : chip * 64 + 32] = jnp.where(even, mine, other)
            weights_ref[matrix, chip * 64 + 32 : chip * 64 + 64] = jnp.where(even, other, mine)
    gain = gain_ref[...]
    count = one_ref.shape[0]
    one = jnp.concatenate([two_ref[count:], one_ref[...]], axis=0)
    for slot, window in enumerate(
        (window_ref[...], one, two_ref[...], four_ref[...], eight_ref[...])
    ):
        for tap, part in enumerate(normed_taps(window, gain)):
            lines_ref[tap, slot * count : (slot + 1) * count] = part
    for tap in range(3):
        taps_ref[tap] = lines_ref[tap, :count]
    keys = product(lines_ref[0], weights_ref[0])
    keys = keys + product(lines_ref[1], weights_ref[1])
    keys_ref[...] = (keys + product(lines_ref[2], weights_ref[2])).astype(bf16)
    values_ref[...] = product(lines_ref[0], weights_ref[3]).astype(bf16)
    query = product(taps_ref[0], weights_ref[4])
    query = query + product(taps_ref[1], weights_ref[5])
    query_ref[...] = (query + product(taps_ref[2], weights_ref[6])).astype(bf16)
    upper_ref[...] = product_right_t(upstream_ref[...], weights_ref[7]).astype(bf16)
    key_ref[...] = keys_ref[:count]
    value_ref[...] = values_ref[:count]

    lane = lax.broadcasted_iota(jnp.int32, (count, 128), 1)
    row = lax.broadcasted_iota(jnp.int32, (count, 128), 0)
    first = lane < 64
    causal = jnp.where(lane <= row, 0.0, hidden)
    table = jnp.zeros((count, 128), f32)
    scaling = 64 ** (-0.5)
    for pair in range(4):
        span = slice(pair * 128, (pair + 1) * 128)
        query = split_heads(query_ref[:, span], first)
        upper = split_heads(upper_ref[:, span], first)
        key, value = keys_ref[:, span], values_ref[:, span]
        scores = product_right_t(query, key) * scaling
        d_prob = product_right_t(upper, value)
        probs_low, d_score = [], []
        for inner in range(2):
            head = pair * 2 + inner
            mine = scores[inner * count : (inner + 1) * count]
            parts = [mine[:, :count] + causal]
            for i in range(4):
                bias = jnp.where(links_ref[head, i] > 0, 0.0, hidden)
                parts.append(mine[:, (i + 1) * count : (i + 2) * count] + bias)
            mine = jnp.concatenate(parts, axis=1)
            highest = jnp.max(mine, axis=1, keepdims=True)
            weight = jnp.exp(mine - highest)
            inverse = 1.0 / jnp.sum(weight, axis=1, keepdims=True)
            probs = weight * inverse
            slope = d_prob[inner * count : (inner + 1) * count]
            centre = jnp.sum(probs * slope, axis=1, keepdims=True)
            probs_low.append(probs.astype(bf16))
            d_score.append((probs * (slope - centre) * scaling).astype(bf16))
            table = jnp.where(lane == head, highest, table)
            table = jnp.where(lane == 8 + head, inverse, table)
            table = jnp.where(lane == 16 + head, centre, table)
        attn = product(jnp.concatenate(probs_low, axis=0), value)
        attn_ref[:, span] = join_heads(attn, first).astype(bf16)
        d_query = product(jnp.concatenate(d_score, axis=0), key)
        d_query_ref[:, span] = join_heads(d_query, first).astype(bf16)
    across = jnp.transpose(table)
    own_stats_ref[...] = across[:24]
    for i in range(4):
        stats_ref[i, :8] = jnp.maximum(across[:8], barred_ref[i])
        stats_ref[i, 8:] = across[8:24]
    mixed = window_ref[edge:].astype(f32) + product(attn_ref[...], weights_ref[7])
    mixed_ref[...] = mixed.astype(bf16)


def later_kernel(
    own_ref, one_ref, two_ref, four_ref, eight_ref, gain_ref, weights_ref,
    queries_ref, uppers_ref,
    lines_ref, cots_ref,
):
    gain = gain_ref[...]
    count = own_ref.shape[0]
    one = jnp.concatenate([own_ref[count - edge :], one_ref[:count]], axis=0)
    size = count + edge
    windows = (one, two_ref[:size], four_ref[:size], eight_ref[:size])
    cots = (one_ref[count:], two_ref[size:], four_ref[size:], eight_ref[size:])
    for slot in range(4):
        rows = slice(slot * count, (slot + 1) * count)
        cots_ref[rows] = cots[slot]
        for tap, part in enumerate(normed_taps(windows[slot], gain)):
            lines_ref[tap, rows] = part
    queries = product(lines_ref[0], weights_ref[4])
    queries = queries + product(lines_ref[1], weights_ref[5])
    queries_ref[...] = (queries + product(lines_ref[2], weights_ref[6])).astype(bf16)
    uppers_ref[...] = product_right_t(cots_ref[...], weights_ref[7]).astype(bf16)


def store_partials(even, term, keep_ref, send_ref, matrix):
    term = term.astype(bf16)
    for chip in range(8):
        low = term[chip * 64 : chip * 64 + 32]
        high = term[chip * 64 + 32 : chip * 64 + 64]
        keep_ref[chip, matrix] = jnp.where(even, low, high)
        send_ref[chip, matrix] = jnp.where(even, high, low)


def partials_kernel(core_ref, taps_ref, d_query_ref, attn_ref, upstream_ref, keep_ref, send_ref):
    even = core_ref[0] == 0
    for tap in range(3):
        term = product_left_t(taps_ref[tap], d_query_ref[...])
        store_partials(even, term, keep_ref, send_ref, tap)
    term = product_left_t(attn_ref[...], upstream_ref[...])
    store_partials(even, term, keep_ref, send_ref, 3)


def columns_kernel(
    core_ref, key_ref, value_ref, query_ref, upper_ref, queries_ref, uppers_ref, taps_ref,
    own_ref, one_ref, two_ref, four_ref, eight_ref,
    d_key_ref, d_value_ref, keep_ref, send_ref,
):
    even = core_ref[0] == 0
    count = key_ref.shape[0]
    lane = lax.broadcasted_iota(jnp.int32, (count, 128), 1)
    row = lax.broadcasted_iota(jnp.int32, (count, 128), 0)
    first = lane < 64
    causal = jnp.concatenate([row <= lane] * 2, axis=1)
    scaling = 64 ** (-0.5)
    all_stats = [own_ref[...], one_ref[...], two_ref[...], four_ref[...], eight_ref[...]]
    all_stats = [
        (jnp.where(stats[8:16] > 0.0, stats[:8], 1e30), stats[8:16], stats[16:24])
        for stats in all_stats
    ]
    for pair in range(4):
        span = slice(pair * 128, (pair + 1) * 128)
        key, value = key_ref[:, span], value_ref[:, span]
        d_key = jnp.zeros((count, 128), f32)
        d_value = jnp.zeros((count, 128), f32)
        for slot in range(5):
            if slot == 0:
                query, upper = query_ref[:, span], upper_ref[:, span]
            else:
                rows = slice((slot - 1) * count, slot * count)
                query, upper = queries_ref[rows, span], uppers_ref[rows, span]
            query, upper = split_heads(query, first), split_heads(upper, first)
            highest, inverse, centre = [
                jnp.concatenate([part[pair * 2 : pair * 2 + 1], part[pair * 2 + 1 : pair * 2 + 2]], axis=1)
                for part in all_stats[slot]
            ]
            scores = product_right_t(key, query) * scaling
            probs = jnp.exp(scores - highest) * inverse
            if slot == 0:
                probs = jnp.where(causal, probs, 0.0)
            d_prob = product_right_t(value, upper)
            d_score = (probs * (d_prob - centre) * scaling).astype(bf16)
            d_key = d_key + product(d_score, query)
            d_value = d_value + product(probs.astype(bf16), upper)
        d_key_ref[:, span] = d_key.astype(bf16)
        d_value_ref[:, span] = d_value.astype(bf16)
    for tap in range(3):
        term = product_left_t(taps_ref[tap], d_key_ref[...])
        store_partials(even, term, keep_ref, send_ref, tap)
    store_partials(even, product_left_t(taps_ref[0], d_value_ref[...]), keep_ref, send_ref, 3)


def series_kernel(
    d_query_ref, d_key_ref, d_value_ref, leading_ref, weights_ref, own_ref, upstream_ref, gain_ref,
    grad_ref, d_gain_ref,
):
    count, features = own_ref.shape
    d_normed = product_right_t(d_value_ref[...], weights_ref[3])
    for which, (ref, base) in enumerate(((d_query_ref, 4), (d_key_ref, 0))):
        after = leading_ref[:, which * features : (which + 1) * features]
        window = jnp.concatenate([ref[...], after], axis=0).astype(f32)
        for tap in range(3):
            part = window[tap : tap + count].astype(bf16)
            d_normed = d_normed + product_right_t(part, weights_ref[base + tap])
    values = own_ref[...].astype(f32)
    scale = inverse_rms(values)
    top, rest = in_two(jnp.sum(d_normed * values * scale, axis=0, keepdims=True))
    blank = jnp.zeros((d_gain_ref.shape[0] - 2, features), f32)
    d_gain_ref[...] = jnp.concatenate(
        [top.astype(f32), rest.astype(f32), blank], axis=0
    ).astype(bf16)
    slope = d_normed * gain_ref[...]
    along = jnp.mean(slope * values, axis=-1, keepdims=True)
    d_values = scale * slope - values * (scale * scale * scale * along)
    grad_ref[...] = (upstream_ref[...].astype(f32) + d_values).astype(bf16)


def halve(keep, send):
    return (keep.astype(f32) + other_core(send).astype(f32)).astype(bf16)


def body(
    series, norm_gain, query_kernel, key_kernel, value_weight, out_weight, block_links, grad_out
):
    core = (lax.axis_index("dp") % 2).reshape(1)
    block = lax.axis_index("ctx")
    heads = block_links.shape[2]
    own, cotangent = series[0], grad_out[0]
    count, features = own.shape
    gain = norm_gain.reshape(1, features)

    shard = jnp.concatenate(
        [key_kernel, value_weight[None], query_kernel, out_weight[None]], axis=0
    )
    before_one = shift_ctx(own, 1)
    after_one = shift_ctx(jnp.concatenate([own, cotangent], axis=0), -1)
    shard, before_one, after_one = lax.optimization_barrier((shard, before_one, after_one))
    window = jnp.concatenate([before_one[count - edge :], own], axis=0)
    carried = jnp.concatenate([window, cotangent], axis=0)
    after_four, after_two = shift_ctx(carried, -4), shift_ctx(carried, -2)
    before_four, before_two = shift_ctx(window, 4), shift_ctx(window, 2)
    mine = over_chips(jnp.broadcast_to(shard[None], (8,) + shard.shape))
    mine, before_two, before_four, after_two, after_four = lax.optimization_barrier(
        (mine, before_two, before_four, after_two, after_four)
    )
    other, before_eight, after_eight = lax.optimization_barrier(
        (other_core(mine), shift_ctx(before_four, 4), shift_ctx(after_four, -4))
    )
    before = (before_two, before_four, before_eight)
    after = (after_one, after_two, after_four, after_eight)

    offsets = jnp.array(block_offsets, dtype=jnp.int32)
    reach = (block_links[0, 0] > 0) & (block >= offsets)[None, :]
    barred = jnp.where(reach.T[:, :, None], -3e38, 1e30).astype(f32)
    barred = jnp.broadcast_to(barred, (4, heads, 128))

    half = ((count, features), bf16)
    (
        weights, mixed, attn, d_query, query, upper, key, value, taps, own_stats, stats
    ) = call(
        rows_kernel,
        [((8, features, features), bf16)] + [half] * 7
        + [((3, count, features), bf16), ((24, count), f32), ((4, 24, count), f32)],
        [
            pltpu.VMEM((3, 5 * count, features), bf16),
            pltpu.VMEM((5 * count, features), bf16),
            pltpu.VMEM((5 * count, features), bf16),
        ],
        smem=2,
        inputs=12,
    )(
        core, reach.astype(jnp.int32), mine, other, window, before_one, *before, cotangent, gain,
        barred,
    )
    returned = [shift_ctx(stats[i], -block_offsets[i]) for i in range(4)]
    parts = ((8, 4, 32, features), bf16)
    keep, send = call(partials_kernel, [parts, parts], smem=1, inputs=5)(
        core, taps, d_query, attn, cotangent
    )
    queries, uppers = call(
        later_kernel,
        [((4 * count, features), bf16)] * 2,
        [pltpu.VMEM((3, 4 * count, features), bf16), pltpu.VMEM((4 * count, features), bf16)],
        inputs=7,
    )(own, *after, gain, weights)
    query_half = halve(keep, send)
    d_key, d_value, keep, send = call(
        columns_kernel, [half, half, parts, parts], smem=1, inputs=13
    )(core, key, value, query, upper, queries, uppers, taps, own_stats, *returned)
    leading = shift_ctx(jnp.concatenate([d_query[:edge], d_key[:edge]], axis=1), -1)
    key_half = halve(keep, send)
    grad_series, d_gain = call(
        series_kernel, [half, ((edge, features), bf16)], inputs=8
    )(d_query, d_key, d_value, leading, weights, own, cotangent, gain)
    terms = jnp.stack([query_half, key_half], axis=1).reshape(16, 128, features)
    d_gain = jnp.broadcast_to(d_gain[None], (16, edge, features))
    arrived = over_plane(jnp.concatenate([terms, d_gain], axis=1))
    arrived = jnp.sum(arrived.astype(f32), axis=0)
    rows = arrived[:128].astype(bf16).reshape(16, 8, features)
    top, rest = in_two(jnp.sum(arrived[128:], axis=0).reshape(4, 128))
    extra = jnp.broadcast_to(jnp.concatenate([top, rest], axis=0)[None], (16, 8, 128))
    arrived = over_z(jnp.concatenate([rows, extra], axis=2)).astype(f32)
    summed = jnp.sum(arrived, axis=0)
    core_gain = summed[:4, features:] + summed[4:, features:]
    gain_total = (core_gain + other_core(core_gain)).reshape(features)
    summed = summed[:, :features].astype(bf16)
    mine = over_z(jnp.broadcast_to(summed[None], (16, 8, features)))
    other = other_side(mine)
    first = block % 2 == 0
    for_query = jnp.where(first, mine, other).reshape(4, 32, features).astype(f32)
    for_key = jnp.where(first, other, mine).reshape(4, 32, features).astype(f32)
    return (
        mixed[None],
        grad_series[None],
        gain_total,
        for_query[:3],
        for_key[:3],
        for_key[3],
        for_query[3],
    )


def solution(mesh):
    placed = (
        P("dp", "ctx", None),
        P(),
        P(None, "dp", None),
        P(None, "dp", None),
        P("dp", None),
        P("dp", None),
        P("dp", "ctx", None, None),
        P("dp", "ctx", None),
    )
    return jax.shard_map(
        body,
        mesh=mesh,
        in_specs=placed,
        out_specs=(
            P("dp", "ctx", None),
            P("dp", "ctx", None),
            P(),
            P(None, "dp", None),
            P(None, "dp", None),
            P("dp", None),
            P("dp", None),
        ),
        check_vma=False,
    )
```

```python
import jax
import jax.numpy as jnp
from jax import lax
from jax.experimental import pallas as pl
from jax.experimental.pallas import tpu as pltpu
from jax.sharding import PartitionSpec as P

block_offsets = (1, 2, 4, 8)
epsilon = 1e-06
hidden = -1e30
f32 = jnp.float32
bf16 = jnp.bfloat16
edge = 16
plane_groups = [
    [(2 * chip + core) * 32 + 2 * z + side for chip in range(8) for side in range(2)]
    for core in range(2)
    for z in range(16)
]
chip_groups = [[2 * chip + core for chip in range(8)] for core in range(2)]
z_groups = [[2 * z + side for z in range(16)] for side in range(2)]


def shift_ctx(shard, by):
    devices = lax.axis_size("ctx")
    pairs = [(i, i + by) for i in range(devices) if 0 <= i + by < devices]
    return lax.ppermute(shard, "ctx", pairs)


def dp_to(shard, dx, dy, dc):
    def target(i):
        x, y, c = i // 8, (i // 2) % 4, i % 2
        return ((x + dx) % 2) * 8 + ((y + dy) % 4) * 2 + (c + dc) % 2

    return lax.ppermute(shard, "dp", [(i, target(i)) for i in range(16)])


def other_core(shard):
    return dp_to(shard, 0, 0, 1)


def over_chips(stacked):
    return lax.all_to_all(stacked, "dp", 0, 0, axis_index_groups=chip_groups, tiled=True)


def over_plane(stacked):
    return lax.all_to_all(
        stacked, ("dp", "ctx"), 0, 0, axis_index_groups=plane_groups, tiled=True
    )


def over_z(stacked):
    return lax.all_to_all(stacked, "ctx", 0, 0, axis_index_groups=z_groups, tiled=True)


def other_side(shard):
    return lax.ppermute(shard, "ctx", [(i, i ^ 1) for i in range(32)])


def product(left, right):
    return jnp.dot(left, right, preferred_element_type=f32)


def product_right_t(left, right):
    return lax.dot_general(left, right, (((1,), (1,)), ((), ())), preferred_element_type=f32)


def product_left_t(left, right):
    return lax.dot_general(left, right, (((0,), (0,)), ((), ())), preferred_element_type=f32)


def in_two(values):
    top = values.astype(bf16)
    return top, (values - top.astype(f32)).astype(bf16)


def inverse_rms(values):
    return lax.rsqrt(jnp.mean(values * values, axis=-1, keepdims=True) + epsilon)


def normed_taps(window, gain):
    values = window.astype(f32)
    normed = values * inverse_rms(values) * gain
    count = window.shape[0] - edge
    return [normed[edge - tap : edge - tap + count].astype(bf16) for tap in range(3)]


def call(kernel, outs, scratch=(), smem=0, inputs=0):
    return pl.pallas_call(
        kernel,
        out_shape=[jax.ShapeDtypeStruct(shape, kind) for shape, kind in outs],
        in_specs=[pl.BlockSpec(memory_space=pltpu.SMEM)] * smem
        + [pl.BlockSpec(memory_space=pltpu.VMEM)] * (inputs - smem),
        out_specs=[pl.BlockSpec(memory_space=pltpu.VMEM)] * len(outs),
        scratch_shapes=list(scratch),
        compiler_params=pltpu.CompilerParams(vmem_limit_bytes=50 * 1024 * 1024),
    )


def split_heads(pair, first):
    wide = pair.astype(f32)
    return jnp.concatenate(
        [jnp.where(first, wide, 0.0), jnp.where(first, 0.0, wide)], axis=0
    ).astype(bf16)


def join_heads(stacked, first):
    count = stacked.shape[0] // 2
    return jnp.where(first, stacked[:count], stacked[count:])


def rows_kernel(
    core_ref, links_ref, mine_ref, other_ref, window_ref, one_ref, two_ref, four_ref, eight_ref, upstream_ref, gain_ref, barred_ref,
    weights_ref, mixed_ref, attn_ref, d_query_ref, query_ref, upper_ref, key_ref, value_ref,
    taps_ref, own_stats_ref, stats_ref,
    lines_ref, keys_ref, values_ref,
):
    even = core_ref[0] == 0
    for chip in range(8):
        for matrix in range(8):
            mine, other = mine_ref[chip, matrix], other_ref[chip, matrix]
            weights_ref[matrix, chip * 64 : chip * 64 + 32] = jnp.where(even, mine, other)
            weights_ref[matrix, chip * 64 + 32 : chip * 64 + 64] = jnp.where(even, other, mine)
    gain = gain_ref[...]
    count = one_ref.shape[0]
    one = jnp.concatenate([two_ref[count:], one_ref[...]], axis=0)
    for slot, window in enumerate(
        (window_ref[...], one, two_ref[...], four_ref[...], eight_ref[...])
    ):
        for tap, part in enumerate(normed_taps(window, gain)):
            lines_ref[tap, slot * count : (slot + 1) * count] = part
    for tap in range(3):
        taps_ref[tap] = lines_ref[tap, :count]
    keys = product(lines_ref[0], weights_ref[0])
    keys = keys + product(lines_ref[1], weights_ref[1])
    keys_ref[...] = (keys + product(lines_ref[2], weights_ref[2])).astype(bf16)
    values_ref[...] = product(lines_ref[0], weights_ref[3]).astype(bf16)
    query = product(taps_ref[0], weights_ref[4])
    query = query + product(taps_ref[1], weights_ref[5])
    query_ref[...] = (query + product(taps_ref[2], weights_ref[6])).astype(bf16)
    upper_ref[...] = product_right_t(upstream_ref[...], weights_ref[7]).astype(bf16)
    key_ref[...] = keys_ref[:count]
    value_ref[...] = values_ref[:count]

    lane = lax.broadcasted_iota(jnp.int32, (count, 128), 1)
    row = lax.broadcasted_iota(jnp.int32, (count, 128), 0)
    first = lane < 64
    causal = jnp.where(lane <= row, 0.0, hidden)
    table = jnp.zeros((count, 128), f32)
    scaling = 64 ** (-0.5)
    for pair in range(4):
        span = slice(pair * 128, (pair + 1) * 128)
        query = split_heads(query_ref[:, span], first)
        upper = split_heads(upper_ref[:, span], first)
        key, value = keys_ref[:, span], values_ref[:, span]
        scores = product_right_t(query, key) * scaling
        d_prob = product_right_t(upper, value)
        probs_low, d_score = [], []
        for inner in range(2):
            head = pair * 2 + inner
            mine = scores[inner * count : (inner + 1) * count]
            parts = [mine[:, :count] + causal]
            for i in range(4):
                bias = jnp.where(links_ref[head, i] > 0, 0.0, hidden)
                parts.append(mine[:, (i + 1) * count : (i + 2) * count] + bias)
            mine = jnp.concatenate(parts, axis=1)
            highest = jnp.max(mine, axis=1, keepdims=True)
            weight = jnp.exp(mine - highest)
            inverse = 1.0 / jnp.sum(weight, axis=1, keepdims=True)
            probs = weight * inverse
            slope = d_prob[inner * count : (inner + 1) * count]
            centre = jnp.sum(probs * slope, axis=1, keepdims=True)
            probs_low.append(probs.astype(bf16))
            d_score.append((probs * (slope - centre) * scaling).astype(bf16))
            table = jnp.where(lane == head, highest, table)
            table = jnp.where(lane == 8 + head, inverse, table)
            table = jnp.where(lane == 16 + head, centre, table)
        attn = product(jnp.concatenate(probs_low, axis=0), value)
        attn_ref[:, span] = join_heads(attn, first).astype(bf16)
        d_query = product(jnp.concatenate(d_score, axis=0), key)
        d_query_ref[:, span] = join_heads(d_query, first).astype(bf16)
    across = jnp.transpose(table)
    own_stats_ref[...] = across[:24]
    for i in range(4):
        stats_ref[i, :8] = jnp.maximum(across[:8], barred_ref[i])
        stats_ref[i, 8:] = across[8:24]
    mixed = window_ref[edge:].astype(f32) + product(attn_ref[...], weights_ref[7])
    mixed_ref[...] = mixed.astype(bf16)


def later_kernel(
    own_ref, one_ref, two_ref, four_ref, eight_ref, gain_ref, weights_ref,
    queries_ref, uppers_ref,
    lines_ref, cots_ref,
):
    gain = gain_ref[...]
    count = own_ref.shape[0]
    one = jnp.concatenate([own_ref[count - edge :], one_ref[:count]], axis=0)
    size = count + edge
    windows = (one, two_ref[:size], four_ref[:size], eight_ref[:size])
    cots = (one_ref[count:], two_ref[size:], four_ref[size:], eight_ref[size:])
    for slot in range(4):
        rows = slice(slot * count, (slot + 1) * count)
        cots_ref[rows] = cots[slot]
        for tap, part in enumerate(normed_taps(windows[slot], gain)):
            lines_ref[tap, rows] = part
    queries = product(lines_ref[0], weights_ref[4])
    queries = queries + product(lines_ref[1], weights_ref[5])
    queries_ref[...] = (queries + product(lines_ref[2], weights_ref[6])).astype(bf16)
    uppers_ref[...] = product_right_t(cots_ref[...], weights_ref[7]).astype(bf16)


def store_partials(even, term, keep_ref, send_ref, matrix):
    term = term.astype(bf16)
    for chip in range(8):
        low = term[chip * 64 : chip * 64 + 32]
        high = term[chip * 64 + 32 : chip * 64 + 64]
        keep_ref[chip, matrix] = jnp.where(even, low, high)
        send_ref[chip, matrix] = jnp.where(even, high, low)


def partials_kernel(core_ref, taps_ref, d_query_ref, attn_ref, upstream_ref, keep_ref, send_ref):
    even = core_ref[0] == 0
    for tap in range(3):
        term = product_left_t(taps_ref[tap], d_query_ref[...])
        store_partials(even, term, keep_ref, send_ref, tap)
    term = product_left_t(attn_ref[...], upstream_ref[...])
    store_partials(even, term, keep_ref, send_ref, 3)


def columns_kernel(
    core_ref, key_ref, value_ref, query_ref, upper_ref, queries_ref, uppers_ref, taps_ref,
    own_ref, one_ref, two_ref, four_ref, eight_ref,
    d_key_ref, d_value_ref, keep_ref, send_ref,
):
    even = core_ref[0] == 0
    count = key_ref.shape[0]
    lane = lax.broadcasted_iota(jnp.int32, (count, 128), 1)
    row = lax.broadcasted_iota(jnp.int32, (count, 128), 0)
    first = lane < 64
    causal = jnp.concatenate([row <= lane] * 2, axis=1)
    scaling = 64 ** (-0.5)
    all_stats = [own_ref[...], one_ref[...], two_ref[...], four_ref[...], eight_ref[...]]
    all_stats = [
        (jnp.where(stats[8:16] > 0.0, stats[:8], 1e30), stats[8:16], stats[16:24])
        for stats in all_stats
    ]
    for pair in range(4):
        span = slice(pair * 128, (pair + 1) * 128)
        key, value = key_ref[:, span], value_ref[:, span]
        d_key = jnp.zeros((count, 128), f32)
        d_value = jnp.zeros((count, 128), f32)
        for slot in range(5):
            if slot == 0:
                query, upper = query_ref[:, span], upper_ref[:, span]
            else:
                rows = slice((slot - 1) * count, slot * count)
                query, upper = queries_ref[rows, span], uppers_ref[rows, span]
            query, upper = split_heads(query, first), split_heads(upper, first)
            highest, inverse, centre = [
                jnp.concatenate([part[pair * 2 : pair * 2 + 1], part[pair * 2 + 1 : pair * 2 + 2]], axis=1)
                for part in all_stats[slot]
            ]
            scores = product_right_t(key, query) * scaling
            probs = jnp.exp(scores - highest) * inverse
            if slot == 0:
                probs = jnp.where(causal, probs, 0.0)
            d_prob = product_right_t(value, upper)
            d_score = (probs * (d_prob - centre) * scaling).astype(bf16)
            d_key = d_key + product(d_score, query)
            d_value = d_value + product(probs.astype(bf16), upper)
        d_key_ref[:, span] = d_key.astype(bf16)
        d_value_ref[:, span] = d_value.astype(bf16)
    for tap in range(3):
        term = product_left_t(taps_ref[tap], d_key_ref[...])
        store_partials(even, term, keep_ref, send_ref, tap)
    store_partials(even, product_left_t(taps_ref[0], d_value_ref[...]), keep_ref, send_ref, 3)


def normed_kernel(
    d_query_ref, d_key_ref, d_value_ref, weights_ref, window_ref, d_normed_ref, back_ref, d_gain_ref
):
    count, features = d_query_ref.shape
    blank = jnp.zeros((edge, features), f32)
    own = product_right_t(d_value_ref[...], weights_ref[3])
    d_normed = jnp.concatenate([blank, own], axis=0)
    for ref, base in ((d_query_ref, 4), (d_key_ref, 0)):
        rows = jnp.concatenate([blank, ref[...].astype(f32), blank], axis=0)
        for tap in range(3):
            part = rows[tap : tap + count + edge].astype(bf16)
            d_normed = d_normed + product_right_t(part, weights_ref[base + tap])
    values = window_ref[...].astype(f32)
    top, rest = in_two(jnp.sum(d_normed * values * inverse_rms(values), axis=0, keepdims=True))
    unused = jnp.zeros((d_gain_ref.shape[0] - 2, features), f32)
    d_gain_ref[...] = jnp.concatenate(
        [top.astype(f32), rest.astype(f32), unused], axis=0
    ).astype(bf16)
    back_ref[...] = d_normed[:edge]
    d_normed_ref[...] = d_normed[edge:]


def series_kernel(d_normed_ref, later_ref, window_ref, upstream_ref, gain_ref, grad_ref):
    count = d_normed_ref.shape[0]
    d_normed = jnp.concatenate(
        [d_normed_ref[: count - edge], d_normed_ref[count - edge :] + later_ref[...]], axis=0
    )
    values = window_ref[edge:].astype(f32)
    scale = inverse_rms(values)
    slope = d_normed * gain_ref[...]
    along = jnp.mean(slope * values, axis=-1, keepdims=True)
    d_values = scale * slope - values * (scale * scale * scale * along)
    grad_ref[...] = (upstream_ref[...].astype(f32) + d_values).astype(bf16)


def halve(keep, send):
    return (keep.astype(f32) + other_core(send).astype(f32)).astype(bf16)


def body(
    series, norm_gain, query_kernel, key_kernel, value_weight, out_weight, block_links, grad_out
):
    core = (lax.axis_index("dp") % 2).reshape(1)
    block = lax.axis_index("ctx")
    heads = block_links.shape[2]
    own, cotangent = series[0], grad_out[0]
    count, features = own.shape
    gain = norm_gain.reshape(1, features)

    shard = jnp.concatenate(
        [key_kernel, value_weight[None], query_kernel, out_weight[None]], axis=0
    )
    before_one = shift_ctx(own, 1)
    after_one = shift_ctx(jnp.concatenate([own, cotangent], axis=0), -1)
    shard, before_one, after_one = lax.optimization_barrier((shard, before_one, after_one))
    window = jnp.concatenate([before_one[count - edge :], own], axis=0)
    carried = jnp.concatenate([window, cotangent], axis=0)
    after_four, after_two = shift_ctx(carried, -4), shift_ctx(carried, -2)
    before_four, before_two = shift_ctx(window, 4), shift_ctx(window, 2)
    mine = over_chips(jnp.broadcast_to(shard[None], (8,) + shard.shape))
    before_eight, after_eight = shift_ctx(before_four, 4), shift_ctx(after_four, -4)
    mine, before_two, before_four, after_two, after_four = lax.optimization_barrier(
        (mine, before_two, before_four, after_two, after_four)
    )
    other, before_eight, after_eight = lax.optimization_barrier(
        (other_core(mine), before_eight, after_eight)
    )
    before = (before_two, before_four, before_eight)
    after = (after_one, after_two, after_four, after_eight)

    offsets = jnp.array(block_offsets, dtype=jnp.int32)
    reach = (block_links[0, 0] > 0) & (block >= offsets)[None, :]
    barred = jnp.where(reach.T[:, :, None], -3e38, 1e30).astype(f32)
    barred = jnp.broadcast_to(barred, (4, heads, 128))

    half = ((count, features), bf16)
    (
        weights, mixed, attn, d_query, query, upper, key, value, taps, own_stats, stats
    ) = call(
        rows_kernel,
        [((8, features, features), bf16)] + [half] * 7
        + [((3, count, features), bf16), ((24, count), f32), ((4, 24, count), f32)],
        [
            pltpu.VMEM((3, 5 * count, features), bf16),
            pltpu.VMEM((5 * count, features), bf16),
            pltpu.VMEM((5 * count, features), bf16),
        ],
        smem=2,
        inputs=12,
    )(
        core, reach.astype(jnp.int32), mine, other, window, before_one, *before, cotangent, gain,
        barred,
    )
    returned = [shift_ctx(stats[i], -block_offsets[i]) for i in range(4)]
    parts = ((8, 4, 32, features), bf16)
    keep, send = call(partials_kernel, [parts, parts], smem=1, inputs=5)(
        core, taps, d_query, attn, cotangent
    )
    queries, uppers = call(
        later_kernel,
        [((4 * count, features), bf16)] * 2,
        [pltpu.VMEM((3, 4 * count, features), bf16), pltpu.VMEM((4 * count, features), bf16)],
        inputs=7,
    )(own, *after, gain, weights)
    query_half = halve(keep, send)
    d_key, d_value, keep, send = call(
        columns_kernel, [half, half, parts, parts], smem=1, inputs=13
    )(core, key, value, query, upper, queries, uppers, taps, own_stats, *returned)
    key_half = halve(keep, send)
    d_normed, back, d_gain = call(
        normed_kernel,
        [((count, features), f32), ((edge, features), f32), ((edge, features), bf16)],
        inputs=5,
    )(d_query, d_key, d_value, weights, window)
    later = shift_ctx(back, -1)
    terms = jnp.stack([query_half, key_half], axis=1).reshape(16, 128, features)
    d_gain = jnp.broadcast_to(d_gain[None], (16, edge, features))
    arrived = over_plane(jnp.concatenate([terms, d_gain], axis=1))
    arrived = jnp.sum(arrived.astype(f32), axis=0)
    rows = arrived[:128].astype(bf16).reshape(16, 8, features)
    top, rest = in_two(jnp.sum(arrived[128:], axis=0).reshape(4, 128))
    extra = jnp.broadcast_to(jnp.concatenate([top, rest], axis=0)[None], (16, 8, 128))
    arrived = over_z(jnp.concatenate([rows, extra], axis=2)).astype(f32)
    summed = jnp.sum(arrived, axis=0)
    d_normed, summed = lax.optimization_barrier((d_normed, summed))
    (grad_series,) = call(series_kernel, [half], inputs=5)(
        d_normed, later, window, cotangent, gain
    )
    core_gain = summed[:4, features:] + summed[4:, features:]
    gain_total = (core_gain + other_core(core_gain)).reshape(features)
    summed = summed[:, :features].astype(bf16)
    mine = over_z(jnp.broadcast_to(summed[None], (16, 8, features)))
    other = other_side(mine)
    first = block % 2 == 0
    for_query = jnp.where(first, mine, other).reshape(4, 32, features).astype(f32)
    for_key = jnp.where(first, other, mine).reshape(4, 32, features).astype(f32)
    return (
        mixed[None],
        grad_series[None],
        gain_total,
        for_query[:3],
        for_key[:3],
        for_key[3],
        for_query[3],
    )


def solution(mesh):
    placed = (
        P("dp", "ctx", None),
        P(),
        P(None, "dp", None),
        P(None, "dp", None),
        P("dp", None),
        P("dp", None),
        P("dp", "ctx", None, None),
        P("dp", "ctx", None),
    )
    return jax.shard_map(
        body,
        mesh=mesh,
        in_specs=placed,
        out_specs=(
            P("dp", "ctx", None),
            P("dp", "ctx", None),
            P(),
            P(None, "dp", None),
            P(None, "dp", None),
            P("dp", None),
            P("dp", None),
        ),
        check_vma=False,
    )
```

```python
import jax
import jax.numpy as jnp
from jax import lax
from jax.experimental import pallas as pl
from jax.experimental.pallas import tpu as pltpu
from jax.sharding import PartitionSpec as P

block_offsets = (1, 2, 4, 8)
epsilon = 1e-06
hidden = -1e30
f32 = jnp.float32
bf16 = jnp.bfloat16
edge = 16
plane_groups = [
    [(2 * chip + core) * 32 + 2 * z + side for chip in range(8) for side in range(2)]
    for core in range(2)
    for z in range(16)
]
chip_groups = [[2 * chip + core for chip in range(8)] for core in range(2)]
z_groups = [[2 * z + side for z in range(16)] for side in range(2)]


def shift_ctx(shard, by):
    devices = lax.axis_size("ctx")
    pairs = [(i, i + by) for i in range(devices) if 0 <= i + by < devices]
    return lax.ppermute(shard, "ctx", pairs)


def dp_to(shard, dx, dy, dc):
    def target(i):
        x, y, c = i // 8, (i // 2) % 4, i % 2
        return ((x + dx) % 2) * 8 + ((y + dy) % 4) * 2 + (c + dc) % 2

    return lax.ppermute(shard, "dp", [(i, target(i)) for i in range(16)])


def other_core(shard):
    return dp_to(shard, 0, 0, 1)


def over_chips(stacked):
    return lax.all_to_all(stacked, "dp", 0, 0, axis_index_groups=chip_groups, tiled=True)


def over_plane(stacked):
    return lax.all_to_all(
        stacked, ("dp", "ctx"), 0, 0, axis_index_groups=plane_groups, tiled=True
    )


def over_z(stacked):
    return lax.all_to_all(stacked, "ctx", 0, 0, axis_index_groups=z_groups, tiled=True)


def other_side(shard):
    return lax.ppermute(shard, "ctx", [(i, i ^ 1) for i in range(32)])


def product(left, right):
    return jnp.dot(left, right, preferred_element_type=f32)


def product_right_t(left, right):
    return lax.dot_general(left, right, (((1,), (1,)), ((), ())), preferred_element_type=f32)


def product_left_t(left, right):
    return lax.dot_general(left, right, (((0,), (0,)), ((), ())), preferred_element_type=f32)


def in_two(values):
    top = values.astype(bf16)
    return top, (values - top.astype(f32)).astype(bf16)


def inverse_rms(values):
    return lax.rsqrt(jnp.mean(values * values, axis=-1, keepdims=True) + epsilon)


def normed_taps(window, gain):
    values = window.astype(f32)
    normed = values * inverse_rms(values) * gain
    count = window.shape[0] - edge
    return [normed[edge - tap : edge - tap + count].astype(bf16) for tap in range(3)]


def call(kernel, outs, scratch=(), smem=0, inputs=0):
    return pl.pallas_call(
        kernel,
        out_shape=[jax.ShapeDtypeStruct(shape, kind) for shape, kind in outs],
        in_specs=[pl.BlockSpec(memory_space=pltpu.SMEM)] * smem
        + [pl.BlockSpec(memory_space=pltpu.VMEM)] * (inputs - smem),
        out_specs=[pl.BlockSpec(memory_space=pltpu.VMEM)] * len(outs),
        scratch_shapes=list(scratch),
        compiler_params=pltpu.CompilerParams(vmem_limit_bytes=50 * 1024 * 1024),
    )


def split_heads(pair, first):
    wide = pair.astype(f32)
    return jnp.concatenate(
        [jnp.where(first, wide, 0.0), jnp.where(first, 0.0, wide)], axis=0
    ).astype(bf16)


def join_heads(stacked, first):
    count = stacked.shape[0] // 2
    return jnp.where(first, stacked[:count], stacked[count:])


def rows_kernel(
    core_ref, links_ref, mine_ref, other_ref, window_ref, one_ref, two_ref, four_ref, eight_ref, upstream_ref, gain_ref, barred_ref,
    weights_ref, mixed_ref, attn_ref, d_query_ref, query_ref, upper_ref, key_ref, value_ref,
    taps_ref, own_stats_ref, stats_ref,
    lines_ref, keys_ref, values_ref,
):
    even = core_ref[0] == 0
    for chip in range(8):
        for matrix in range(8):
            mine, other = mine_ref[chip, matrix], other_ref[chip, matrix]
            weights_ref[matrix, chip * 64 : chip * 64 + 32] = jnp.where(even, mine, other)
            weights_ref[matrix, chip * 64 + 32 : chip * 64 + 64] = jnp.where(even, other, mine)
    gain = gain_ref[...]
    count = one_ref.shape[0]
    one = jnp.concatenate([two_ref[count:], one_ref[...]], axis=0)
    for slot, window in enumerate(
        (window_ref[...], one, two_ref[...], four_ref[...], eight_ref[...])
    ):
        for tap, part in enumerate(normed_taps(window, gain)):
            lines_ref[tap, slot * count : (slot + 1) * count] = part
    for tap in range(3):
        taps_ref[tap] = lines_ref[tap, :count]
    keys = product(lines_ref[0], weights_ref[0])
    keys = keys + product(lines_ref[1], weights_ref[1])
    keys_ref[...] = (keys + product(lines_ref[2], weights_ref[2])).astype(bf16)
    values_ref[...] = product(lines_ref[0], weights_ref[3]).astype(bf16)
    query = product(taps_ref[0], weights_ref[4])
    query = query + product(taps_ref[1], weights_ref[5])
    query_ref[...] = (query + product(taps_ref[2], weights_ref[6])).astype(bf16)
    upper_ref[...] = product_right_t(upstream_ref[...], weights_ref[7]).astype(bf16)
    key_ref[...] = keys_ref[:count]
    value_ref[...] = values_ref[:count]

    lane = lax.broadcasted_iota(jnp.int32, (count, 128), 1)
    row = lax.broadcasted_iota(jnp.int32, (count, 128), 0)
    first = lane < 64
    causal = jnp.where(lane <= row, 0.0, hidden)
    table = jnp.zeros((count, 128), f32)
    scaling = 64 ** (-0.5)
    for pair in range(4):
        span = slice(pair * 128, (pair + 1) * 128)
        query = split_heads(query_ref[:, span], first)
        upper = split_heads(upper_ref[:, span], first)
        key, value = keys_ref[:, span], values_ref[:, span]
        scores = product_right_t(query, key) * scaling
        d_prob = product_right_t(upper, value)
        probs_low, d_score = [], []
        for inner in range(2):
            head = pair * 2 + inner
            mine = scores[inner * count : (inner + 1) * count]
            parts = [mine[:, :count] + causal]
            for i in range(4):
                bias = jnp.where(links_ref[head, i] > 0, 0.0, hidden)
                parts.append(mine[:, (i + 1) * count : (i + 2) * count] + bias)
            mine = jnp.concatenate(parts, axis=1)
            highest = jnp.max(mine, axis=1, keepdims=True)
            weight = jnp.exp(mine - highest)
            inverse = 1.0 / jnp.sum(weight, axis=1, keepdims=True)
            probs = weight * inverse
            slope = d_prob[inner * count : (inner + 1) * count]
            centre = jnp.sum(probs * slope, axis=1, keepdims=True)
            probs_low.append(probs.astype(bf16))
            d_score.append((probs * (slope - centre) * scaling).astype(bf16))
            table = jnp.where(lane == head, highest, table)
            table = jnp.where(lane == 8 + head, inverse, table)
            table = jnp.where(lane == 16 + head, centre, table)
        attn = product(jnp.concatenate(probs_low, axis=0), value)
        attn_ref[:, span] = join_heads(attn, first).astype(bf16)
        d_query = product(jnp.concatenate(d_score, axis=0), key)
        d_query_ref[:, span] = join_heads(d_query, first).astype(bf16)
    across = jnp.transpose(table)
    own_stats_ref[...] = across[:24]
    for i in range(4):
        stats_ref[i, :8] = jnp.maximum(across[:8], barred_ref[i])
        stats_ref[i, 8:] = across[8:24]
    mixed = window_ref[edge:].astype(f32) + product(attn_ref[...], weights_ref[7])
    mixed_ref[...] = mixed.astype(bf16)


def later_kernel(
    own_ref, one_ref, two_ref, four_ref, eight_ref, gain_ref, weights_ref,
    queries_ref, uppers_ref,
    lines_ref, cots_ref,
):
    gain = gain_ref[...]
    count = own_ref.shape[0]
    one = jnp.concatenate([own_ref[count - edge :], one_ref[:count]], axis=0)
    size = count + edge
    windows = (one, two_ref[:size], four_ref[:size], eight_ref[:size])
    cots = (one_ref[count:], two_ref[size:], four_ref[size:], eight_ref[size:])
    for slot in range(4):
        rows = slice(slot * count, (slot + 1) * count)
        cots_ref[rows] = cots[slot]
        for tap, part in enumerate(normed_taps(windows[slot], gain)):
            lines_ref[tap, rows] = part
    queries = product(lines_ref[0], weights_ref[4])
    queries = queries + product(lines_ref[1], weights_ref[5])
    queries_ref[...] = (queries + product(lines_ref[2], weights_ref[6])).astype(bf16)
    uppers_ref[...] = product_right_t(cots_ref[...], weights_ref[7]).astype(bf16)


def store_partials(even, term, keep_ref, send_ref, matrix):
    term = term.astype(bf16)
    for chip in range(8):
        low = term[chip * 64 : chip * 64 + 32]
        high = term[chip * 64 + 32 : chip * 64 + 64]
        keep_ref[chip, matrix] = jnp.where(even, low, high)
        send_ref[chip, matrix] = jnp.where(even, high, low)


def partials_kernel(core_ref, taps_ref, d_query_ref, attn_ref, upstream_ref, keep_ref, send_ref):
    even = core_ref[0] == 0
    for tap in range(3):
        term = product_left_t(taps_ref[tap], d_query_ref[...])
        store_partials(even, term, keep_ref, send_ref, tap)
    term = product_left_t(attn_ref[...], upstream_ref[...])
    store_partials(even, term, keep_ref, send_ref, 3)


def columns_kernel(
    core_ref, key_ref, value_ref, query_ref, upper_ref, queries_ref, uppers_ref, taps_ref,
    own_ref, one_ref, two_ref, four_ref, eight_ref,
    d_key_ref, d_value_ref, keep_ref, send_ref,
):
    even = core_ref[0] == 0
    count = key_ref.shape[0]
    lane = lax.broadcasted_iota(jnp.int32, (count, 128), 1)
    row = lax.broadcasted_iota(jnp.int32, (count, 128), 0)
    first = lane < 64
    causal = jnp.concatenate([row <= lane] * 2, axis=1)
    scaling = 64 ** (-0.5)
    all_stats = [own_ref[...], one_ref[...], two_ref[...], four_ref[...], eight_ref[...]]
    all_stats = [
        (jnp.where(stats[8:16] > 0.0, stats[:8], 1e30), stats[8:16], stats[16:24])
        for stats in all_stats
    ]
    for pair in range(4):
        span = slice(pair * 128, (pair + 1) * 128)
        key, value = key_ref[:, span], value_ref[:, span]
        d_key = jnp.zeros((count, 128), f32)
        d_value = jnp.zeros((count, 128), f32)
        for slot in range(5):
            if slot == 0:
                query, upper = query_ref[:, span], upper_ref[:, span]
            else:
                rows = slice((slot - 1) * count, slot * count)
                query, upper = queries_ref[rows, span], uppers_ref[rows, span]
            query, upper = split_heads(query, first), split_heads(upper, first)
            highest, inverse, centre = [
                jnp.concatenate([part[pair * 2 : pair * 2 + 1], part[pair * 2 + 1 : pair * 2 + 2]], axis=1)
                for part in all_stats[slot]
            ]
            scores = product_right_t(key, query) * scaling
            probs = jnp.exp(scores - highest) * inverse
            if slot == 0:
                probs = jnp.where(causal, probs, 0.0)
            d_prob = product_right_t(value, upper)
            d_score = (probs * (d_prob - centre) * scaling).astype(bf16)
            d_key = d_key + product(d_score, query)
            d_value = d_value + product(probs.astype(bf16), upper)
        d_key_ref[:, span] = d_key.astype(bf16)
        d_value_ref[:, span] = d_value.astype(bf16)
    for tap in range(3):
        term = product_left_t(taps_ref[tap], d_key_ref[...])
        store_partials(even, term, keep_ref, send_ref, tap)
    store_partials(even, product_left_t(taps_ref[0], d_value_ref[...]), keep_ref, send_ref, 3)


def normed_kernel(
    d_query_ref, d_key_ref, d_value_ref, weights_ref, window_ref, d_normed_ref, back_ref, d_gain_ref
):
    count, features = d_query_ref.shape
    blank = jnp.zeros((edge, features), f32)
    own = product_right_t(d_value_ref[...], weights_ref[3])
    d_normed = jnp.concatenate([blank, own], axis=0)
    for ref, base in ((d_query_ref, 4), (d_key_ref, 0)):
        rows = jnp.concatenate([blank, ref[...].astype(f32), blank], axis=0)
        for tap in range(3):
            part = rows[tap : tap + count + edge].astype(bf16)
            d_normed = d_normed + product_right_t(part, weights_ref[base + tap])
    values = window_ref[...].astype(f32)
    top, rest = in_two(jnp.sum(d_normed * values * inverse_rms(values), axis=0, keepdims=True))
    unused = jnp.zeros((d_gain_ref.shape[0] - 2, features), f32)
    d_gain_ref[...] = jnp.concatenate(
        [top.astype(f32), rest.astype(f32), unused], axis=0
    ).astype(bf16)
    back_ref[...] = d_normed[:edge]
    d_normed_ref[...] = d_normed[edge:]


def series_kernel(d_normed_ref, later_ref, window_ref, upstream_ref, gain_ref, grad_ref):
    count = d_normed_ref.shape[0]
    d_normed = jnp.concatenate(
        [d_normed_ref[: count - edge], d_normed_ref[count - edge :] + later_ref[...]], axis=0
    )
    values = window_ref[edge:].astype(f32)
    scale = inverse_rms(values)
    slope = d_normed * gain_ref[...]
    along = jnp.mean(slope * values, axis=-1, keepdims=True)
    d_values = scale * slope - values * (scale * scale * scale * along)
    grad_ref[...] = (upstream_ref[...].astype(f32) + d_values).astype(bf16)


def halve(keep, send):
    return (keep.astype(f32) + other_core(send).astype(f32)).astype(bf16)


def body(
    series, norm_gain, query_kernel, key_kernel, value_weight, out_weight, block_links, grad_out
):
    core = (lax.axis_index("dp") % 2).reshape(1)
    block = lax.axis_index("ctx")
    heads = block_links.shape[2]
    own, cotangent = series[0], grad_out[0]
    count, features = own.shape
    gain = norm_gain.reshape(1, features)

    shard = jnp.concatenate(
        [key_kernel, value_weight[None], query_kernel, out_weight[None]], axis=0
    )
    before_one = shift_ctx(own, 1)
    after_one = shift_ctx(jnp.concatenate([own, cotangent], axis=0), -1)
    shard, before_one, after_one = lax.optimization_barrier((shard, before_one, after_one))
    window = jnp.concatenate([before_one[count - edge :], own], axis=0)
    carried = jnp.concatenate([window, cotangent], axis=0)
    after_four, after_two = shift_ctx(carried, -4), shift_ctx(carried, -2)
    before_four, before_two = shift_ctx(window, 4), shift_ctx(window, 2)
    mine = over_chips(jnp.broadcast_to(shard[None], (8,) + shard.shape))
    before_eight, after_eight = shift_ctx(before_four, 4), shift_ctx(after_four, -4)
    mine, before_two, before_four, after_two, after_four = lax.optimization_barrier(
        (mine, before_two, before_four, after_two, after_four)
    )
    other, before_eight = lax.optimization_barrier((other_core(mine), before_eight))
    before = (before_two, before_four, before_eight)

    offsets = jnp.array(block_offsets, dtype=jnp.int32)
    reach = (block_links[0, 0] > 0) & (block >= offsets)[None, :]
    barred = jnp.where(reach.T[:, :, None], -3e38, 1e30).astype(f32)
    barred = jnp.broadcast_to(barred, (4, heads, 128))

    half = ((count, features), bf16)
    (
        weights, mixed, attn, d_query, query, upper, key, value, taps, own_stats, stats
    ) = call(
        rows_kernel,
        [((8, features, features), bf16)] + [half] * 7
        + [((3, count, features), bf16), ((24, count), f32), ((4, 24, count), f32)],
        [
            pltpu.VMEM((3, 5 * count, features), bf16),
            pltpu.VMEM((5 * count, features), bf16),
            pltpu.VMEM((5 * count, features), bf16),
        ],
        smem=2,
        inputs=12,
    )(
        core, reach.astype(jnp.int32), mine, other, window, before_one, *before, cotangent, gain,
        barred,
    )
    attn, stats, after_eight = lax.optimization_barrier((attn, stats, after_eight))
    after = (after_one, after_two, after_four, after_eight)
    returned = [shift_ctx(stats[i], -block_offsets[i]) for i in range(4)]
    parts = ((8, 4, 32, features), bf16)
    keep, send = call(partials_kernel, [parts, parts], smem=1, inputs=5)(
        core, taps, d_query, attn, cotangent
    )
    queries, uppers = call(
        later_kernel,
        [((4 * count, features), bf16)] * 2,
        [pltpu.VMEM((3, 4 * count, features), bf16), pltpu.VMEM((4 * count, features), bf16)],
        inputs=7,
    )(own, *after, gain, weights)
    query_half = halve(keep, send)
    d_key, d_value, keep, send = call(
        columns_kernel, [half, half, parts, parts], smem=1, inputs=13
    )(core, key, value, query, upper, queries, uppers, taps, own_stats, *returned)
    key_half = halve(keep, send)
    d_normed, back, d_gain = call(
        normed_kernel,
        [((count, features), f32), ((edge, features), f32), ((edge, features), bf16)],
        inputs=5,
    )(d_query, d_key, d_value, weights, window)
    later = shift_ctx(back, -1)
    terms = jnp.stack([query_half, key_half], axis=1).reshape(16, 128, features)
    d_gain = jnp.broadcast_to(d_gain[None], (16, edge, features))
    arrived = over_plane(jnp.concatenate([terms, d_gain], axis=1))
    arrived = jnp.sum(arrived.astype(f32), axis=0)
    rows = arrived[:128].astype(bf16).reshape(16, 8, features)
    top, rest = in_two(jnp.sum(arrived[128:], axis=0).reshape(4, 128))
    extra = jnp.broadcast_to(jnp.concatenate([top, rest], axis=0)[None], (16, 8, 128))
    arrived = over_z(jnp.concatenate([rows, extra], axis=2)).astype(f32)
    summed = jnp.sum(arrived, axis=0)
    d_normed, summed = lax.optimization_barrier((d_normed, summed))
    (grad_series,) = call(series_kernel, [half], inputs=5)(
        d_normed, later, window, cotangent, gain
    )
    core_gain = summed[:4, features:] + summed[4:, features:]
    gain_total = (core_gain + other_core(core_gain)).reshape(features)
    summed = summed[:, :features].astype(bf16)
    mine = over_z(jnp.broadcast_to(summed[None], (16, 8, features)))
    other = other_side(mine)
    first = block % 2 == 0
    for_query = jnp.where(first, mine, other).reshape(4, 32, features).astype(f32)
    for_key = jnp.where(first, other, mine).reshape(4, 32, features).astype(f32)
    return (
        mixed[None],
        grad_series[None],
        gain_total,
        for_query[:3],
        for_key[:3],
        for_key[3],
        for_query[3],
    )


def solution(mesh):
    placed = (
        P("dp", "ctx", None),
        P(),
        P(None, "dp", None),
        P(None, "dp", None),
        P("dp", None),
        P("dp", None),
        P("dp", "ctx", None, None),
        P("dp", "ctx", None),
    )
    return jax.shard_map(
        body,
        mesh=mesh,
        in_specs=placed,
        out_specs=(
            P("dp", "ctx", None),
            P("dp", "ctx", None),
            P(),
            P(None, "dp", None),
            P(None, "dp", None),
            P("dp", None),
            P("dp", None),
        ),
        check_vma=False,
    )
```

```python
import jax
import jax.numpy as jnp
from jax import lax
from jax.experimental import pallas as pl
from jax.experimental.pallas import tpu as pltpu
from jax.sharding import PartitionSpec as P

block_offsets = (1, 2, 4, 8)
epsilon = 1e-06
hidden = -1e30
f32 = jnp.float32
bf16 = jnp.bfloat16
edge = 16
plane_groups = [
    [(2 * chip + core) * 32 + 2 * z + side for chip in range(8) for side in range(2)]
    for core in range(2)
    for z in range(16)
]
chip_groups = [[2 * chip + core for chip in range(8)] for core in range(2)]
z_groups = [[2 * z + side for z in range(16)] for side in range(2)]


def shift_ctx(shard, by):
    devices = lax.axis_size("ctx")
    pairs = [(i, i + by) for i in range(devices) if 0 <= i + by < devices]
    return lax.ppermute(shard, "ctx", pairs)


def dp_to(shard, dx, dy, dc):
    def target(i):
        x, y, c = i // 8, (i // 2) % 4, i % 2
        return ((x + dx) % 2) * 8 + ((y + dy) % 4) * 2 + (c + dc) % 2

    return lax.ppermute(shard, "dp", [(i, target(i)) for i in range(16)])


def other_core(shard):
    return dp_to(shard, 0, 0, 1)


def over_chips(stacked):
    return lax.all_to_all(stacked, "dp", 0, 0, axis_index_groups=chip_groups, tiled=True)


def over_plane(stacked):
    return lax.all_to_all(
        stacked, ("dp", "ctx"), 0, 0, axis_index_groups=plane_groups, tiled=True
    )


def over_z(stacked):
    return lax.all_to_all(stacked, "ctx", 0, 0, axis_index_groups=z_groups, tiled=True)


def other_side(shard):
    return lax.ppermute(shard, "ctx", [(i, i ^ 1) for i in range(32)])


def product(left, right):
    return jnp.dot(left, right, preferred_element_type=f32)


def product_right_t(left, right):
    return lax.dot_general(left, right, (((1,), (1,)), ((), ())), preferred_element_type=f32)


def product_left_t(left, right):
    return lax.dot_general(left, right, (((0,), (0,)), ((), ())), preferred_element_type=f32)


def in_two(values):
    top = values.astype(bf16)
    return top, (values - top.astype(f32)).astype(bf16)


def inverse_rms(values):
    return lax.rsqrt(jnp.mean(values * values, axis=-1, keepdims=True) + epsilon)


def normed_taps(window, gain):
    values = window.astype(f32)
    normed = values * inverse_rms(values) * gain
    count = window.shape[0] - edge
    return [normed[edge - tap : edge - tap + count].astype(bf16) for tap in range(3)]


def call(kernel, outs, scratch=(), smem=0, inputs=0):
    return pl.pallas_call(
        kernel,
        out_shape=[jax.ShapeDtypeStruct(shape, kind) for shape, kind in outs],
        in_specs=[pl.BlockSpec(memory_space=pltpu.SMEM)] * smem
        + [pl.BlockSpec(memory_space=pltpu.VMEM)] * (inputs - smem),
        out_specs=[pl.BlockSpec(memory_space=pltpu.VMEM)] * len(outs),
        scratch_shapes=list(scratch),
        compiler_params=pltpu.CompilerParams(vmem_limit_bytes=50 * 1024 * 1024),
    )


def split_heads(pair, first):
    wide = pair.astype(f32)
    return jnp.concatenate(
        [jnp.where(first, wide, 0.0), jnp.where(first, 0.0, wide)], axis=0
    ).astype(bf16)


def join_heads(stacked, first):
    count = stacked.shape[0] // 2
    return jnp.where(first, stacked[:count], stacked[count:])


def rows_kernel(
    core_ref, links_ref, mine_ref, other_ref, window_ref, one_ref, two_ref, four_ref, eight_ref, upstream_ref, gain_ref, barred_ref,
    weights_ref, mixed_ref, attn_ref, d_query_ref, query_ref, upper_ref, key_ref, value_ref,
    taps_ref, own_stats_ref, stats_ref,
    lines_ref, keys_ref, values_ref,
):
    even = core_ref[0] == 0
    for chip in range(8):
        for matrix in range(8):
            mine, other = mine_ref[chip, matrix], other_ref[chip, matrix]
            weights_ref[matrix, chip * 64 : chip * 64 + 32] = jnp.where(even, mine, other)
            weights_ref[matrix, chip * 64 + 32 : chip * 64 + 64] = jnp.where(even, other, mine)
    gain = gain_ref[...]
    count = one_ref.shape[0]
    one = jnp.concatenate([two_ref[count:], one_ref[...]], axis=0)
    for slot, window in enumerate(
        (window_ref[...], one, two_ref[...], four_ref[...], eight_ref[...])
    ):
        for tap, part in enumerate(normed_taps(window, gain)):
            lines_ref[tap, slot * count : (slot + 1) * count] = part
    for tap in range(3):
        taps_ref[tap] = lines_ref[tap, :count]
    keys = product(lines_ref[0], weights_ref[0])
    keys = keys + product(lines_ref[1], weights_ref[1])
    keys_ref[...] = (keys + product(lines_ref[2], weights_ref[2])).astype(bf16)
    values_ref[...] = product(lines_ref[0], weights_ref[3]).astype(bf16)
    query = product(taps_ref[0], weights_ref[4])
    query = query + product(taps_ref[1], weights_ref[5])
    query_ref[...] = (query + product(taps_ref[2], weights_ref[6])).astype(bf16)
    upper_ref[...] = product_right_t(upstream_ref[...], weights_ref[7]).astype(bf16)
    key_ref[...] = keys_ref[:count]
    value_ref[...] = values_ref[:count]

    lane = lax.broadcasted_iota(jnp.int32, (count, 128), 1)
    row = lax.broadcasted_iota(jnp.int32, (count, 128), 0)
    first = lane < 64
    causal = jnp.where(lane <= row, 0.0, hidden)
    table = jnp.zeros((count, 128), f32)
    scaling = 64 ** (-0.5)
    for pair in range(4):
        span = slice(pair * 128, (pair + 1) * 128)
        query = split_heads(query_ref[:, span], first)
        upper = split_heads(upper_ref[:, span], first)
        key, value = keys_ref[:, span], values_ref[:, span]
        scores = product_right_t(query, key) * scaling
        d_prob = product_right_t(upper, value)
        probs_low, d_score = [], []
        for inner in range(2):
            head = pair * 2 + inner
            mine = scores[inner * count : (inner + 1) * count]
            parts = [mine[:, :count] + causal]
            for i in range(4):
                bias = jnp.where(links_ref[head, i] > 0, 0.0, hidden)
                parts.append(mine[:, (i + 1) * count : (i + 2) * count] + bias)
            mine = jnp.concatenate(parts, axis=1)
            highest = jnp.max(mine, axis=1, keepdims=True)
            weight = jnp.exp(mine - highest)
            inverse = 1.0 / jnp.sum(weight, axis=1, keepdims=True)
            probs = weight * inverse
            slope = d_prob[inner * count : (inner + 1) * count]
            centre = jnp.sum(probs * slope, axis=1, keepdims=True)
            probs_low.append(probs.astype(bf16))
            d_score.append((probs * (slope - centre) * scaling).astype(bf16))
            table = jnp.where(lane == head, highest, table)
            table = jnp.where(lane == 8 + head, inverse, table)
            table = jnp.where(lane == 16 + head, centre, table)
        attn = product(jnp.concatenate(probs_low, axis=0), value)
        attn_ref[:, span] = join_heads(attn, first).astype(bf16)
        d_query = product(jnp.concatenate(d_score, axis=0), key)
        d_query_ref[:, span] = join_heads(d_query, first).astype(bf16)
    across = jnp.transpose(table)
    own_stats_ref[...] = across[:24]
    for i in range(4):
        stats_ref[i, :8] = jnp.maximum(across[:8], barred_ref[i])
        stats_ref[i, 8:] = across[8:24]
    mixed = window_ref[edge:].astype(f32) + product(attn_ref[...], weights_ref[7])
    mixed_ref[...] = mixed.astype(bf16)


def later_kernel(
    own_ref, one_ref, two_ref, four_ref, eight_ref, gain_ref, weights_ref,
    queries_ref, uppers_ref,
    lines_ref, cots_ref,
):
    gain = gain_ref[...]
    count = own_ref.shape[0]
    one = jnp.concatenate([own_ref[count - edge :], one_ref[:count]], axis=0)
    size = count + edge
    windows = (one, two_ref[:size], four_ref[:size], eight_ref[:size])
    cots = (one_ref[count:], two_ref[size:], four_ref[size:], eight_ref[size:])
    for slot in range(4):
        rows = slice(slot * count, (slot + 1) * count)
        cots_ref[rows] = cots[slot]
        for tap, part in enumerate(normed_taps(windows[slot], gain)):
            lines_ref[tap, rows] = part
    queries = product(lines_ref[0], weights_ref[4])
    queries = queries + product(lines_ref[1], weights_ref[5])
    queries_ref[...] = (queries + product(lines_ref[2], weights_ref[6])).astype(bf16)
    uppers_ref[...] = product_right_t(cots_ref[...], weights_ref[7]).astype(bf16)


def store_partials(even, term, keep_ref, send_ref, matrix):
    term = term.astype(bf16)
    for chip in range(8):
        low = term[chip * 64 : chip * 64 + 32]
        high = term[chip * 64 + 32 : chip * 64 + 64]
        keep_ref[chip, matrix] = jnp.where(even, low, high)
        send_ref[chip, matrix] = jnp.where(even, high, low)


def partials_kernel(core_ref, taps_ref, d_query_ref, attn_ref, upstream_ref, keep_ref, send_ref):
    even = core_ref[0] == 0
    for tap in range(3):
        term = product_left_t(taps_ref[tap], d_query_ref[...])
        store_partials(even, term, keep_ref, send_ref, tap)
    term = product_left_t(attn_ref[...], upstream_ref[...])
    store_partials(even, term, keep_ref, send_ref, 3)


def columns_kernel(
    core_ref, key_ref, value_ref, query_ref, upper_ref, queries_ref, uppers_ref, taps_ref,
    own_ref, one_ref, two_ref, four_ref, eight_ref,
    d_key_ref, d_value_ref, keep_ref, send_ref,
):
    even = core_ref[0] == 0
    count = key_ref.shape[0]
    lane = lax.broadcasted_iota(jnp.int32, (count, 128), 1)
    row = lax.broadcasted_iota(jnp.int32, (count, 128), 0)
    first = lane < 64
    causal = jnp.concatenate([row <= lane] * 2, axis=1)
    scaling = 64 ** (-0.5)
    all_stats = [own_ref[...], one_ref[...], two_ref[...], four_ref[...], eight_ref[...]]
    all_stats = [
        (jnp.where(stats[8:16] > 0.0, stats[:8], 1e30), stats[8:16], stats[16:24])
        for stats in all_stats
    ]
    for pair in range(4):
        span = slice(pair * 128, (pair + 1) * 128)
        key, value = key_ref[:, span], value_ref[:, span]
        d_key = jnp.zeros((count, 128), f32)
        d_value = jnp.zeros((count, 128), f32)
        for slot in range(5):
            if slot == 0:
                query, upper = query_ref[:, span], upper_ref[:, span]
            else:
                rows = slice((slot - 1) * count, slot * count)
                query, upper = queries_ref[rows, span], uppers_ref[rows, span]
            query, upper = split_heads(query, first), split_heads(upper, first)
            highest, inverse, centre = [
                jnp.concatenate([part[pair * 2 : pair * 2 + 1], part[pair * 2 + 1 : pair * 2 + 2]], axis=1)
                for part in all_stats[slot]
            ]
            scores = product_right_t(key, query) * scaling
            probs = jnp.exp(scores - highest) * inverse
            if slot == 0:
                probs = jnp.where(causal, probs, 0.0)
            d_prob = product_right_t(value, upper)
            d_score = (probs * (d_prob - centre) * scaling).astype(bf16)
            d_key = d_key + product(d_score, query)
            d_value = d_value + product(probs.astype(bf16), upper)
        d_key_ref[:, span] = d_key.astype(bf16)
        d_value_ref[:, span] = d_value.astype(bf16)
    for tap in range(3):
        term = product_left_t(taps_ref[tap], d_key_ref[...])
        store_partials(even, term, keep_ref, send_ref, tap)
    store_partials(even, product_left_t(taps_ref[0], d_value_ref[...]), keep_ref, send_ref, 3)


def normed_kernel(
    d_query_ref, d_key_ref, d_value_ref, weights_ref, window_ref, d_normed_ref, back_ref, d_gain_ref
):
    count, features = d_query_ref.shape
    blank = jnp.zeros((edge, features), f32)
    own = product_right_t(d_value_ref[...], weights_ref[3])
    d_normed = jnp.concatenate([blank, own], axis=0)
    for ref, base in ((d_query_ref, 4), (d_key_ref, 0)):
        rows = jnp.concatenate([blank, ref[...].astype(f32), blank], axis=0)
        for tap in range(3):
            part = rows[tap : tap + count + edge].astype(bf16)
            d_normed = d_normed + product_right_t(part, weights_ref[base + tap])
    values = window_ref[...].astype(f32)
    top, rest = in_two(jnp.sum(d_normed * values * inverse_rms(values), axis=0, keepdims=True))
    unused = jnp.zeros((d_gain_ref.shape[0] - 2, features), f32)
    d_gain_ref[...] = jnp.concatenate(
        [top.astype(f32), rest.astype(f32), unused], axis=0
    ).astype(bf16)
    back_ref[...] = d_normed[:edge]
    d_normed_ref[...] = d_normed[edge:]


def series_kernel(d_normed_ref, later_ref, window_ref, upstream_ref, gain_ref, grad_ref):
    count = d_normed_ref.shape[0]
    d_normed = jnp.concatenate(
        [d_normed_ref[: count - edge], d_normed_ref[count - edge :] + later_ref[...]], axis=0
    )
    values = window_ref[edge:].astype(f32)
    scale = inverse_rms(values)
    slope = d_normed * gain_ref[...]
    along = jnp.mean(slope * values, axis=-1, keepdims=True)
    d_values = scale * slope - values * (scale * scale * scale * along)
    grad_ref[...] = (upstream_ref[...].astype(f32) + d_values).astype(bf16)


def halve(keep, send):
    return (keep.astype(f32) + other_core(send).astype(f32)).astype(bf16)


def body(
    series, norm_gain, query_kernel, key_kernel, value_weight, out_weight, block_links, grad_out
):
    core = (lax.axis_index("dp") % 2).reshape(1)
    block = lax.axis_index("ctx")
    heads = block_links.shape[2]
    own, cotangent = series[0], grad_out[0]
    count, features = own.shape
    gain = norm_gain.reshape(1, features)

    shard = jnp.concatenate(
        [key_kernel, value_weight[None], query_kernel, out_weight[None]], axis=0
    )
    before_one = shift_ctx(own, 1)
    after_one = shift_ctx(jnp.concatenate([own, cotangent], axis=0), -1)
    shard, before_one, after_one = lax.optimization_barrier((shard, before_one, after_one))
    window = jnp.concatenate([before_one[count - edge :], own], axis=0)
    carried = jnp.concatenate([window, cotangent], axis=0)
    after_four, after_two = shift_ctx(carried, -4), shift_ctx(carried, -2)
    before_four, before_two = shift_ctx(window, 4), shift_ctx(window, 2)
    mine = over_chips(jnp.broadcast_to(shard[None], (8,) + shard.shape))
    before_eight, after_eight = shift_ctx(before_four, 4), shift_ctx(after_four, -4)
    mine, before_two, before_four, after_two, after_four = lax.optimization_barrier(
        (mine, before_two, before_four, after_two, after_four)
    )
    other, before_eight = lax.optimization_barrier((other_core(mine), before_eight))
    before = (before_two, before_four, before_eight)

    offsets = jnp.array(block_offsets, dtype=jnp.int32)
    reach = (block_links[0, 0] > 0) & (block >= offsets)[None, :]
    barred = jnp.where(reach.T[:, :, None], -3e38, 1e30).astype(f32)
    barred = jnp.broadcast_to(barred, (4, heads, 128))

    half = ((count, features), bf16)
    (
        weights, mixed, attn, d_query, query, upper, key, value, taps, own_stats, stats
    ) = call(
        rows_kernel,
        [((8, features, features), bf16)] + [half] * 7
        + [((3, count, features), bf16), ((24, count), f32), ((4, 24, count), f32)],
        [
            pltpu.VMEM((3, 5 * count, features), bf16),
            pltpu.VMEM((5 * count, features), bf16),
            pltpu.VMEM((5 * count, features), bf16),
        ],
        smem=2,
        inputs=12,
    )(
        core, reach.astype(jnp.int32), mine, other, window, before_one, *before, cotangent, gain,
        barred,
    )
    attn, stats, after_eight = lax.optimization_barrier((attn, stats, after_eight))
    after = (after_one, after_two, after_four, after_eight)
    returned = [shift_ctx(stats[i], -block_offsets[i]) for i in range(4)]
    parts = ((8, 4, 32, features), bf16)
    keep, send = call(partials_kernel, [parts, parts], smem=1, inputs=5)(
        core, taps, d_query, attn, cotangent
    )
    queries, uppers = call(
        later_kernel,
        [((4 * count, features), bf16)] * 2,
        [pltpu.VMEM((3, 4 * count, features), bf16), pltpu.VMEM((4 * count, features), bf16)],
        inputs=7,
    )(own, *after, gain, weights)
    query_half = halve(keep, send)
    d_key, d_value, keep, send = call(
        columns_kernel, [half, half, parts, parts], smem=1, inputs=13
    )(core, key, value, query, upper, queries, uppers, taps, own_stats, *returned)
    key_half = halve(keep, send)
    d_normed, back, d_gain = call(
        normed_kernel,
        [((count, features), f32), ((edge, features), f32), ((edge, features), bf16)],
        inputs=5,
    )(d_query, d_key, d_value, weights, window)
    later = shift_ctx(back, -1)
    terms = jnp.stack([query_half, key_half], axis=1).reshape(16, 128, features)
    d_gain = jnp.broadcast_to(d_gain[None, :8], (16, 8, features))
    arrived = over_plane(jnp.concatenate([terms, d_gain], axis=1))
    arrived = jnp.sum(arrived.astype(f32), axis=0)
    rows = arrived[:128].astype(bf16).reshape(16, 8, features)
    top, rest = in_two(jnp.sum(arrived[128:], axis=0).reshape(4, 128))
    extra = jnp.broadcast_to(jnp.concatenate([top, rest], axis=0)[None], (16, 8, 128))
    arrived = over_z(jnp.concatenate([rows, extra], axis=2)).astype(f32)
    summed = jnp.sum(arrived, axis=0)
    d_normed, summed = lax.optimization_barrier((d_normed, summed))
    (grad_series,) = call(series_kernel, [half], inputs=5)(
        d_normed, later, window, cotangent, gain
    )
    core_gain = summed[:4, features:] + summed[4:, features:]
    gain_total = (core_gain + other_core(core_gain)).reshape(features)
    summed = summed[:, :features].astype(bf16)
    mine = over_z(jnp.broadcast_to(summed[None], (16, 8, features)))
    other = other_side(mine)
    first = block % 2 == 0
    for_query = jnp.where(first, mine, other).reshape(4, 32, features).astype(f32)
    for_key = jnp.where(first, other, mine).reshape(4, 32, features).astype(f32)
    return (
        mixed[None],
        grad_series[None],
        gain_total,
        for_query[:3],
        for_key[:3],
        for_key[3],
        for_query[3],
    )


def solution(mesh):
    placed = (
        P("dp", "ctx", None),
        P(),
        P(None, "dp", None),
        P(None, "dp", None),
        P("dp", None),
        P("dp", None),
        P("dp", "ctx", None, None),
        P("dp", "ctx", None),
    )
    return jax.shard_map(
        body,
        mesh=mesh,
        in_specs=placed,
        out_specs=(
            P("dp", "ctx", None),
            P("dp", "ctx", None),
            P(),
            P(None, "dp", None),
            P(None, "dp", None),
            P("dp", None),
            P("dp", None),
        ),
        check_vma=False,
    )
```
